128 devices in a mesh: group: 16 (over z_lo, y, core), tp: 8 (over x, z_hi).
Axes of the slice: x: 4, y: 4, z: 4 (z_hi: 2, z_lo: 2; z = z_hi * 2 + z_lo), core: 2. Of those that a mesh axis runs over, the one named last changes fastest.
Arguments:
- activations: bfloat16 [8192, 8192], P('group'), may hold values from -20.4 to 20.4
- query_weight: bfloat16 [8192, 8192], P('group', 'tp'), may hold values from -0.0625 to 0.0625
- key_matrix: bfloat16 [8192, 1024], P('group', 'tp'), may hold values from -0.0625 to 0.0625
- value_matrix: bfloat16 [8192, 1024], P('group', 'tp'), may hold values from -0.0625 to 0.0625
- output_weight: bfloat16 [8192, 8192], P('tp', 'group'), may hold values from -0.0625 to 0.0625
- prompt_lengths: int32 [16, 8], P('group'), may hold values from 1 to 256, 512 in all within a row
Outputs:
- attended: bfloat16 [8192, 8192], P(('group', 'tp'))
The draws below stay inside these ranges and needn't reach their ends.
Inputs may be any that keep to these rules, and one draw needn't show every extreme that they name: `prompt_lengths`: each group's 8 lengths sum to 512; the largest of each group is exactly 256.
All inputs are finite; a program needn't handle non-finite values.
Results may differ from the reference program's by a relative error of at most 0.019.
The reference program's roundings to bfloat16 on the way count: a program that leaves them out, or rounds other values in their place, can miss the bound.
Values may be sent and summed in bfloat16 or wider, within the bound.
A program may use at most 128 MiB of HBM per device.

```python
import math
import jax
import jax.numpy as jnp
import numpy as np
from jax import lax

MODEL_WIDTH = 8192
HEAD_SIZE = 128
QUERY_HEAD_COUNT = 64
KEY_VALUE_HEADS = 8
DOCS = 8
SPAN = 512
MOST = 256
GROUPS = 16
TOKENS = 8192
N_TP = 8


def draw_activations(key, part):
    key = jax.random.fold_in(key, 7)
    first, second = jax.random.split(key)
    base = jax.random.truncated_normal(first, -6.0, 6.0, (TOKENS, MODEL_WIDTH), jnp.float32)
    spread = jnp.exp(jax.random.uniform(second, (TOKENS, 1), jnp.float32) * math.log(3.0))
    return (base * spread).astype(jnp.bfloat16)


def block_scale(rng, shape, pieces, low, high):
    def one(axis_at, blocks):
        steps = jax.random.uniform(jax.random.fold_in(jax.random.fold_in(rng, 6), axis_at), (blocks,), jnp.float32, low / len(pieces), high / len(pieces))
        return jnp.repeat(jnp.exp(steps), shape[axis_at] // blocks).reshape((-1,) + (1,) * (len(shape) - axis_at - 1))

    gain = one(*pieces[0])
    for cut in pieces[1:]:
        gain = gain * one(*cut)
    return gain


def split_up(count, total, limit, slope):
    portions = [(1 << 20) // math.isqrt(rank ** slope) + 1 for rank in range(2, count + 1)]
    spare, counts = total - limit - (count - 1), [1] * (count - 1)
    while spare > 0:
        free = [i for i in range(count - 1) if counts[i] < limit]
        whole, left = sum([portions[i] for i in free]), spare
        for i in free:
            more = min(limit - counts[i], max(1, left * portions[i] // whole), spare)
            counts[i] = counts[i] + more
            spare = spare - more
    return np.array([limit] + counts)


def ragged(stream_key, number_of, total, reach, lean):
    if number_of == 2:
        one = jax.random.randint(stream_key, (), max(1, total - reach), min(reach, total - 1) + 1)
        return jnp.stack([one, total - one])
    sizes = jnp.asarray(split_up(number_of, total, reach, lean), jnp.int32)
    pairs = (number_of - 1) // 2
    giver, taker = sizes[1:1 + 2 * pairs:2], sizes[2:2 + 2 * pairs:2]
    room = jnp.minimum(giver - 1, reach - taker)
    passed = jax.random.randint(jax.random.fold_in(stream_key, 1), (pairs,), 0, 1 << 20) % (room + 1)
    sizes = sizes.at[1:1 + 2 * pairs:2].set(giver - passed).at[2:2 + 2 * pairs:2].set(taker + passed)
    return sizes[jax.random.permutation(jax.random.fold_in(stream_key, 2), number_of)]


def normal_values(own_key, extent, scale, most, cuts=(), kind=jnp.bfloat16):
    gain = block_scale(own_key, extent, cuts, -0.22, 0.18) if cuts else 1.0
    values = jax.random.normal(own_key, extent, jnp.float32) * scale * gain
    return jnp.minimum(jnp.maximum(values, -most), most).astype(kind)


def setup_inputs(seed: int = 0) -> dict:
    seeds = jax.random.split(jax.random.key(seed), 7)
    return {
        "activations": draw_activations(jax.random.fold_in(seeds[6], 71), 0),
        "query_weight": normal_values(seeds[1], (MODEL_WIDTH, QUERY_HEAD_COUNT * HEAD_SIZE), MODEL_WIDTH ** -0.5, 0.0625, ((0, 16), (1, 8))),
        "key_matrix": normal_values(seeds[2], (MODEL_WIDTH, KEY_VALUE_HEADS * HEAD_SIZE), MODEL_WIDTH ** -0.5, 0.0625, ((0, 16), (1, 8))),
        "value_matrix": normal_values(seeds[3], (MODEL_WIDTH, KEY_VALUE_HEADS * HEAD_SIZE), MODEL_WIDTH ** -0.5, 0.0625, ((0, 16), (1, 8))),
        "output_weight": normal_values(seeds[4], (QUERY_HEAD_COUNT * HEAD_SIZE, MODEL_WIDTH), (QUERY_HEAD_COUNT * HEAD_SIZE) ** -0.5, 0.0625, ((0, 8), (1, 16))),
        "prompt_lengths": jax.vmap(lambda own: ragged(own, DOCS, SPAN, MOST, 1))(jax.random.split(seeds[5], GROUPS)).reshape((GROUPS, DOCS)).astype(jnp.int32),
    }


def doc_positions(lengths_row, token_count):
    ends = jnp.cumsum(lengths_row)
    place = jnp.arange(token_count, dtype=jnp.int32)
    after = (place[:, None] >= ends[None, :]).astype(jnp.int32)
    segment = lax.optimization_barrier(jnp.sum(after, axis=1))
    token_offset = place - lax.optimization_barrier(jnp.sum(after * lengths_row[None, :], axis=1))
    return (place, segment, token_offset)

def apply_rotary(value_states, token_offset):
    half = HEAD_SIZE // 2
    freq = 500000.0 ** (-2.0 * jnp.arange(half, dtype=jnp.float32) / HEAD_SIZE)
    angle = token_offset.astype(jnp.float32)[:, None] * freq[None, :]
    cosine = jnp.cos(angle)[:, None, :]
    sine = jnp.sin(angle)[:, None, :]
    first = value_states[..., :half]
    second = value_states[..., half:]
    return jnp.concatenate([first * cosine - second * sine, second * cosine + first * sine], axis=-1)

def one_group(operands):
    token_block, lengths_row, query_weight, key_matrix, value_matrix, output_weight = operands
    token_count = token_block.shape[0]
    place, segment, token_offset = doc_positions(lengths_row, token_count)
    query_states = jnp.dot(token_block, query_weight, preferred_element_type=jnp.float32).reshape(token_count, QUERY_HEAD_COUNT, HEAD_SIZE)
    key_states = jnp.dot(token_block, key_matrix, preferred_element_type=jnp.float32).reshape(token_count, KEY_VALUE_HEADS, HEAD_SIZE)
    value_states = jnp.dot(token_block, value_matrix, preferred_element_type=jnp.float32).reshape(token_count, KEY_VALUE_HEADS, HEAD_SIZE)
    rotated_query = apply_rotary(query_states, token_offset).astype(jnp.bfloat16).reshape(token_count, KEY_VALUE_HEADS, QUERY_HEAD_COUNT // KEY_VALUE_HEADS, HEAD_SIZE)
    rk = apply_rotary(key_states, token_offset).astype(jnp.bfloat16)
    rv = value_states.astype(jnp.bfloat16)
    score = jnp.einsum('sgrd,tgd->grst', rotated_query.astype(jnp.float32), rk.astype(jnp.float32)) / jnp.sqrt(jnp.float32(HEAD_SIZE))
    allowed = (segment[:, None] == segment[None, :]) & (place[None, :] <= place[:, None])
    score = jnp.where(allowed, score, -1e+30)
    top = lax.optimization_barrier(jnp.max(score, axis=-1, keepdims=True))
    weights = jnp.exp(score - top)
    probs = (weights / lax.optimization_barrier(jnp.sum(weights, axis=-1, keepdims=True))).astype(jnp.bfloat16)
    context = jnp.einsum('grst,tgd->sgrd', probs.astype(jnp.float32), rv.astype(jnp.float32))
    context = context.astype(jnp.bfloat16).reshape(token_count, QUERY_HEAD_COUNT * HEAD_SIZE)
    width = QUERY_HEAD_COUNT * HEAD_SIZE // N_TP
    total = jnp.zeros((token_count, MODEL_WIDTH), jnp.float32)
    for blockid in range(N_TP):
        part = jnp.dot(context[:, blockid * width:(blockid + 1) * width], output_weight[blockid * width:(blockid + 1) * width, :], preferred_element_type=jnp.float32)
        total = total + part.astype(jnp.bfloat16).astype(jnp.float32)
    return total.astype(jnp.bfloat16)

def reference(activations, query_weight, key_matrix, value_matrix, output_weight, prompt_lengths):
    blocks = activations.reshape(GROUPS, SPAN, MODEL_WIDTH)

    def step(pair):
        return one_group((pair[0], pair[1], query_weight, key_matrix, value_matrix, output_weight))
    result = lax.map(step, (blocks, prompt_lengths))
    return result.reshape(TOKENS, MODEL_WIDTH)
```

```python
import jax
import jax.numpy as jnp
from jax import lax
from jax.sharding import PartitionSpec as P

HEAD_SIZE = 128


def doc_positions(lengths_row, token_count):
    ends = jnp.cumsum(lengths_row)
    place = jnp.arange(token_count, dtype=jnp.int32)
    after = (place[:, None] >= ends[None, :]).astype(jnp.int32)
    segment = jnp.sum(after, axis=1)
    token_offset = place - jnp.sum(after * lengths_row[None, :], axis=1)
    return (place, segment, token_offset)


def apply_rotary(value_states, token_offset):
    half = HEAD_SIZE // 2
    freq = 500000.0 ** (-2.0 * jnp.arange(half, dtype=jnp.float32) / HEAD_SIZE)
    angle = token_offset.astype(jnp.float32)[:, None] * freq[None, :]
    cosine = jnp.cos(angle)[:, None, :]
    sine = jnp.sin(angle)[:, None, :]
    first = value_states[..., :half]
    second = value_states[..., half:]
    return jnp.concatenate(
        [first * cosine - second * sine, second * cosine + first * sine], axis=-1
    )


def add_rows(token_block, piece):
    return jnp.dot(token_block, piece, preferred_element_type=jnp.float32)


def local(activations, query_weight, key_matrix, value_matrix, output_weight, prompt_lengths):
    token_count = activations.shape[0]
    query_heads = query_weight.shape[1] // HEAD_SIZE
    kv_heads = key_matrix.shape[1] // HEAD_SIZE
    query_states = add_rows(activations, lax.all_gather(query_weight, "group", axis=0, tiled=True))
    key_states = add_rows(activations, lax.all_gather(key_matrix, "group", axis=0, tiled=True))
    value_states = add_rows(activations, lax.all_gather(value_matrix, "group", axis=0, tiled=True))
    place, segment, token_offset = doc_positions(prompt_lengths[0], token_count)
    rotated_query = apply_rotary(
        query_states.reshape(token_count, query_heads, HEAD_SIZE), token_offset
    ).astype(jnp.bfloat16)
    rotated_query = rotated_query.reshape(token_count, kv_heads, query_heads // kv_heads, HEAD_SIZE)
    rk = apply_rotary(key_states.reshape(token_count, kv_heads, HEAD_SIZE), token_offset).astype(
        jnp.bfloat16
    )
    rv = value_states.reshape(token_count, kv_heads, HEAD_SIZE).astype(jnp.bfloat16)
    score = jnp.einsum(
        "sgrd,tgd->grst", rotated_query, rk, preferred_element_type=jnp.float32
    ) / jnp.sqrt(jnp.float32(HEAD_SIZE))
    allowed = (segment[:, None] == segment[None, :]) & (place[None, :] <= place[:, None])
    score = jnp.where(allowed, score, -1e30)
    top = jnp.max(score, axis=-1, keepdims=True)
    weights = jnp.exp(score - top)
    probs = (weights / jnp.sum(weights, axis=-1, keepdims=True)).astype(jnp.bfloat16)
    context = jnp.einsum("grst,tgd->sgrd", probs, rv, preferred_element_type=jnp.float32)
    context = context.astype(jnp.bfloat16).reshape(token_count, query_heads * HEAD_SIZE)
    partial_out = jnp.dot(
        context,
        lax.all_gather(output_weight, "group", axis=1, tiled=True),
        preferred_element_type=jnp.float32,
    )
    return lax.psum_scatter(
        partial_out.astype(jnp.bfloat16), "tp", scatter_dimension=0, tiled=True
    )


def solution(mesh):
    placed = (
        P("group", None),
        P("group", "tp"),
        P("group", "tp"),
        P("group", "tp"),
        P("tp", "group"),
        P("group", None),
    )
    return jax.shard_map(
        local, mesh=mesh, in_specs=placed, out_specs=P(("group", "tp"), None), check_vma=False
    )
```

```python
import math

import jax
import jax.numpy as jnp
from jax import lax
from jax.experimental import pallas as pl
from jax.experimental.pallas import tpu as pltpu
from jax.sharding import PartitionSpec as P

MESH = pl.DeviceIdType.MESH
SPAN = 512
WIDTH = 8192
HEAD = 128
QCOLS = 1024
COLS = 1280
DEPTH = 512
OROWS = 4096
DOCS = 8
F32 = jnp.float32
BF16 = jnp.bfloat16


def ring(v, step, size):
    return lax.rem(v + (step + size), size)


class Place:
    def __init__(self):
        g = lax.axis_index("group")
        t = lax.axis_index("tp")
        self.g, self.t = g, t
        self.core = lax.rem(g, 2)
        self.y = lax.rem(lax.div(g, 2), 4)
        self.zl = lax.div(g, 8)
        self.x = lax.div(t, 2)
        self.zh = lax.rem(t, 2)

    def chip(self, dz, dy):
        return ring(self.zl, dz, 2) * 4 + ring(self.y, dy, 4)

    def dev(self, dz=0, dy=0, dc=0, dx=0, dh=0):
        group = self.chip(dz, dy) * 2 + ring(self.core, dc, 2)
        return (group, ring(self.x, dx, 4) * 2 + ring(self.zh, dh, 2))


class Gather:
    def __init__(self, place, view, rows, part, send, recv):
        self.place, self.view, self.send, self.recv = place, view, send, recv
        half = part // 2
        rest = rows - part
        self.a, self.a1, self.a2 = (0, part), (0, half), (half, part - half)
        self.b, self.b1, self.b2 = (part, rest), (part, rest // 2), (part + rest // 2, rest - rest // 2)
        self.all = (0, rows)
        up, down, over, twin = place.dev(dy=1), place.dev(dy=-1), place.dev(dz=1), place.dev(dc=1)
        mine, p_up, p_down, p_far = (0, 0), (0, 1), (0, -1), (0, 2)
        z_mine, z_up, z_down, z_far = (1, 0), (1, 1), (1, -1), (1, 2)
        self.steps = [
            (mine, self.a, up, p_down),
            (mine, self.a, down, p_up),
            (mine, self.b, over, z_mine),
            (mine, self.b, up, p_down),
            (mine, self.b, down, p_up),
            (mine, self.a, over, z_mine),
            (p_down, self.a1, up, p_far),
            (p_up, self.a2, down, p_far),
            (p_down, self.a, over, z_down),
            (p_up, self.a, over, z_up),
            (z_mine, self.b, up, z_down),
            (z_mine, self.b, down, z_up),
            (p_down, self.b1, up, p_far),
            (p_up, self.b2, down, p_far),
            (p_far, self.a, over, z_far),
            (z_down, self.b1, up, z_far),
            (z_up, self.b2, down, z_far),
        ]
        self.blocks = [mine, p_down, p_up, z_mine, p_far, z_down, z_up, z_far]
        for block in self.blocks:
            self.steps.append((block, self.all, twin, block))

    def copy(self, step, arriving=False):
        block, rows, target, lands = self.steps[step]
        core = self.place.core
        if arriving:
            block = lands
            if step >= 17:
                core = 1 - core
        ref = self.view(self.place.chip(*block), core, *rows)
        return pltpu.make_async_remote_copy(
            src_ref=ref,
            dst_ref=ref,
            send_sem=self.send.at[step],
            recv_sem=self.recv.at[step],
            device_id=target,
            device_id_type=MESH,
        )

    def start(self, *steps):
        for step in steps:
            self.copy(step).start()

    def arrive(self, *steps):
        for step in steps:
            self.copy(step, arriving=True).wait_recv()

    def finish(self):
        for step in range(len(self.steps)):
            self.copy(step).wait_send()


def starts_of(row, lengths):
    start = jnp.zeros_like(row)
    end = 0
    for j in range(DOCS):
        end = end + lengths[j]
        start = start + jnp.where(row >= end, lengths[j], 0)
    return start


def kernel(
    act, wq, wk, wv, wo, lens, out,
    xbuf, wbuf, obuf, acc, ctx, cosb, sinb, bias, rkb, rvb, sbuf, rbuf, fbuf, gbuf,
    q_send, q_recv, o_send, o_recv, e_send, e_recv, c_send, c_recv, z_send, z_recv, f_send, f_recv,
    x_sem, w_sem,
):
    place = Place()
    me = place.g

    own = [
        pltpu.make_async_copy(wq, wbuf.at[me, :, pl.ds(0, QCOLS)], w_sem.at[0]),
        pltpu.make_async_copy(wk, wbuf.at[me, :, pl.ds(QCOLS, HEAD)], w_sem.at[1]),
        pltpu.make_async_copy(wv, wbuf.at[me, :, pl.ds(QCOLS + HEAD, HEAD)], w_sem.at[2]),
    ]
    for copy in own:
        copy.start()
    chip0 = place.chip(0, 0)
    e_rows = pl.ds(pl.multiple_of(place.x * 1024, 1024), 1024)
    e_cols = pl.ds(pl.multiple_of(place.core * HEAD, HEAD), HEAD)
    own_o = pltpu.make_async_copy(
        wo.at[:, pl.ds(pl.multiple_of(place.x * HEAD, HEAD), HEAD)], obuf.at[chip0, e_rows, e_cols], w_sem.at[3]
    )
    own_o.start()

    def x_copy(s):
        cols = pl.ds(pl.multiple_of(s * DEPTH, DEPTH), DEPTH)
        return pltpu.make_async_copy(act.at[:, cols], xbuf.at[s], x_sem.at[s])

    for s in range(16):
        x_copy(s).start()

    barrier = pltpu.get_barrier_semaphore()
    partners = [
        place.dev(dy=1), place.dev(dy=-1), place.dev(dz=1), place.dev(dc=1),
        place.dev(dx=1), place.dev(dx=2), place.dev(dx=3), place.dev(dh=1),
    ]
    for partner in partners:
        pl.semaphore_signal(barrier, inc=1, device_id=partner, device_id_type=MESH)
    pl.semaphore_wait(barrier, len(partners))

    def w_view(chip, core, first, count):
        return wbuf.at[chip * 2 + core, pl.ds(first, count)]

    def o_view(chip, core, first, count):
        return obuf.at[chip, pl.ds(first, count), pl.ds(pl.multiple_of(core * HEAD, HEAD), HEAD)]

    qg = Gather(place, w_view, DEPTH, 224, q_send, q_recv)
    og = Gather(place, o_view, OROWS, 1792, o_send, o_recv)

    for copy in own:
        copy.wait()
    qg.start(0, 1, 2, 17, 3, 4, 5)

    def exchange(d, arriving=False):
        to = ring(place.x, d, 4)
        frm = ring(place.x, -d, 4)
        row = frm if arriving else place.x
        return pltpu.make_async_remote_copy(
            src_ref=wo.at[:, pl.ds(pl.multiple_of(to * HEAD, HEAD), HEAD)],
            dst_ref=obuf.at[chip0, pl.ds(pl.multiple_of(row * 1024, 1024), 1024), e_cols],
            send_sem=e_send.at[d - 1],
            recv_sem=e_recv.at[d - 1],
            device_id=place.dev(dx=d),
            device_id_type=MESH,
        )

    for d in (1, 3, 2):
        exchange(d).start()

    lengths = [lens[0, j] for j in range(DOCS)]
    row = lax.broadcasted_iota(jnp.int32, (SPAN, HEAD), 0)
    lane = lax.broadcasted_iota(jnp.int32, (SPAN, HEAD), 1)
    low = lane < HEAD // 2
    index = jnp.where(low, lane, lane - HEAD // 2).astype(F32)
    freq = jnp.exp(index * (-2.0 * math.log(500000.0) / HEAD))
    angle = (row - starts_of(row, lengths)).astype(F32) * freq
    cosb[...] = jnp.cos(angle)
    sine = jnp.sin(angle)
    sinb[...] = jnp.where(low, -sine, sine)
    for j, (first, count) in enumerate(TILES):
        q = lax.broadcasted_iota(jnp.int32, (128, count), 0) + j * 128
        k = lax.broadcasted_iota(jnp.int32, (128, count), 1) + first
        keep = (k >= starts_of(q, lengths)) & (k <= q)
        bias[j, :, :count] = jnp.where(keep, 0.0, -1e30)

    for s in range(16):
        x_copy(s).wait()

    def project(block, other=False, fresh=False):
        slot = place.chip(*block) * 2 + ((1 - place.core) if other else place.core)

        def tile(n, carry):
            cols = pl.ds(pl.multiple_of(n * 256, 256), 256)
            part = jnp.dot(xbuf[slot], wbuf[slot, :, cols], preferred_element_type=F32)
            if fresh:
                acc[n] = part
            else:
                acc[n] += part
            return carry

        lax.fori_loop(0, COLS // 256, tile, 0)

    b0, b_dn, b_up, b_z, b_far, b_zdn, b_zup, b_zfar = qg.blocks
    project(b0, fresh=True)
    qg.arrive(17)
    project(b0, other=True)
    qg.arrive(0)
    qg.start(6, 8)
    qg.arrive(1)
    qg.start(7, 9)
    qg.arrive(2)
    qg.start(10, 11)
    qg.arrive(3)
    qg.start(12, 18)
    qg.arrive(4)
    qg.start(13, 19)
    project(b_dn)
    project(b_up)
    qg.arrive(5)
    qg.start(20)
    qg.arrive(6, 7)
    qg.start(14)
    qg.arrive(18)
    project(b_dn, other=True)
    qg.arrive(10)
    qg.start(15)
    qg.arrive(11)
    qg.start(16)
    project(b_z)
    qg.arrive(19)
    project(b_up, other=True)
    qg.arrive(20)
    project(b_z, other=True)
    qg.arrive(8)
    qg.start(22)
    qg.arrive(9)
    qg.start(23)
    for d in (1, 3, 2):
        exchange(d, arriving=True).wait_recv()
    own_o.wait()
    og.start(0, 1, 2, 17, 3, 4, 5)
    project(b_zdn)
    project(b_zup)
    qg.arrive(12, 13)
    qg.start(21)
    project(b_far)
    qg.arrive(22)
    project(b_zdn, other=True)
    qg.arrive(23)
    project(b_zup, other=True)
    qg.arrive(21)
    project(b_far, other=True)
    qg.arrive(14, 15, 16)
    qg.start(24)
    project(b_zfar)
    qg.arrive(24)
    project(b_zfar, other=True)

    def rotate(u):
        return u * cosb[...] + pltpu.roll(u, HEAD // 2, 1) * sinb[...]

    kv = acc[4]
    rkb[...] = rotate(kv[:, :HEAD]).astype(BF16)
    rvb[...] = kv[:, HEAD:].astype(BF16)
    scale = 1.0 / math.sqrt(HEAD)

    def ctx_copy(kind, n, arriving=False):
        cols = pl.ds(pl.multiple_of(n * 256, 256), 256)
        dx = 1 if kind in (0, 2) else -1
        if kind < 2:
            owner, rows = 0, pl.ds(0, SPAN)
        else:
            owner, rows = -dx, pl.ds(0 if kind == 2 else 256, 256)
        if arriving:
            owner = owner - dx
        ref = ctx.at[ring(place.x, owner % 4, 4), rows, cols]
        return pltpu.make_async_remote_copy(
            src_ref=ref,
            dst_ref=ref,
            send_sem=c_send.at[kind, n],
            recv_sem=c_recv.at[kind, n],
            device_id=place.dev(dx=dx),
            device_id_type=MESH,
        )

    def two_heads(n, carry):
        pair = acc[n]
        rq = [rotate(pair[:, :HEAD]).astype(BF16), rotate(pair[:, HEAD:]).astype(BF16)]
        cols = pl.ds(pl.multiple_of(n * 256, 256), 256)
        for j, (first, count) in enumerate(TILES):
            rows = slice(j * 128, (j + 1) * 128)
            q = jnp.concatenate([rq[0][rows], rq[1][rows]], axis=0)
            keys = rkb[first : first + count, :]
            score = lax.dot_general(q, keys, (((1,), (1,)), ((), ())), preferred_element_type=F32)
            mask = bias[j, :, :count]
            score = score * scale + jnp.concatenate([mask, mask], axis=0)
            top = jnp.max(score, axis=-1, keepdims=True)
            weights = jnp.exp(score - top)
            probs = (weights * (1.0 / jnp.sum(weights, axis=-1, keepdims=True))).astype(BF16)
            context = jnp.dot(probs, rvb[first : first + count, :], preferred_element_type=F32)
            context = context.astype(BF16)
            ctx[place.x, rows, cols] = jnp.concatenate([context[:128], context[128:]], axis=1)
        ctx_copy(0, n).start()
        ctx_copy(1, n).start()
        return carry

    lax.fori_loop(0, 4, two_heads, 0)

    def relay(n, carry):
        ctx_copy(0, n, arriving=True).wait_recv()
        ctx_copy(2, n).start()
        ctx_copy(1, n, arriving=True).wait_recv()
        ctx_copy(3, n).start()
        return carry

    og.arrive(0)
    og.start(6, 8)
    og.arrive(1)
    og.start(7, 9)
    og.arrive(2)
    og.start(10, 11)
    lax.fori_loop(0, 2, relay, 0)
    og.arrive(3)
    og.start(12, 18)
    og.arrive(4)
    og.start(13, 19)
    og.arrive(5)
    og.start(20)
    lax.fori_loop(2, 4, relay, 0)
    og.arrive(6, 7)
    og.start(14)
    og.arrive(10)
    og.start(15)
    og.arrive(11)
    og.start(16)
    og.arrive(8)
    og.start(22)
    og.arrive(9)
    og.start(23)

    def far(n, carry):
        ctx_copy(2, n, arriving=True).wait_recv()
        ctx_copy(3, n, arriving=True).wait_recv()
        return carry

    lax.fori_loop(0, 4, far, 0)

    def z_copy(chip):
        return pltpu.make_async_remote_copy(
            src_ref=sbuf.at[chip],
            dst_ref=rbuf.at[chip],
            send_sem=z_send.at[chip],
            recv_sem=z_recv.at[chip],
            device_id=place.dev(dh=1),
            device_id_type=MESH,
        )

    def multiply(block):
        chip = place.chip(*block)

        def term(s, carry):
            rows = pl.ds(pl.multiple_of(s * 1024, 1024), 1024)
            part = jnp.dot(ctx[s], obuf[chip, rows, :], preferred_element_type=F32)
            acc[4] += part
            return carry

        acc[4] = jnp.zeros((SPAN, 256), F32)
        lax.fori_loop(0, 4, term, 0)
        for i in range(4):
            there = pl.ds(pl.multiple_of(i * 128 + (1 - place.zh) * 64, 64), 64)
            here = pl.ds(pl.multiple_of(i * 128 + place.zh * 64, 64), 64)
            sbuf[chip, i] = acc[4, there, :].astype(BF16)
            acc[lax.div(chip, 2), pl.ds(pl.multiple_of(lax.rem(chip, 2) * 256 + i * 64, 64), 64), :] = acc[4, here, :]
        z_copy(chip).start()

    def f_copy(chip, d, arriving=False):
        to = ring(place.x, d, 4)
        source = ring(place.x, -d, 4) if arriving else place.x
        return pltpu.make_async_remote_copy(
            src_ref=fbuf.at[chip, to],
            dst_ref=gbuf.at[chip, source],
            send_sem=f_send.at[chip, d - 1],
            recv_sem=f_recv.at[chip, d - 1],
            device_id=place.dev(dx=d),
            device_id_type=MESH,
        )

    def settle(block):
        chip = place.chip(*block)
        z_copy(chip).wait_recv()
        kept = lax.div(chip, 2)
        for i in range(4):
            rows = pl.ds(pl.multiple_of(lax.rem(chip, 2) * 256 + i * 64, 64), 64)
            fbuf[chip, i] = (acc[kept, rows, :] + rbuf[chip, i].astype(F32)).astype(BF16)
        for d in (1, 3, 2):
            f_copy(chip, d).start()

    og.arrive(17)
    multiply(b0)
    og.arrive(18)
    multiply(b_dn)
    settle(b0)
    og.arrive(19)
    multiply(b_up)
    settle(b_dn)
    og.arrive(20)
    multiply(b_z)
    settle(b_up)
    og.arrive(22)
    multiply(b_zdn)
    settle(b_z)
    og.arrive(12, 13)
    og.start(21)
    og.arrive(23)
    multiply(b_zup)
    settle(b_zdn)
    og.arrive(14, 15, 16)
    og.start(24)
    og.arrive(21)
    multiply(b_far)
    settle(b_zup)
    og.arrive(24)
    multiply(b_zfar)
    settle(b_far)
    settle(b_zfar)

    def place_rows(chip, carry):
        for d in (1, 3, 2):
            f_copy(chip, d, arriving=True).wait_recv()
        gbuf[chip, place.x] = fbuf[chip, place.x]
        for core in range(2):
            for s in range(4):
                cols = pl.ds(pl.multiple_of(chip * 1024 + core * 512 + s * HEAD, HEAD), HEAD)
                out[:, cols] = gbuf[chip, s, :, core * HEAD : (core + 1) * HEAD]
        return carry

    lax.fori_loop(0, 8, place_rows, 0)

    qg.finish()
    og.finish()
    for d in (1, 3, 2):
        exchange(d).wait_send()

    def drain(n, carry):
        for kind in range(4):
            ctx_copy(kind, n).wait_send()
        return carry

    lax.fori_loop(0, 4, drain, 0)

    def drain_out(chip, carry):
        z_copy(chip).wait_send()
        for d in (1, 3, 2):
            f_copy(chip, d).wait_send()
        return carry

    lax.fori_loop(0, 8, drain_out, 0)


TILES = ((0, 128), (0, 256), (0, 384), (128, 384))


def local(activations, query_weight, key_matrix, value_matrix, output_weight, prompt_lengths):
    anywhere = pl.BlockSpec(memory_space=pl.ANY)
    dma = pltpu.SemaphoreType.DMA
    return pl.pallas_call(
        kernel,
        out_shape=jax.ShapeDtypeStruct((64, WIDTH), BF16),
        in_specs=[anywhere] * 5 + [pl.BlockSpec(memory_space=pltpu.SMEM)],
        out_specs=pl.BlockSpec(memory_space=pltpu.VMEM),
        scratch_shapes=[
            pltpu.VMEM((16, SPAN, DEPTH), BF16),
            pltpu.VMEM((16, DEPTH, COLS), BF16),
            pltpu.VMEM((8, OROWS, 256), BF16),
            pltpu.VMEM((5, SPAN, 256), F32),
            pltpu.VMEM((4, SPAN, QCOLS), BF16),
            pltpu.VMEM((SPAN, HEAD), F32),
            pltpu.VMEM((SPAN, HEAD), F32),
            pltpu.VMEM((4, 128, 384), F32),
            pltpu.VMEM((SPAN, HEAD), BF16),
            pltpu.VMEM((SPAN, HEAD), BF16),
            pltpu.VMEM((8, 4, 64, 256), BF16),
            pltpu.VMEM((8, 4, 64, 256), BF16),
            pltpu.VMEM((8, 4, 64, 256), BF16),
            pltpu.VMEM((8, 4, 64, 256), BF16),
            dma((25,)), dma((25,)), dma((25,)), dma((25,)), dma((3,)), dma((3,)),
            dma((4, 4)), dma((4, 4)), dma((8,)), dma((8,)), dma((8, 3)), dma((8, 3)),
            dma((16,)), dma((4,)),
        ],
        compiler_params=pltpu.CompilerParams(collective_id=0, has_side_effects=True, vmem_limit_bytes=62 << 20),
        cost_estimate=pl.CostEstimate(flops=20 * 10**9, bytes_accessed=12 << 20, transcendentals=1 << 20),
        name="attention_layer",
    )(activations, query_weight, key_matrix, value_matrix, output_weight, prompt_lengths)


def solution(mesh):
    placed = (
        P("group", None),
        P("group", "tp"),
        P("group", "tp"),
        P("group", "tp"),
        P("tp", "group"),
        P("group", None),
    )
    return jax.shard_map(
        local, mesh=mesh, in_specs=placed, out_specs=P(("group", "tp"), None), check_vma=False
    )
```

```python
import math

import jax
import jax.numpy as jnp
from jax import lax
from jax.experimental import pallas as pl
from jax.experimental.pallas import tpu as pltpu
from jax.sharding import PartitionSpec as P

MESH = pl.DeviceIdType.MESH
SPAN = 512
WIDTH = 8192
HEAD = 128
QCOLS = 1024
DEPTH = 512
OROWS = 4096
DOCS = 8
F32 = jnp.float32
BF16 = jnp.bfloat16


def ring(v, step, size):
    return lax.rem(v + (step + size), size)


class Place:
    def __init__(self):
        g = lax.axis_index("group")
        t = lax.axis_index("tp")
        self.g, self.t = g, t
        self.core = lax.rem(g, 2)
        self.y = lax.rem(lax.div(g, 2), 4)
        self.zl = lax.div(g, 8)
        self.x = lax.div(t, 2)
        self.zh = lax.rem(t, 2)

    def chip(self, dz, dy):
        return ring(self.zl, dz, 2) * 4 + ring(self.y, dy, 4)

    def dev(self, dz=0, dy=0, dc=0, dx=0, dh=0):
        group = self.chip(dz, dy) * 2 + ring(self.core, dc, 2)
        return (group, ring(self.x, dx, 4) * 2 + ring(self.zh, dh, 2))


class Gather:
    def __init__(self, place, view, rows, part, send, recv):
        self.place, self.view, self.send, self.recv = place, view, send, recv
        half = part // 2
        rest = rows - part
        self.a, self.a1, self.a2 = (0, part), (0, half), (half, part - half)
        self.b, self.b1, self.b2 = (part, rest), (part, rest // 2), (part + rest // 2, rest - rest // 2)
        self.all = (0, rows)
        up, down, over, twin = place.dev(dy=1), place.dev(dy=-1), place.dev(dz=1), place.dev(dc=1)
        mine, p_up, p_down, p_far = (0, 0), (0, 1), (0, -1), (0, 2)
        z_mine, z_up, z_down, z_far = (1, 0), (1, 1), (1, -1), (1, 2)
        self.steps = [
            (mine, self.a, up, p_down),
            (mine, self.a, down, p_up),
            (mine, self.b, over, z_mine),
            (mine, self.b, up, p_down),
            (mine, self.b, down, p_up),
            (mine, self.a, over, z_mine),
            (p_down, self.a1, up, p_far),
            (p_up, self.a2, down, p_far),
            (p_down, self.a, over, z_down),
            (p_up, self.a, over, z_up),
            (z_mine, self.b, up, z_down),
            (z_mine, self.b, down, z_up),
            (p_down, self.b1, up, p_far),
            (p_up, self.b2, down, p_far),
            (p_far, self.a, over, z_far),
            (z_down, self.b1, up, z_far),
            (z_up, self.b2, down, z_far),
        ]
        self.blocks = [mine, p_down, p_up, z_mine, p_far, z_down, z_up, z_far]
        for block in self.blocks:
            self.steps.append((block, self.all, twin, block))

    def copy(self, p, step, arriving=False):
        block, rows, target, lands = self.steps[step]
        core = self.place.core
        if arriving:
            block = lands
            if step >= 17:
                core = 1 - core
        ref = self.view(p, self.place.chip(*block), core, *rows)
        return pltpu.make_async_remote_copy(
            src_ref=ref,
            dst_ref=ref,
            send_sem=self.send.at[p, step],
            recv_sem=self.recv.at[p, step],
            device_id=target,
            device_id_type=MESH,
        )

    def start(self, p, *steps):
        for step in steps:
            self.copy(p, step).start()

    def arrive(self, p, *steps):
        for step in steps:
            self.copy(p, step, arriving=True).wait_recv()

    def finish(self, p):
        for step in range(len(self.steps)):
            self.copy(p, step).wait_send()


class Ring:
    def __init__(self, place, view, rows, send, recv):
        self.place, self.view, self.send, self.recv = place, view, send, recv
        whole, first, second = (0, rows), (0, rows // 2), (rows // 2, rows // 2)
        up, down, twin = place.dev(dy=1), place.dev(dy=-1), place.dev(dc=1)
        self.steps = [
            (0, whole, up, -1),
            (0, whole, down, 1),
            (-1, first, up, 2),
            (1, second, down, 2),
            (0, whole, twin, 0),
            (-1, whole, twin, -1),
            (1, whole, twin, 1),
            (2, whole, twin, 2),
        ]

    def copy(self, step, arriving=False):
        block, rows, target, lands = self.steps[step]
        core = self.place.core
        if arriving:
            block = lands
            if step >= 4:
                core = 1 - core
        ref = self.view(ring(self.place.y, block, 4), core, *rows)
        return pltpu.make_async_remote_copy(
            src_ref=ref,
            dst_ref=ref,
            send_sem=self.send.at[step],
            recv_sem=self.recv.at[step],
            device_id=target,
            device_id_type=MESH,
        )

    def start(self, *steps):
        for step in steps:
            self.copy(step).start()

    def arrive(self, *steps):
        for step in steps:
            self.copy(step, arriving=True).wait_recv()

    def finish(self):
        for step in range(len(self.steps)):
            self.copy(step).wait_send()


def starts_of(row, lengths):
    start = jnp.zeros_like(row)
    end = 0
    for j in range(DOCS):
        end = end + lengths[j]
        start = start + jnp.where(row >= end, lengths[j], 0)
    return start


def kernel(
    act, wq, wk, wv, wo, lens, out,
    xbuf, wbuf, obuf, acc, ctx, cosb, sinb, bias, rkb, rvb, sbuf, rbuf, fbuf, gbuf,
    q_send, q_recv, o_send, o_recv, e_send, e_recv, c_send, c_recv, z_send, z_recv, f_send, f_recv,
    x_sem, w_sem,
):
    place = Place()
    me = place.g
    role = lax.rem(place.zl + place.zh, 2)
    swap = lax.rem(place.core + role, 2)

    kv_own = [
        pltpu.make_async_copy(wk, wbuf.at[0, me, :, pl.ds(0, HEAD)], w_sem.at[0]),
        pltpu.make_async_copy(wv, wbuf.at[0, me, :, pl.ds(HEAD, HEAD)], w_sem.at[1]),
    ]

    def q_own(n):
        cols = pl.ds(pl.multiple_of(n * 256, 256), 256)
        return pltpu.make_async_copy(wq.at[:, cols], wbuf.at[n + 1, me], w_sem.at[n + 2])

    for copy in kv_own:
        copy.start()
    for n in range(4):
        q_own(n).start()

    def x_copy(s):
        cols = pl.ds(pl.multiple_of(s * DEPTH, DEPTH), DEPTH)
        return pltpu.make_async_copy(act.at[:, cols], xbuf.at[s], x_sem.at[s])

    for s in range(16):
        x_copy(s).start()

    own_o = pltpu.make_async_copy(
        wo.at[:, pl.ds(pl.multiple_of(place.x * HEAD, HEAD), HEAD)],
        obuf.at[place.y, place.core, pl.ds(pl.multiple_of(place.x * 1024, 1024), 1024)],
        w_sem.at[6],
    )

    barrier = pltpu.get_barrier_semaphore()
    partners = [place.dev(dy=1), place.dev(dy=-1), place.dev(dc=1), place.dev(dz=1, dh=1)]
    partners += [place.dev(dx=d) for d in (1, 2, 3)]
    partners += [place.dev(dx=d, dz=1) for d in range(4)]
    partners += [place.dev(dx=d, dz=1, dc=1) for d in range(4)]
    for partner in partners:
        pl.semaphore_signal(barrier, inc=1, device_id=partner, device_id_type=MESH)
    pl.semaphore_wait(barrier, len(partners))

    def w_view(p, chip, core, first, count):
        return wbuf.at[p, chip * 2 + core, pl.ds(first, count)]

    def o_view(y, core, first, count):
        return obuf.at[y, core, pl.ds(first, count)]

    qg = Gather(place, w_view, DEPTH, 192, q_send, q_recv)
    og = Ring(place, o_view, OROWS, o_send, o_recv)
    first_steps = (0, 1, 2, 17, 3, 4, 5)

    for copy in kv_own:
        copy.wait()
    qg.start(0, *first_steps)

    def exchange(d, arriving=False):
        to = ring(place.x, d, 4)
        row = ring(place.x, -d, 4) if arriving else place.x
        core = place.core if arriving else ring(place.core, swap, 2)
        return pltpu.make_async_remote_copy(
            src_ref=wo.at[:, pl.ds(pl.multiple_of(to * HEAD, HEAD), HEAD)],
            dst_ref=obuf.at[place.y, core, pl.ds(pl.multiple_of(row * 1024, 1024), 1024)],
            send_sem=e_send.at[d],
            recv_sem=e_recv.at[d],
            device_id=place.dev(dx=d, dz=swap, dc=swap),
            device_id_type=MESH,
        )

    def exchange_start():
        for d in (1, 3, 2):
            exchange(d).start()

        @pl.when(swap == 0)
        def _():
            own_o.start()

        @pl.when(swap == 1)
        def _():
            exchange(0).start()

    def exchange_arrive():
        for d in (1, 3, 2):
            exchange(d, arriving=True).wait_recv()

        @pl.when(swap == 0)
        def _():
            own_o.wait()

        @pl.when(swap == 1)
        def _():
            exchange(0, arriving=True).wait_recv()

    lengths = [lens[0, j] for j in range(DOCS)]
    row = lax.broadcasted_iota(jnp.int32, (SPAN, HEAD), 0)
    lane = lax.broadcasted_iota(jnp.int32, (SPAN, HEAD), 1)
    low = lane < HEAD // 2
    index = jnp.where(low, lane, lane - HEAD // 2).astype(F32)
    freq = jnp.exp(index * (-2.0 * math.log(500000.0) / HEAD))
    angle = (row - starts_of(row, lengths)).astype(F32) * freq
    cosb[...] = jnp.cos(angle)
    sine = jnp.sin(angle)
    sinb[...] = jnp.where(low, -sine, sine)
    for j, (first, count) in enumerate(TILES):
        q = lax.broadcasted_iota(jnp.int32, (128, count), 0) + j * 128
        k = lax.broadcasted_iota(jnp.int32, (128, count), 1) + first
        keep = (k >= starts_of(q, lengths)) & (k <= q)
        bias[j, :, :count] = jnp.where(keep, 0.0, -1e30)

    for s in range(16):
        x_copy(s).wait()

    def project(p, block, other=False, fresh=False):
        slot = place.chip(*block) * 2 + ((1 - place.core) if other else place.core)
        part = jnp.dot(xbuf[slot], wbuf[p, slot], preferred_element_type=F32)
        if fresh:
            acc[4] = part
        else:
            acc[4] += part

    def rotate(u):
        return u * cosb[...] + pltpu.roll(u, HEAD // 2, 1) * sinb[...]

    scale = 1.0 / math.sqrt(HEAD)
    far = SPAN // 2
    routes = [
        (0, 0, 0, SPAN, dict(dx=1), (0, -1)),
        (0, 0, 0, SPAN, dict(dx=-1), (0, 1)),
        (0, 0, 0, SPAN, dict(dz=1), (1, 0)),
        (0, -1, 0, far, dict(dx=1), (0, 2)),
        (0, 1, far, far, dict(dx=-1), (0, 2)),
        (1, 0, 0, SPAN, dict(dx=1), (1, -1)),
        (1, 0, 0, SPAN, dict(dx=-1), (1, 1)),
        (1, -1, 0, far, dict(dx=1), (1, 2)),
        (1, 1, far, far, dict(dx=-1), (1, 2)),
    ]

    def ctx_copy(kind, n, arriving=False):
        which, owner, first, count, target, lands = routes[kind]
        if arriving:
            which, owner = lands
        cols = pl.ds(pl.multiple_of(n * 256, 256), 256)
        ref = ctx.at[ring(place.zl, which, 2), ring(place.x, owner, 4), pl.ds(first, count), cols]
        return pltpu.make_async_remote_copy(
            src_ref=ref,
            dst_ref=ref,
            send_sem=c_send.at[kind, n],
            recv_sem=c_recv.at[kind, n],
            device_id=place.dev(**target),
            device_id_type=MESH,
        )

    def ctx_start(n, *kinds):
        for kind in kinds:
            ctx_copy(kind, n).start()

    def ctx_arrive(n, *kinds):
        for kind in kinds:
            ctx_copy(kind, n, arriving=True).wait_recv()

    def two_heads(n):
        pair = acc[4]
        rq = [rotate(pair[:, :HEAD]).astype(BF16), rotate(pair[:, HEAD:]).astype(BF16)]
        cols = pl.ds(pl.multiple_of(n * 256, 256), 256)
        for j, (first, count) in enumerate(TILES):
            rows = slice(j * 128, (j + 1) * 128)
            q = jnp.concatenate([rq[0][rows], rq[1][rows]], axis=0)
            keys = rkb[first : first + count, :]
            score = lax.dot_general(q, keys, (((1,), (1,)), ((), ())), preferred_element_type=F32)
            mask = bias[j, :, :count]
            score = score * scale + jnp.concatenate([mask, mask], axis=0)
            top = jnp.max(score, axis=-1, keepdims=True)
            weights = jnp.exp(score - top)
            probs = (weights * (1.0 / jnp.sum(weights, axis=-1, keepdims=True))).astype(BF16)
            context = jnp.dot(probs, rvb[first : first + count, :], preferred_element_type=F32)
            context = context.astype(BF16)
            ctx[place.zl, place.x, rows, cols] = jnp.concatenate([context[:128], context[128:]], axis=1)

    b0, b_dn, b_up, b_z, b_far, b_zdn, b_zup, b_zfar = qg.blocks

    def phase(p, carry):
        project(p, b0, fresh=True)
        qg.arrive(p, 17)
        project(p, b0, other=True)
        qg.arrive(p, 0)
        qg.start(p, 6, 8)
        qg.arrive(p, 1)
        qg.start(p, 7, 9)
        qg.arrive(p, 2)
        qg.start(p, 10, 11)

        @pl.when(p < 4)
        def _():
            q_own(p).wait()
            qg.start(p + 1, *first_steps)

        @pl.when(p == 1)
        def _():
            exchange_start()

        @pl.when(p >= 2)
        def _():
            ctx_arrive(p - 2, 0)
            ctx_start(p - 2, 3)
            ctx_arrive(p - 2, 1)
            ctx_start(p - 2, 4)
            ctx_arrive(p - 2, 2)
            ctx_start(p - 2, 5, 6)

        qg.arrive(p, 3)
        qg.start(p, 12, 18)
        qg.arrive(p, 4)
        qg.start(p, 13, 19)
        project(p, b_dn)
        project(p, b_up)
        qg.arrive(p, 5)
        qg.start(p, 20)
        qg.arrive(p, 6, 7)
        qg.start(p, 14)
        qg.arrive(p, 10)
        qg.start(p, 15)
        qg.arrive(p, 11)
        qg.start(p, 16)
        project(p, b_z)
        qg.arrive(p, 18)
        project(p, b_dn, other=True)
        qg.arrive(p, 19)
        project(p, b_up, other=True)
        qg.arrive(p, 20)
        project(p, b_z, other=True)
        qg.arrive(p, 8)
        qg.start(p, 22)
        qg.arrive(p, 9)
        qg.start(p, 23)

        @pl.when(p == 4)
        def _():
            exchange_arrive()
            og.start(0, 1, 4)

        project(p, b_zdn)
        project(p, b_zup)
        qg.arrive(p, 12, 13)
        qg.start(p, 21)
        project(p, b_far)
        qg.arrive(p, 22)
        project(p, b_zdn, other=True)
        qg.arrive(p, 23)
        project(p, b_zup, other=True)

        @pl.when(p >= 2)
        def _():
            ctx_arrive(p - 2, 5)
            ctx_start(p - 2, 7)
            ctx_arrive(p - 2, 6)
            ctx_start(p - 2, 8)

        qg.arrive(p, 21)
        project(p, b_far, other=True)
        qg.arrive(p, 14, 15, 16)
        qg.start(p, 24)
        project(p, b_zfar)
        qg.arrive(p, 24)
        project(p, b_zfar, other=True)

        @pl.when(p == 0)
        def _():
            kv = acc[4]
            rkb[...] = rotate(kv[:, :HEAD]).astype(BF16)
            rvb[...] = kv[:, HEAD:].astype(BF16)

        @pl.when(p > 0)
        def _():
            two_heads(p - 1)
            ctx_start(p - 1, 2, 0, 1)

        return carry

    lax.fori_loop(0, 5, phase, 0)

    ctx_arrive(3, 2)
    ctx_start(3, 5, 6)
    ctx_arrive(3, 0)
    ctx_start(3, 3)
    ctx_arrive(3, 1)
    ctx_start(3, 4)
    og.arrive(0)
    og.start(2, 5)
    og.arrive(1)
    og.start(3, 6)
    ctx_arrive(3, 5)
    ctx_start(3, 7)
    ctx_arrive(3, 6)
    ctx_start(3, 8)

    def ctx_far(n, carry):
        ctx_arrive(n, 3, 4, 7, 8)
        return carry

    lax.fori_loop(0, 4, ctx_far, 0)

    def z_copy(y):
        return pltpu.make_async_remote_copy(
            src_ref=sbuf.at[y],
            dst_ref=rbuf.at[y],
            send_sem=z_send.at[y],
            recv_sem=z_recv.at[y],
            device_id=place.dev(dz=1, dh=1),
            device_id_type=MESH,
        )

    def multiply(block):
        y = ring(place.y, block, 4)

        def tokens(s, carry):
            def term(x, inner):
                rows = pl.ds(pl.multiple_of(x * 1024, 1024), 1024)
                weights = jnp.concatenate([obuf[y, place.zh, rows, :], obuf[y, 1 - place.zh, rows, :]], axis=1)
                acc[4] += jnp.dot(ctx[s, x], weights, preferred_element_type=F32)
                return inner

            acc[4] = jnp.zeros((SPAN, 256), F32)
            lax.fori_loop(0, 4, term, 0)
            for i in range(4):
                there = pl.ds(pl.multiple_of(i * 128 + (1 - place.zh) * 64, 64), 64)
                here = pl.ds(pl.multiple_of(i * 128 + place.zh * 64, 64), 64)
                sbuf[y, s, i] = acc[4, there, :].astype(BF16)
                acc[y, pl.ds(pl.multiple_of(s * 256 + i * 64, 64), 64), :] = acc[4, here, :]
            return carry

        lax.fori_loop(0, 2, tokens, 0)
        z_copy(y).start()

    def f_copy(y, k, arriving=False):
        dz, dx = k // 4, k % 4
        if arriving:
            spot = ring(place.zl, dz, 2) * 4 + ring(place.x, -dx, 4)
        else:
            spot = place.zl * 4 + place.x
        return pltpu.make_async_remote_copy(
            src_ref=fbuf.at[y, ring(place.zl, dz, 2), ring(place.x, dx, 4)],
            dst_ref=gbuf.at[y, spot],
            send_sem=f_send.at[y, k - 1],
            recv_sem=f_recv.at[y, k - 1],
            device_id=place.dev(dx=dx, dz=dz),
            device_id_type=MESH,
        )

    f_order = (6, 5, 7, 4, 2, 1, 3)

    def settle(block):
        y = ring(place.y, block, 4)
        z_copy(y).wait_recv()
        for s in range(2):
            for i in range(4):
                kept = acc[y, s * 256 + i * 64 : s * 256 + (i + 1) * 64, :]
                fbuf[y, s, i] = (kept + rbuf[y, s, i].astype(F32)).astype(BF16)
        for k in f_order:
            f_copy(y, k).start()

    og.arrive(4)
    multiply(0)
    og.arrive(5)
    multiply(-1)
    settle(0)
    og.arrive(2, 3)
    og.start(7)
    og.arrive(6)
    multiply(1)
    settle(-1)
    og.arrive(7)
    multiply(2)
    settle(1)
    settle(2)

    def place_rows(y, carry):
        for k in f_order:
            f_copy(y, k, arriving=True).wait_recv()
        gbuf[y, place.zl * 4 + place.x] = fbuf[y, place.zl, place.x]
        for zl in range(2):
            taken = lax.rem(place.zh + zl, 2)
            for x in range(4):
                for half in range(2):
                    first = half * 4096 + y * 1024 + taken * 512 + x * HEAD
                    out[:, pl.ds(pl.multiple_of(first, HEAD), HEAD)] = gbuf[y, zl * 4 + x, :, half * HEAD : (half + 1) * HEAD]
        return carry

    lax.fori_loop(0, 4, place_rows, 0)

    def drain(p, carry):
        qg.finish(p)
        return carry

    lax.fori_loop(0, 5, drain, 0)
    og.finish()
    for d in (1, 3, 2):
        exchange(d).wait_send()

    @pl.when(swap == 1)
    def _():
        exchange(0).wait_send()

    def drain_out(n, carry):
        for kind in range(len(routes)):
            ctx_copy(kind, n).wait_send()
        z_copy(n).wait_send()
        for k in f_order:
            f_copy(n, k).wait_send()
        return carry

    lax.fori_loop(0, 4, drain_out, 0)


TILES = ((0, 128), (0, 256), (0, 384), (128, 384))


def local(activations, query_weight, key_matrix, value_matrix, output_weight, prompt_lengths):
    anywhere = pl.BlockSpec(memory_space=pl.ANY)
    dma = pltpu.SemaphoreType.DMA
    return pl.pallas_call(
        kernel,
        out_shape=jax.ShapeDtypeStruct((64, WIDTH), BF16),
        in_specs=[anywhere] * 5 + [pl.BlockSpec(memory_space=pltpu.SMEM)],
        out_specs=pl.BlockSpec(memory_space=pltpu.VMEM),
        scratch_shapes=[
            pltpu.VMEM((16, SPAN, DEPTH), BF16),
            pltpu.VMEM((5, 16, DEPTH, 256), BF16),
            pltpu.VMEM((4, 2, OROWS, HEAD), BF16),
            pltpu.VMEM((5, SPAN, 256), F32),
            pltpu.VMEM((2, 4, SPAN, QCOLS), BF16),
            pltpu.VMEM((SPAN, HEAD), F32),
            pltpu.VMEM((SPAN, HEAD), F32),
            pltpu.VMEM((4, 128, 384), F32),
            pltpu.VMEM((SPAN, HEAD), BF16),
            pltpu.VMEM((SPAN, HEAD), BF16),
            pltpu.VMEM((4, 2, 4, 64, 256), BF16),
            pltpu.VMEM((4, 2, 4, 64, 256), BF16),
            pltpu.VMEM((4, 2, 4, 64, 256), BF16),
            pltpu.VMEM((4, 8, 64, 256), BF16),
            dma((5, 25)), dma((5, 25)), dma((8,)), dma((8,)), dma((4,)), dma((4,)),
            dma((9, 4)), dma((9, 4)), dma((4,)), dma((4,)), dma((4, 7)), dma((4, 7)),
            dma((16,)), dma((7,)),
        ],
        compiler_params=pltpu.CompilerParams(collective_id=0, has_side_effects=True, vmem_limit_bytes=62 << 20),
        cost_estimate=pl.CostEstimate(flops=20 * 10**9, bytes_accessed=12 << 20, transcendentals=1 << 20),
        name="attention_layer",
    )(activations, query_weight, key_matrix, value_matrix, output_weight, prompt_lengths)


def solution(mesh):
    placed = (
        P("group", None),
        P("group", "tp"),
        P("group", "tp"),
        P("group", "tp"),
        P("tp", "group"),
        P("group", None),
    )
    return jax.shard_map(
        local, mesh=mesh, in_specs=placed, out_specs=P(("group", "tp"), None), check_vma=False
    )
```

```python
import math

import jax
import jax.numpy as jnp
from jax import lax
from jax.experimental import pallas as pl
from jax.experimental.pallas import tpu as pltpu
from jax.sharding import PartitionSpec as P

MESH = pl.DeviceIdType.MESH
SPAN = 512
WIDTH = 8192
HEAD = 128
QCOLS = 1024
COLS = 1280
DEPTH = 512
OROWS = 4096
DOCS = 8
F32 = jnp.float32
BF16 = jnp.bfloat16


def ring(v, step, size):
    return lax.rem(v + (step + size), size)


class Place:
    def __init__(self):
        g = lax.axis_index("group")
        t = lax.axis_index("tp")
        self.g, self.t = g, t
        self.core = lax.rem(g, 2)
        self.y = lax.rem(lax.div(g, 2), 4)
        self.zl = lax.div(g, 8)
        self.x = lax.div(t, 2)
        self.zh = lax.rem(t, 2)

    def chip(self, dz, dy):
        return ring(self.zl, dz, 2) * 4 + ring(self.y, dy, 4)

    def dev(self, dz=0, dy=0, dc=0, dx=0, dh=0):
        group = self.chip(dz, dy) * 2 + ring(self.core, dc, 2)
        return (group, ring(self.x, dx, 4) * 2 + ring(self.zh, dh, 2))


class Gather:
    def __init__(self, place, view, rows, part, send, recv):
        self.place, self.view, self.send, self.recv = place, view, send, recv
        half = part // 2
        rest = rows - part
        self.a, self.a1, self.a2 = (0, part), (0, half), (half, part - half)
        self.b, self.b1, self.b2 = (part, rest), (part, rest // 2), (part + rest // 2, rest - rest // 2)
        self.all = (0, rows)
        up, down, over, twin = place.dev(dy=1), place.dev(dy=-1), place.dev(dz=1), place.dev(dc=1)
        mine, p_up, p_down, p_far = (0, 0), (0, 1), (0, -1), (0, 2)
        z_mine, z_up, z_down, z_far = (1, 0), (1, 1), (1, -1), (1, 2)
        self.steps = [
            (mine, self.a, up, p_down),
            (mine, self.a, down, p_up),
            (mine, self.b, over, z_mine),
            (mine, self.b, up, p_down),
            (mine, self.b, down, p_up),
            (mine, self.a, over, z_mine),
            (p_down, self.a1, up, p_far),
            (p_up, self.a2, down, p_far),
            (p_down, self.a, over, z_down),
            (p_up, self.a, over, z_up),
            (z_mine, self.b, up, z_down),
            (z_mine, self.b, down, z_up),
            (p_down, self.b1, up, p_far),
            (p_up, self.b2, down, p_far),
            (p_far, self.a, over, z_far),
            (z_down, self.b1, up, z_far),
            (z_up, self.b2, down, z_far),
        ]
        self.blocks = [mine, p_down, p_up, z_mine, p_far, z_down, z_up, z_far]
        for block in self.blocks:
            self.steps.append((block, self.all, twin, block))

    def copy(self, step, arriving=False):
        block, rows, target, lands = self.steps[step]
        core = self.place.core
        if arriving:
            block = lands
            if step >= 17:
                core = 1 - core
        ref = self.view(self.place.chip(*block), core, *rows)
        return pltpu.make_async_remote_copy(
            src_ref=ref,
            dst_ref=ref,
            send_sem=self.send.at[step],
            recv_sem=self.recv.at[step],
            device_id=target,
            device_id_type=MESH,
        )

    def start(self, *steps):
        for step in steps:
            self.copy(step).start()

    def arrive(self, *steps):
        for step in steps:
            self.copy(step, arriving=True).wait_recv()

    def finish(self):
        for step in range(len(self.steps)):
            self.copy(step).wait_send()


class Ring:
    def __init__(self, place, view, rows, send, recv):
        self.place, self.view, self.send, self.recv = place, view, send, recv
        whole, first, second = (0, rows), (0, rows // 2), (rows // 2, rows // 2)
        up, down, twin = place.dev(dy=1), place.dev(dy=-1), place.dev(dc=1)
        self.steps = [
            (0, whole, up, -1),
            (0, whole, down, 1),
            (-1, first, up, 2),
            (1, second, down, 2),
            (0, whole, twin, 0),
            (-1, whole, twin, -1),
            (1, whole, twin, 1),
            (2, whole, twin, 2),
        ]

    def copy(self, step, arriving=False):
        block, rows, target, lands = self.steps[step]
        core = self.place.core
        if arriving:
            block = lands
            if step >= 4:
                core = 1 - core
        ref = self.view(ring(self.place.y, block, 4), core, *rows)
        return pltpu.make_async_remote_copy(
            src_ref=ref,
            dst_ref=ref,
            send_sem=self.send.at[step],
            recv_sem=self.recv.at[step],
            device_id=target,
            device_id_type=MESH,
        )

    def start(self, *steps):
        for step in steps:
            self.copy(step).start()

    def arrive(self, *steps):
        for step in steps:
            self.copy(step, arriving=True).wait_recv()

    def finish(self):
        for step in range(len(self.steps)):
            self.copy(step).wait_send()


def starts_of(row, lengths):
    start = jnp.zeros_like(row)
    end = 0
    for j in range(DOCS):
        end = end + lengths[j]
        start = start + jnp.where(row >= end, lengths[j], 0)
    return start


def kernel(
    act, wq, wk, wv, wo, lens, out,
    xown, xpar, wbuf, obuf, acc, tmp, psend, precv, ctx, cosb, sinb, bias, rkb, rvb, sbuf, rbuf, fbuf, gbuf,
    w_send, w_recv, o_send, o_recv, x_send, x_recv, p_send, p_recv, e_send, e_recv, c_send, c_recv,
    z_send, z_recv, f_send, f_recv, x_sem, w_sem,
):
    place = Place()
    mine = place.y * 2 + place.core

    own = [
        pltpu.make_async_copy(wq, wbuf.at[mine, :, pl.ds(0, QCOLS)], w_sem.at[0]),
        pltpu.make_async_copy(wk, wbuf.at[mine, :, pl.ds(QCOLS, HEAD)], w_sem.at[1]),
        pltpu.make_async_copy(wv, wbuf.at[mine, :, pl.ds(QCOLS + HEAD, HEAD)], w_sem.at[2]),
    ]
    for copy in own:
        copy.start()
    chip0 = place.chip(0, 0)
    own_o = pltpu.make_async_copy(
        wo.at[:, pl.ds(pl.multiple_of(place.x * HEAD, HEAD), HEAD)],
        obuf.at[chip0, place.core, pl.ds(pl.multiple_of(place.x * 1024, 1024), 1024)],
        w_sem.at[3],
    )

    def own_x(s):
        cols = pl.ds(pl.multiple_of((place.zl * 8 + s) * DEPTH, DEPTH), DEPTH)
        return pltpu.make_async_copy(act.at[:, cols], xown.at[s], x_sem.at[s])

    for s in range(8):
        own_x(s).start()
    own_o.start()

    barrier = pltpu.get_barrier_semaphore()
    partners = [
        place.dev(dy=1), place.dev(dy=-1), place.dev(dz=1), place.dev(dc=1),
        place.dev(dx=1), place.dev(dx=2), place.dev(dx=3), place.dev(dh=1),
    ]
    for partner in partners:
        pl.semaphore_signal(barrier, inc=1, device_id=partner, device_id_type=MESH)
    pl.semaphore_wait(barrier, len(partners))

    def w_view(y, core, first, count):
        return wbuf.at[y * 2 + core, pl.ds(first, count)]

    def o_view(chip, core, first, count):
        return obuf.at[chip, core, pl.ds(first, count)]

    wg = Ring(place, w_view, DEPTH, w_send, w_recv)
    og = Gather(place, o_view, OROWS, 1024, o_send, o_recv)

    x_routes = [(0, dict(dz=1), 0), (0, dict(dx=1), -1), (0, dict(dx=-1), 1), (-1, dict(dx=1), 2), (1, dict(dx=-1), 2)]

    def x_copy(kind, i, arriving=False):
        owner, target, lands = x_routes[kind]
        slot = ring(place.x, lands if arriving else owner, 4) * 2 + i // 2
        rows = pl.ds((i % 2) * 256, 256)
        ref = xpar.at[slot, rows]
        source = ref
        if kind == 0:
            first = (1 - place.zl) * 4096 + slot * DEPTH
            source = act.at[rows, pl.ds(pl.multiple_of(first, DEPTH), DEPTH)]
        return pltpu.make_async_remote_copy(
            src_ref=source,
            dst_ref=ref,
            send_sem=x_send.at[kind, i],
            recv_sem=x_recv.at[kind, i],
            device_id=place.dev(**target),
            device_id_type=MESH,
        )

    for i in range(4):
        x_copy(0, i).start()

    def exchange(d, arriving=False):
        to = ring(place.x, d, 4)
        row = ring(place.x, -d, 4) if arriving else place.x
        return pltpu.make_async_remote_copy(
            src_ref=wo.at[:, pl.ds(pl.multiple_of(to * HEAD, HEAD), HEAD)],
            dst_ref=obuf.at[chip0, place.core, pl.ds(pl.multiple_of(row * 1024, 1024), 1024)],
            send_sem=e_send.at[d - 1],
            recv_sem=e_recv.at[d - 1],
            device_id=place.dev(dx=d),
            device_id_type=MESH,
        )

    for d in (1, 3, 2):
        exchange(d).start()
    for copy in own:
        copy.wait()
    wg.start(0, 1, 4)

    lengths = [lens[0, j] for j in range(DOCS)]
    row = lax.broadcasted_iota(jnp.int32, (SPAN, HEAD), 0)
    lane = lax.broadcasted_iota(jnp.int32, (SPAN, HEAD), 1)
    low = lane < HEAD // 2
    index = jnp.where(low, lane, lane - HEAD // 2).astype(F32)
    freq = jnp.exp(index * (-2.0 * math.log(500000.0) / HEAD))
    angle = (row - starts_of(row, lengths)).astype(F32) * freq
    cosb[...] = jnp.cos(angle)
    sine = jnp.sin(angle)
    sinb[...] = jnp.where(low, -sine, sine)
    for j, (first, count) in enumerate(TILES):
        q = lax.broadcasted_iota(jnp.int32, (128, count), 0) + j * 128
        k = lax.broadcasted_iota(jnp.int32, (128, count), 1) + first
        keep = (k >= starts_of(q, lengths)) & (k <= q)
        bias[j, :, :count] = jnp.where(keep, 0.0, -1e30)

    for s in range(8):
        own_x(s).wait()

    def project(block, other=False, fresh=False):
        slot = ring(place.y, block, 4) * 2 + ((1 - place.core) if other else place.core)

        def tile(n, carry):
            cols = pl.ds(pl.multiple_of(n * 256, 256), 256)
            part = jnp.dot(xown[slot], wbuf[slot, :, cols], preferred_element_type=F32)
            if fresh:
                acc[n] = part
            else:
                acc[n] += part
            return carry

        lax.fori_loop(0, COLS // 256, tile, 0)

    def x_pass(i):
        x_copy(0, i, arriving=True).wait_recv()
        x_copy(1, i).start()
        x_copy(2, i).start()

    project(0, fresh=True)
    x_pass(0)
    wg.arrive(4)
    project(0, other=True)
    for d in (1, 3, 2):
        exchange(d, arriving=True).wait_recv()
    own_o.wait()
    og.start(2, 5, 17)
    x_pass(1)
    x_pass(2)
    x_pass(3)
    for i in (0, 1):
        x_copy(1, i, arriving=True).wait_recv()
        x_copy(3, i).start()
    wg.arrive(0)
    wg.start(2, 5)
    wg.arrive(1)
    wg.start(3, 6)
    og.start(0, 1, 3, 4)
    project(-1)
    project(1)
    for i in (2, 3):
        x_copy(2, i, arriving=True).wait_recv()
        x_copy(4, i).start()
    wg.arrive(5)
    project(-1, other=True)
    wg.arrive(6)
    project(1, other=True)
    wg.arrive(2, 3)
    wg.start(7)
    project(2)
    wg.arrive(7)
    project(2, other=True)
    for i in range(4):
        if i >= 2:
            x_copy(1, i, arriving=True).wait_recv()
        else:
            x_copy(2, i, arriving=True).wait_recv()
    for i in (0, 1):
        x_copy(3, i, arriving=True).wait_recv()
        x_copy(4, i + 2, arriving=True).wait_recv()

    def p_copy(n):
        return pltpu.make_async_remote_copy(
            src_ref=psend.at[n],
            dst_ref=precv.at[n],
            send_sem=p_send.at[n],
            recv_sem=p_recv.at[n],
            device_id=place.dev(dz=1),
            device_id_type=MESH,
        )

    def their_tile(i, carry):
        n = lax.rem(i + 4, 5)
        cols = pl.ds(pl.multiple_of(n * 256, 256), 256)

        def term(s, inner):
            tmp[...] += jnp.dot(xpar[s], wbuf[s, :, cols], preferred_element_type=F32)
            return inner

        tmp[...] = jnp.dot(xpar[0], wbuf[0, :, cols], preferred_element_type=F32)
        lax.fori_loop(1, 8, term, 0)
        psend[n] = tmp[...].astype(BF16)
        p_copy(n).start()
        return carry

    lax.fori_loop(0, 5, their_tile, 0)

    def rotate(u):
        return u * cosb[...] + pltpu.roll(u, HEAD // 2, 1) * sinb[...]

    scale = 1.0 / math.sqrt(HEAD)

    def ctx_copy(kind, n, arriving=False):
        cols = pl.ds(pl.multiple_of(n * 256, 256), 256)
        dx = 1 if kind in (0, 2) else -1
        if kind < 2:
            owner, rows = 0, pl.ds(0, SPAN)
        else:
            owner, rows = -dx, pl.ds(0 if kind == 2 else 256, 256)
        if arriving:
            owner = owner - dx
        ref = ctx.at[ring(place.x, owner % 4, 4), rows, cols]
        return pltpu.make_async_remote_copy(
            src_ref=ref,
            dst_ref=ref,
            send_sem=c_send.at[kind, n],
            recv_sem=c_recv.at[kind, n],
            device_id=place.dev(dx=dx),
            device_id_type=MESH,
        )

    def two_heads(n):
        p_copy(n).wait_recv()
        pair = acc[n] + precv[n].astype(F32)
        rq = [rotate(pair[:, :HEAD]).astype(BF16), rotate(pair[:, HEAD:]).astype(BF16)]
        cols = pl.ds(n * 256, 256)
        for j, (first, count) in enumerate(TILES):
            rows = slice(j * 128, (j + 1) * 128)
            q = jnp.concatenate([rq[0][rows], rq[1][rows]], axis=0)
            keys = rkb[first : first + count, :]
            score = lax.dot_general(q, keys, (((1,), (1,)), ((), ())), preferred_element_type=F32)
            mask = bias[j, :, :count]
            score = score * scale + jnp.concatenate([mask, mask], axis=0)
            top = jnp.max(score, axis=-1, keepdims=True)
            weights = jnp.exp(score - top)
            probs = (weights * (1.0 / jnp.sum(weights, axis=-1, keepdims=True))).astype(BF16)
            context = jnp.dot(probs, rvb[first : first + count, :], preferred_element_type=F32)
            context = context.astype(BF16)
            ctx[place.x, rows, cols] = jnp.concatenate([context[:128], context[128:]], axis=1)
        ctx_copy(0, n).start()
        ctx_copy(1, n).start()

    def relay(n):
        ctx_copy(0, n, arriving=True).wait_recv()
        ctx_copy(2, n).start()
        ctx_copy(1, n, arriving=True).wait_recv()
        ctx_copy(3, n).start()

    og.arrive(2)
    og.start(10, 11)
    og.arrive(0)
    og.start(6, 8)
    og.arrive(1)
    og.start(7, 9)
    p_copy(4).wait_recv()
    kv = acc[4] + precv[4].astype(F32)
    rkb[...] = rotate(kv[:, :HEAD]).astype(BF16)
    rvb[...] = kv[:, HEAD:].astype(BF16)
    two_heads(0)
    og.arrive(5)
    og.start(20)
    two_heads(1)
    og.arrive(3)
    og.start(12, 18)
    og.arrive(4)
    og.start(13, 19)
    relay(0)
    two_heads(2)
    relay(1)
    two_heads(3)
    relay(2)
    og.arrive(6, 7)
    og.start(14)
    og.arrive(10)
    og.start(15)
    og.arrive(11)
    og.start(16)
    relay(3)
    og.arrive(8)
    og.start(22)
    og.arrive(9)
    og.start(23)

    def far(n, carry):
        ctx_copy(2, n, arriving=True).wait_recv()
        ctx_copy(3, n, arriving=True).wait_recv()
        return carry

    lax.fori_loop(0, 4, far, 0)

    def z_copy(chip):
        return pltpu.make_async_remote_copy(
            src_ref=sbuf.at[chip],
            dst_ref=rbuf.at[chip],
            send_sem=z_send.at[chip],
            recv_sem=z_recv.at[chip],
            device_id=place.dev(dh=1),
            device_id_type=MESH,
        )

    def multiply(block):
        chip = place.chip(*block)

        def term(s, carry):
            rows = pl.ds(pl.multiple_of(s * 1024, 1024), 1024)
            weights = jnp.concatenate([obuf[chip, 0, rows, :], obuf[chip, 1, rows, :]], axis=1)
            part = jnp.dot(ctx[s], weights, preferred_element_type=F32)
            acc[4] += part
            return carry

        acc[4] = jnp.zeros((SPAN, 256), F32)
        lax.fori_loop(0, 4, term, 0)
        for i in range(4):
            there = pl.ds(pl.multiple_of(i * 128 + (1 - place.zh) * 64, 64), 64)
            here = pl.ds(pl.multiple_of(i * 128 + place.zh * 64, 64), 64)
            sbuf[chip, i] = acc[4, there, :].astype(BF16)
            acc[lax.div(chip, 2), pl.ds(pl.multiple_of(lax.rem(chip, 2) * 256 + i * 64, 64), 64), :] = acc[4, here, :]
        z_copy(chip).start()

    def f_copy(chip, d, arriving=False):
        to = ring(place.x, d, 4)
        source = ring(place.x, -d, 4) if arriving else place.x
        return pltpu.make_async_remote_copy(
            src_ref=fbuf.at[chip, to],
            dst_ref=gbuf.at[chip, source],
            send_sem=f_send.at[chip, d - 1],
            recv_sem=f_recv.at[chip, d - 1],
            device_id=place.dev(dx=d),
            device_id_type=MESH,
        )

    def settle(block):
        chip = place.chip(*block)
        z_copy(chip).wait_recv()
        kept = lax.div(chip, 2)
        for i in range(4):
            rows = pl.ds(pl.multiple_of(lax.rem(chip, 2) * 256 + i * 64, 64), 64)
            fbuf[chip, i] = (acc[kept, rows, :] + rbuf[chip, i].astype(F32)).astype(BF16)
        for d in (1, 3, 2):
            f_copy(chip, d).start()

    b0, b_dn, b_up, b_z, b_far, b_zdn, b_zup, b_zfar = og.blocks
    og.arrive(17)
    multiply(b0)
    og.arrive(18)
    multiply(b_dn)
    settle(b0)
    og.arrive(19)
    multiply(b_up)
    settle(b_dn)
    og.arrive(20)
    multiply(b_z)
    settle(b_up)
    og.arrive(22)
    multiply(b_zdn)
    settle(b_z)
    og.arrive(12, 13)
    og.start(21)
    og.arrive(23)
    multiply(b_zup)
    settle(b_zdn)
    og.arrive(14, 15, 16)
    og.start(24)
    og.arrive(21)
    multiply(b_far)
    settle(b_zup)
    og.arrive(24)
    multiply(b_zfar)
    settle(b_far)
    settle(b_zfar)

    def place_rows(chip, carry):
        for d in (1, 3, 2):
            f_copy(chip, d, arriving=True).wait_recv()
        gbuf[chip, place.x] = fbuf[chip, place.x]
        for core in range(2):
            for s in range(4):
                cols = pl.ds(pl.multiple_of(chip * 1024 + core * 512 + s * HEAD, HEAD), HEAD)
                out[:, cols] = gbuf[chip, s, :, core * HEAD : (core + 1) * HEAD]
        return carry

    lax.fori_loop(0, 8, place_rows, 0)

    wg.finish()
    og.finish()
    for d in (1, 3, 2):
        exchange(d).wait_send()

    for i in range(4):
        for kind in (0, 1, 2, 3 if i < 2 else 4):
            x_copy(kind, i).wait_send()
    for n in range(5):
        p_copy(n).wait_send()

    def drain(n, carry):
        for kind in range(4):
            ctx_copy(kind, n).wait_send()
        return carry

    lax.fori_loop(0, 4, drain, 0)

    def drain_out(chip, carry):
        z_copy(chip).wait_send()
        for d in (1, 3, 2):
            f_copy(chip, d).wait_send()
        return carry

    lax.fori_loop(0, 8, drain_out, 0)


TILES = ((0, 128), (0, 256), (0, 384), (128, 384))


def local(activations, query_weight, key_matrix, value_matrix, output_weight, prompt_lengths):
    anywhere = pl.BlockSpec(memory_space=pl.ANY)
    dma = pltpu.SemaphoreType.DMA
    return pl.pallas_call(
        kernel,
        out_shape=jax.ShapeDtypeStruct((64, WIDTH), BF16),
        in_specs=[anywhere] * 5 + [pl.BlockSpec(memory_space=pltpu.SMEM)],
        out_specs=pl.BlockSpec(memory_space=pltpu.VMEM),
        scratch_shapes=[
            pltpu.VMEM((8, SPAN, DEPTH), BF16),
            pltpu.VMEM((8, SPAN, DEPTH), BF16),
            pltpu.VMEM((8, DEPTH, COLS), BF16),
            pltpu.VMEM((8, 2, OROWS, HEAD), BF16),
            pltpu.VMEM((5, SPAN, 256), F32),
            pltpu.VMEM((SPAN, 256), F32),
            pltpu.VMEM((5, SPAN, 256), BF16),
            pltpu.VMEM((5, SPAN, 256), BF16),
            pltpu.VMEM((4, SPAN, QCOLS), BF16),
            pltpu.VMEM((SPAN, HEAD), F32),
            pltpu.VMEM((SPAN, HEAD), F32),
            pltpu.VMEM((4, 128, 384), F32),
            pltpu.VMEM((SPAN, HEAD), BF16),
            pltpu.VMEM((SPAN, HEAD), BF16),
            pltpu.VMEM((8, 4, 64, 256), BF16),
            pltpu.VMEM((8, 4, 64, 256), BF16),
            pltpu.VMEM((8, 4, 64, 256), BF16),
            pltpu.VMEM((8, 4, 64, 256), BF16),
            dma((8,)), dma((8,)), dma((25,)), dma((25,)), dma((5, 4)), dma((5, 4)), dma((5,)), dma((5,)), dma((3,)), dma((3,)),
            dma((4, 4)), dma((4, 4)), dma((8,)), dma((8,)), dma((8, 3)), dma((8, 3)), dma((8,)), dma((4,)),
        ],
        compiler_params=pltpu.CompilerParams(collective_id=0, has_side_effects=True, vmem_limit_bytes=62 << 20),
        cost_estimate=pl.CostEstimate(flops=20 * 10**9, bytes_accessed=12 << 20, transcendentals=1 << 20),
        name="attention_layer",
    )(activations, query_weight, key_matrix, value_matrix, output_weight, prompt_lengths)


def solution(mesh):
    placed = (
        P("group", None),
        P("group", "tp"),
        P("group", "tp"),
        P("group", "tp"),
        P("tp", "group"),
        P("group", None),
    )
    return jax.shard_map(
        local, mesh=mesh, in_specs=placed, out_specs=P(("group", "tp"), None), check_vma=False
    )
```

```python
import math

import jax
import jax.numpy as jnp
from jax import lax
from jax.experimental import pallas as pl
from jax.experimental.pallas import tpu as pltpu
from jax.sharding import PartitionSpec as P

MESH = pl.DeviceIdType.MESH
SPAN = 512
WIDTH = 8192
HEAD = 128
QCOLS = 1024
COLS = 1280
DEPTH = 512
HALF = 4096
OROWS = 4096
DOCS = 8
F32 = jnp.float32
BF16 = jnp.bfloat16


def ring(v, step, size):
    return lax.rem(v + (step + size), size)


class Place:
    def __init__(self):
        g = lax.axis_index("group")
        t = lax.axis_index("tp")
        self.g, self.t = g, t
        self.core = lax.rem(g, 2)
        self.y = lax.rem(lax.div(g, 2), 4)
        self.zl = lax.div(g, 8)
        self.x = lax.div(t, 2)
        self.zh = lax.rem(t, 2)

    def chip(self, dz, dy):
        return ring(self.zl, dz, 2) * 4 + ring(self.y, dy, 4)

    def dev(self, dz=0, dy=0, dc=0, dx=0, dh=0):
        group = self.chip(dz, dy) * 2 + ring(self.core, dc, 2)
        return (group, ring(self.x, dx, 4) * 2 + ring(self.zh, dh, 2))


class Gather:
    def __init__(self, place, view, rows, part, send, recv):
        self.place, self.view, self.send, self.recv = place, view, send, recv
        half = part // 2
        rest = rows - part
        self.a, self.a1, self.a2 = (0, part), (0, half), (half, part - half)
        self.b, self.b1, self.b2 = (part, rest), (part, rest // 2), (part + rest // 2, rest - rest // 2)
        self.all = (0, rows)
        up, down, over, twin = place.dev(dy=1), place.dev(dy=-1), place.dev(dz=1), place.dev(dc=1)
        mine, p_up, p_down, p_far = (0, 0), (0, 1), (0, -1), (0, 2)
        z_mine, z_up, z_down, z_far = (1, 0), (1, 1), (1, -1), (1, 2)
        self.steps = [
            (mine, self.a, up, p_down),
            (mine, self.a, down, p_up),
            (mine, self.b, over, z_mine),
            (mine, self.b, up, p_down),
            (mine, self.b, down, p_up),
            (mine, self.a, over, z_mine),
            (p_down, self.a1, up, p_far),
            (p_up, self.a2, down, p_far),
            (p_down, self.a, over, z_down),
            (p_up, self.a, over, z_up),
            (z_mine, self.b, up, z_down),
            (z_mine, self.b, down, z_up),
            (p_down, self.b1, up, p_far),
            (p_up, self.b2, down, p_far),
            (p_far, self.a, over, z_far),
            (z_down, self.b1, up, z_far),
            (z_up, self.b2, down, z_far),
        ]
        self.blocks = [mine, p_down, p_up, z_mine, p_far, z_down, z_up, z_far]
        for block in self.blocks:
            self.steps.append((block, self.all, twin, block))

    def copy(self, step, arriving=False):
        block, rows, target, lands = self.steps[step]
        core = self.place.core
        if arriving:
            block = lands
            if step >= 17:
                core = 1 - core
        ref = self.view(self.place.chip(*block), core, *rows)
        return pltpu.make_async_remote_copy(
            src_ref=ref,
            dst_ref=ref,
            send_sem=self.send.at[step],
            recv_sem=self.recv.at[step],
            device_id=target,
            device_id_type=MESH,
        )

    def start(self, *steps):
        for step in steps:
            self.copy(step).start()

    def arrive(self, *steps):
        for step in steps:
            self.copy(step, arriving=True).wait_recv()

    def finish(self):
        for step in range(len(self.steps)):
            self.copy(step).wait_send()


class Ring:
    def __init__(self, place, view, rows, send, recv):
        self.place, self.view, self.send, self.recv = place, view, send, recv
        whole, first, second = (0, rows), (0, rows // 2), (rows // 2, rows // 2)
        up, down, twin = place.dev(dy=1), place.dev(dy=-1), place.dev(dc=1)
        self.steps = [
            (0, first, up, -1),
            (0, second, down, 1),
            (0, second, up, -1),
            (0, first, down, 1),
            (-1, first, up, 2),
            (1, second, down, 2),
            (0, whole, twin, 0),
            (-1, whole, twin, -1),
            (1, whole, twin, 1),
            (2, whole, twin, 2),
        ]

    def copy(self, step, arriving=False):
        block, rows, target, lands = self.steps[step]
        core = self.place.core
        if arriving:
            block = lands
            if step >= 6:
                core = 1 - core
        ref = self.view(ring(self.place.y, block, 4), core, *rows)
        return pltpu.make_async_remote_copy(
            src_ref=ref,
            dst_ref=ref,
            send_sem=self.send.at[step],
            recv_sem=self.recv.at[step],
            device_id=target,
            device_id_type=MESH,
        )

    def start(self, *steps):
        for step in steps:
            self.copy(step).start()

    def arrive(self, *steps):
        for step in steps:
            self.copy(step, arriving=True).wait_recv()

    def finish(self):
        for step in range(len(self.steps)):
            self.copy(step).wait_send()


def starts_of(row, lengths):
    start = jnp.zeros_like(row)
    end = 0
    for j in range(DOCS):
        end = end + lengths[j]
        start = start + jnp.where(row >= end, lengths[j], 0)
    return start


def kernel(
    act, wq, wk, wv, wo, lens, out,
    xown, xpar, wbuf, obuf, acc, tmp, psend, precv, ctx, cosb, sinb, bias, rkb, rvb, sbuf, rbuf, fbuf, gbuf,
    w_send, w_recv, o_send, o_recv, x_send, x_recv, p_send, p_recv, e_send, e_recv, c_send, c_recv,
    z_send, z_recv, f_send, f_recv, w_sem,
):
    place = Place()
    mine = pl.ds(pl.multiple_of((place.y * 2 + place.core) * DEPTH, DEPTH), DEPTH)

    own = [
        pltpu.make_async_copy(wq, wbuf.at[mine, pl.ds(0, QCOLS)], w_sem.at[0]),
        pltpu.make_async_copy(wk, wbuf.at[mine, pl.ds(QCOLS, HEAD)], w_sem.at[1]),
        pltpu.make_async_copy(wv, wbuf.at[mine, pl.ds(QCOLS + HEAD, HEAD)], w_sem.at[2]),
    ]
    for copy in own:
        copy.start()
    chip0 = place.chip(0, 0)
    o_cols = pl.ds(pl.multiple_of(place.core * HEAD, HEAD), HEAD)
    own_o = pltpu.make_async_copy(
        wo.at[:, pl.ds(pl.multiple_of(place.x * HEAD, HEAD), HEAD)],
        obuf.at[chip0, pl.ds(pl.multiple_of(place.x * 1024, 1024), 1024), o_cols],
        w_sem.at[3],
    )

    own_x = pltpu.make_async_copy(act.at[:, pl.ds(pl.multiple_of(place.zl * HALF, HALF), HALF)], xown, w_sem.at[4])

    barrier = pltpu.get_barrier_semaphore()
    partners = [
        place.dev(dy=1), place.dev(dy=-1), place.dev(dz=1), place.dev(dc=1),
        place.dev(dx=1), place.dev(dx=2), place.dev(dx=3), place.dev(dh=1),
        place.dev(dz=1, dh=1),
    ]
    for partner in partners:
        pl.semaphore_signal(barrier, inc=1, device_id=partner, device_id_type=MESH)
    pl.semaphore_wait(barrier, len(partners))

    def w_view(y, core, first, count):
        return wbuf.at[pl.ds(pl.multiple_of((y * 2 + core) * DEPTH + first, count), count)]

    def o_view(chip, core, first, count):
        return obuf.at[chip, pl.ds(first, count), pl.ds(pl.multiple_of(core * HEAD, HEAD), HEAD)]

    wg = Ring(place, w_view, DEPTH, w_send, w_recv)
    og = Gather(place, o_view, OROWS, 512, o_send, o_recv)

    x_routes = [(0, dict(dz=1, dh=1), 0), (0, dict(dx=1), -1), (0, dict(dx=-1), 1), (-1, dict(dx=1), 2), (1, dict(dx=-1), 2)]

    def x_copy(kind, i, arriving=False):
        owner, target, lands = x_routes[kind]
        slot = ring(place.x, lands if arriving else owner, 4) * 2 + i // 2
        rows = pl.ds((i % 2) * 256, 256)
        ref = xpar.at[rows, pl.ds(pl.multiple_of(slot * DEPTH, DEPTH), DEPTH)]
        source = ref
        if kind == 0:
            first = (1 - place.zl) * HALF + slot * DEPTH
            source = act.at[rows, pl.ds(pl.multiple_of(first, DEPTH), DEPTH)]
        return pltpu.make_async_remote_copy(
            src_ref=source,
            dst_ref=ref,
            send_sem=x_send.at[kind, i],
            recv_sem=x_recv.at[kind, i],
            device_id=place.dev(**target),
            device_id_type=MESH,
        )

    for i in range(4):
        x_copy(0, i).start()

    def exchange(d, arriving=False):
        to = ring(place.x, d, 4)
        row = ring(place.x, -d, 4) if arriving else place.x
        return pltpu.make_async_remote_copy(
            src_ref=wo.at[:, pl.ds(pl.multiple_of(to * HEAD, HEAD), HEAD)],
            dst_ref=obuf.at[chip0, pl.ds(pl.multiple_of(row * 1024, 1024), 1024), o_cols],
            send_sem=e_send.at[d - 1],
            recv_sem=e_recv.at[d - 1],
            device_id=place.dev(dx=d),
            device_id_type=MESH,
        )

    for d in (1, 3, 2):
        exchange(d).start()
    for copy in own:
        copy.wait()
    wg.start(0, 1, 2, 3, 6)
    own_x.start()
    own_o.start()

    lengths = [lens[0, j] for j in range(DOCS)]
    row = lax.broadcasted_iota(jnp.int32, (SPAN, HEAD), 0)
    lane = lax.broadcasted_iota(jnp.int32, (SPAN, HEAD), 1)
    low = lane < HEAD // 2
    index = jnp.where(low, lane, lane - HEAD // 2).astype(F32)
    freq = jnp.exp(index * (-2.0 * math.log(500000.0) / HEAD))
    angle = (row - starts_of(row, lengths)).astype(F32) * freq
    cosb[...] = jnp.cos(angle)
    sine = jnp.sin(angle)
    sinb[...] = jnp.where(low, -sine, sine)
    for j, (first, count) in enumerate(TILES):
        q = lax.broadcasted_iota(jnp.int32, (128, count), 0) + j * 128
        k = lax.broadcasted_iota(jnp.int32, (128, count), 1) + first
        keep = (k >= starts_of(q, lengths)) & (k <= q)
        bias[j, :, :count] = jnp.where(keep, 0.0, -1e30)

    def x_pass(i):
        x_copy(0, i, arriving=True).wait_recv()
        x_copy(1, i).start()
        x_copy(2, i).start()

    x_pass(0)
    x_pass(1)
    for d in (1, 3, 2):
        exchange(d, arriving=True).wait_recv()
    own_o.wait()
    og.start(2, 5, 17)
    wg.arrive(0)
    wg.start(4)
    wg.arrive(1)
    wg.start(5)
    x_pass(2)
    x_pass(3)
    og.start(0, 1, 3, 4)
    for i in (0, 1):
        x_copy(1, i, arriving=True).wait_recv()
        x_copy(3, i).start()
    wg.arrive(2)
    wg.start(7)
    wg.arrive(3)
    wg.start(8)
    for i in (2, 3):
        x_copy(2, i, arriving=True).wait_recv()
        x_copy(4, i).start()
    og.arrive(2)
    og.start(10, 11)
    wg.arrive(6, 7, 8, 4, 5)
    wg.start(9)
    own_x.wait()
    for i in range(4):
        x_copy(1 if i >= 2 else 2, i, arriving=True).wait_recv()
    for i in (0, 1):
        x_copy(3, i, arriving=True).wait_recv()
        x_copy(4, i + 2, arriving=True).wait_recv()
    wg.arrive(9)

    def p_copy(n):
        return pltpu.make_async_remote_copy(
            src_ref=psend.at[n],
            dst_ref=precv.at[n],
            send_sem=p_send.at[n],
            recv_sem=p_recv.at[n],
            device_id=place.dev(dz=1),
            device_id_type=MESH,
        )

    def their_tile(i, carry):
        n = lax.rem(i + 4, 5)
        cols = pl.ds(pl.multiple_of(n * 256, 256), 256)
        psend[n] = jnp.dot(xpar[...], wbuf[:, cols], preferred_element_type=F32).astype(BF16)
        p_copy(n).start()
        return carry

    def own_tile(i, carry):
        n = lax.rem(i + 4, 5)
        cols = pl.ds(pl.multiple_of(n * 256, 256), 256)
        acc[n] = jnp.dot(xown[...], wbuf[:, cols], preferred_element_type=F32)
        return carry

    lax.fori_loop(0, 5, their_tile, 0)
    lax.fori_loop(0, 5, own_tile, 0)

    def rotate(u):
        return u * cosb[...] + pltpu.roll(u, HEAD // 2, 1) * sinb[...]

    scale = 1.0 / math.sqrt(HEAD)

    def ctx_copy(kind, n, arriving=False):
        dx = 1 if kind in (0, 2) else -1
        if kind < 2:
            owner, rows = 0, pl.ds(0, SPAN)
        else:
            owner, rows = -dx, pl.ds(0 if kind == 2 else 256, 256)
        if arriving:
            owner = owner - dx
        first = ring(place.x, owner % 4, 4) * QCOLS + n * 256
        ref = ctx.at[rows, pl.ds(pl.multiple_of(first, 256), 256)]
        return pltpu.make_async_remote_copy(
            src_ref=ref,
            dst_ref=ref,
            send_sem=c_send.at[kind, n],
            recv_sem=c_recv.at[kind, n],
            device_id=place.dev(dx=dx),
            device_id_type=MESH,
        )

    def two_heads(n):
        p_copy(n).wait_recv()
        pair = acc[n] + precv[n].astype(F32)
        rq = [rotate(pair[:, :HEAD]).astype(BF16), rotate(pair[:, HEAD:]).astype(BF16)]
        cols = pl.ds(pl.multiple_of(place.x * QCOLS + n * 256, 256), 256)
        for j, (first, count) in enumerate(TILES):
            rows = slice(j * 128, (j + 1) * 128)
            q = jnp.concatenate([rq[0][rows], rq[1][rows]], axis=0)
            keys = rkb[first : first + count, :]
            score = lax.dot_general(q, keys, (((1,), (1,)), ((), ())), preferred_element_type=F32)
            mask = bias[j, :, :count]
            score = score * scale + jnp.concatenate([mask, mask], axis=0)
            top = jnp.max(score, axis=-1, keepdims=True)
            weights = jnp.exp(score - top)
            probs = (weights * (1.0 / jnp.sum(weights, axis=-1, keepdims=True))).astype(BF16)
            context = jnp.dot(probs, rvb[first : first + count, :], preferred_element_type=F32)
            context = context.astype(BF16)
            ctx[rows, cols] = jnp.concatenate([context[:128], context[128:]], axis=1)
        ctx_copy(0, n).start()
        ctx_copy(1, n).start()

    def relay(n):
        ctx_copy(0, n, arriving=True).wait_recv()
        ctx_copy(2, n).start()
        ctx_copy(1, n, arriving=True).wait_recv()
        ctx_copy(3, n).start()

    og.arrive(0)
    og.start(6, 8)
    og.arrive(1)
    og.start(7, 9)
    p_copy(4).wait_recv()
    kv = acc[4] + precv[4].astype(F32)
    rkb[...] = rotate(kv[:, :HEAD]).astype(BF16)
    rvb[...] = kv[:, HEAD:].astype(BF16)
    two_heads(0)
    og.arrive(5)
    og.start(20)
    two_heads(1)
    og.arrive(3)
    og.start(12, 18)
    og.arrive(4)
    og.start(13, 19)
    relay(0)
    two_heads(2)
    relay(1)
    two_heads(3)
    relay(2)
    og.arrive(6, 7)
    og.start(14)
    og.arrive(10)
    og.start(15)
    og.arrive(11)
    og.start(16)
    relay(3)
    og.arrive(8)
    og.start(22)
    og.arrive(9)
    og.start(23)

    def far(n, carry):
        ctx_copy(2, n, arriving=True).wait_recv()
        ctx_copy(3, n, arriving=True).wait_recv()
        return carry

    lax.fori_loop(0, 4, far, 0)

    def z_copy(chip):
        return pltpu.make_async_remote_copy(
            src_ref=sbuf.at[chip],
            dst_ref=rbuf.at[chip],
            send_sem=z_send.at[chip],
            recv_sem=z_recv.at[chip],
            device_id=place.dev(dh=1),
            device_id_type=MESH,
        )

    def multiply(block):
        chip = place.chip(*block)

        tmp[...] = jnp.dot(ctx[...], obuf[chip], preferred_element_type=F32)
        for i in range(4):
            there = pl.ds(pl.multiple_of(i * 128 + (1 - place.zh) * 64, 64), 64)
            here = pl.ds(pl.multiple_of(i * 128 + place.zh * 64, 64), 64)
            sbuf[chip, i] = tmp[there, :].astype(BF16)
            acc[lax.div(chip, 2), pl.ds(pl.multiple_of(lax.rem(chip, 2) * 256 + i * 64, 64), 64), :] = tmp[here, :]
        z_copy(chip).start()

    def f_copy(chip, d, arriving=False):
        to = ring(place.x, d, 4)
        source = ring(place.x, -d, 4) if arriving else place.x
        return pltpu.make_async_remote_copy(
            src_ref=fbuf.at[chip, to],
            dst_ref=gbuf.at[chip, source],
            send_sem=f_send.at[chip, d - 1],
            recv_sem=f_recv.at[chip, d - 1],
            device_id=place.dev(dx=d),
            device_id_type=MESH,
        )

    def settle(block):
        chip = place.chip(*block)
        z_copy(chip).wait_recv()
        kept = lax.div(chip, 2)
        for i in range(4):
            rows = pl.ds(pl.multiple_of(lax.rem(chip, 2) * 256 + i * 64, 64), 64)
            fbuf[chip, i] = (acc[kept, rows, :] + rbuf[chip, i].astype(F32)).astype(BF16)
        for d in (1, 3, 2):
            f_copy(chip, d).start()

    def place_rows(block):
        chip = place.chip(*block)
        for d in (1, 3, 2):
            f_copy(chip, d, arriving=True).wait_recv()
        gbuf[chip, place.x] = fbuf[chip, place.x]
        for core in range(2):
            for s in range(4):
                cols = pl.ds(pl.multiple_of(chip * 1024 + core * 512 + s * HEAD, HEAD), HEAD)
                out[:, cols] = gbuf[chip, s, :, core * HEAD : (core + 1) * HEAD]

    b0, b_dn, b_up, b_z, b_far, b_zdn, b_zup, b_zfar = og.blocks
    og.arrive(17)
    multiply(b0)
    og.arrive(18)
    multiply(b_dn)
    settle(b0)
    og.arrive(19)
    multiply(b_up)
    settle(b_dn)
    og.arrive(20)
    multiply(b_z)
    settle(b_up)
    place_rows(b0)
    og.arrive(22)
    multiply(b_zdn)
    settle(b_z)
    place_rows(b_dn)
    og.arrive(12, 13)
    og.start(21)
    og.arrive(23)
    multiply(b_zup)
    settle(b_zdn)
    place_rows(b_up)
    og.arrive(21)
    multiply(b_far)
    settle(b_zup)
    place_rows(b_z)
    og.arrive(14, 15, 16)
    og.start(24)
    place_rows(b_zdn)
    settle(b_far)
    og.arrive(24)
    multiply(b_zfar)
    place_rows(b_zup)
    place_rows(b_far)
    settle(b_zfar)
    place_rows(b_zfar)

    wg.finish()
    og.finish()
    for d in (1, 3, 2):
        exchange(d).wait_send()

    for i in range(4):
        for kind in (0, 1, 2, 3 if i < 2 else 4):
            x_copy(kind, i).wait_send()
    for n in range(5):
        p_copy(n).wait_send()

    def drain(n, carry):
        for kind in range(4):
            ctx_copy(kind, n).wait_send()
        return carry

    lax.fori_loop(0, 4, drain, 0)

    def drain_out(chip, carry):
        z_copy(chip).wait_send()
        for d in (1, 3, 2):
            f_copy(chip, d).wait_send()
        return carry

    lax.fori_loop(0, 8, drain_out, 0)


TILES = ((0, 128), (0, 256), (0, 384), (128, 384))


def local(activations, query_weight, key_matrix, value_matrix, output_weight, prompt_lengths):
    anywhere = pl.BlockSpec(memory_space=pl.ANY)
    dma = pltpu.SemaphoreType.DMA
    return pl.pallas_call(
        kernel,
        out_shape=jax.ShapeDtypeStruct((64, WIDTH), BF16),
        in_specs=[anywhere] * 5 + [pl.BlockSpec(memory_space=pltpu.SMEM)],
        out_specs=pl.BlockSpec(memory_space=pltpu.VMEM),
        scratch_shapes=[
            pltpu.VMEM((SPAN, HALF), BF16),
            pltpu.VMEM((SPAN, HALF), BF16),
            pltpu.VMEM((HALF, COLS), BF16),
            pltpu.VMEM((8, OROWS, 256), BF16),
            pltpu.VMEM((5, SPAN, 256), F32),
            pltpu.VMEM((SPAN, 256), F32),
            pltpu.VMEM((5, SPAN, 256), BF16),
            pltpu.VMEM((5, SPAN, 256), BF16),
            pltpu.VMEM((SPAN, 4 * QCOLS), BF16),
            pltpu.VMEM((SPAN, HEAD), F32),
            pltpu.VMEM((SPAN, HEAD), F32),
            pltpu.VMEM((4, 128, 384), F32),
            pltpu.VMEM((SPAN, HEAD), BF16),
            pltpu.VMEM((SPAN, HEAD), BF16),
            pltpu.VMEM((8, 4, 64, 256), BF16),
            pltpu.VMEM((8, 4, 64, 256), BF16),
            pltpu.VMEM((8, 4, 64, 256), BF16),
            pltpu.VMEM((8, 4, 64, 256), BF16),
            dma((10,)), dma((10,)), dma((25,)), dma((25,)), dma((5, 4)), dma((5, 4)), dma((5,)), dma((5,)), dma((3,)), dma((3,)),
            dma((4, 4)), dma((4, 4)), dma((8,)), dma((8,)), dma((8, 3)), dma((8, 3)), dma((5,)),
        ],
        compiler_params=pltpu.CompilerParams(collective_id=0, has_side_effects=True, vmem_limit_bytes=62 << 20),
        cost_estimate=pl.CostEstimate(flops=20 * 10**9, bytes_accessed=12 << 20, transcendentals=1 << 20),
        name="attention_layer",
    )(activations, query_weight, key_matrix, value_matrix, output_weight, prompt_lengths)


def solution(mesh):
    placed = (
        P("group", None),
        P("group", "tp"),
        P("group", "tp"),
        P("group", "tp"),
        P("tp", "group"),
        P("group", None),
    )
    return jax.shard_map(
        local, mesh=mesh, in_specs=placed, out_specs=P(("group", "tp"), None), check_vma=False
    )
```

```python
import math

import jax
import jax.numpy as jnp
from jax import lax
from jax.experimental import pallas as pl
from jax.experimental.pallas import tpu as pltpu
from jax.sharding import PartitionSpec as P

MESH = pl.DeviceIdType.MESH
SPAN = 512
WIDTH = 8192
HEAD = 128
QCOLS = 1024
COLS = 1280
DEPTH = 512
HALF = 4096
OROWS = 4096
DOCS = 8
F32 = jnp.float32
BF16 = jnp.bfloat16


def ring(v, step, size):
    return lax.rem(v + (step + size), size)


class Place:
    def __init__(self):
        g = lax.axis_index("group")
        t = lax.axis_index("tp")
        self.g, self.t = g, t
        self.core = lax.rem(g, 2)
        self.y = lax.rem(lax.div(g, 2), 4)
        self.zl = lax.div(g, 8)
        self.x = lax.div(t, 2)
        self.zh = lax.rem(t, 2)

    def chip(self, dz, dy):
        return ring(self.zl, dz, 2) * 4 + ring(self.y, dy, 4)

    def dev(self, dz=0, dy=0, dc=0, dx=0, dh=0):
        group = self.chip(dz, dy) * 2 + ring(self.core, dc, 2)
        return (group, ring(self.x, dx, 4) * 2 + ring(self.zh, dh, 2))


class Gather:
    def __init__(self, place, view, rows, part, send, recv):
        self.place, self.view, self.send, self.recv = place, view, send, recv
        half = part // 2
        rest = rows - part
        self.a, self.a1, self.a2 = (0, part), (0, half), (half, part - half)
        self.b, self.b1, self.b2 = (part, rest), (part, rest // 2), (part + rest // 2, rest - rest // 2)
        self.all = (0, rows)
        up, down, over, twin = place.dev(dy=1), place.dev(dy=-1), place.dev(dz=1), place.dev(dc=1)
        mine, p_up, p_down, p_far = (0, 0), (0, 1), (0, -1), (0, 2)
        z_mine, z_up, z_down, z_far = (1, 0), (1, 1), (1, -1), (1, 2)
        self.steps = [
            (mine, self.a, up, p_down),
            (mine, self.a, down, p_up),
            (mine, self.b, over, z_mine),
            (mine, self.b, up, p_down),
            (mine, self.b, down, p_up),
            (mine, self.a, over, z_mine),
            (p_down, self.a1, up, p_far),
            (p_up, self.a2, down, p_far),
            (p_down, self.a, over, z_down),
            (p_up, self.a, over, z_up),
            (z_mine, self.b, up, z_down),
            (z_mine, self.b, down, z_up),
            (p_down, self.b1, up, p_far),
            (p_up, self.b2, down, p_far),
            (p_far, self.a, over, z_far),
            (z_down, self.b1, up, z_far),
            (z_up, self.b2, down, z_far),
        ]
        self.blocks = [mine, p_down, p_up, z_mine, p_far, z_down, z_up, z_far]
        for block in self.blocks:
            self.steps.append((block, self.all, twin, block))

    def copy(self, step, arriving=False):
        block, rows, target, lands = self.steps[step]
        core = self.place.core
        if arriving:
            block = lands
            if step >= 17:
                core = 1 - core
        ref = self.view(self.place.chip(*block), core, *rows)
        return pltpu.make_async_remote_copy(
            src_ref=ref,
            dst_ref=ref,
            send_sem=self.send.at[step],
            recv_sem=self.recv.at[step],
            device_id=target,
            device_id_type=MESH,
        )

    def start(self, *steps):
        for step in steps:
            self.copy(step).start()

    def arrive(self, *steps):
        for step in steps:
            self.copy(step, arriving=True).wait_recv()

    def finish(self):
        for step in range(len(self.steps)):
            self.copy(step).wait_send()


class Ring:
    def __init__(self, place, view, rows, send, recv):
        self.place, self.view, self.send, self.recv = place, view, send, recv
        whole, first, second = (0, rows), (0, rows // 2), (rows // 2, rows // 2)
        up, down, twin = place.dev(dy=1), place.dev(dy=-1), place.dev(dc=1)
        self.steps = [
            (0, first, up, -1),
            (0, second, down, 1),
            (0, second, up, -1),
            (0, first, down, 1),
            (-1, first, up, 2),
            (1, second, down, 2),
            (0, whole, twin, 0),
            (-1, whole, twin, -1),
            (1, whole, twin, 1),
            (2, whole, twin, 2),
        ]

    def copy(self, step, arriving=False):
        block, rows, target, lands = self.steps[step]
        core = self.place.core
        if arriving:
            block = lands
            if step >= 6:
                core = 1 - core
        ref = self.view(ring(self.place.y, block, 4), core, *rows)
        return pltpu.make_async_remote_copy(
            src_ref=ref,
            dst_ref=ref,
            send_sem=self.send.at[step],
            recv_sem=self.recv.at[step],
            device_id=target,
            device_id_type=MESH,
        )

    def start(self, *steps):
        for step in steps:
            self.copy(step).start()

    def arrive(self, *steps):
        for step in steps:
            self.copy(step, arriving=True).wait_recv()

    def finish(self):
        for step in range(len(self.steps)):
            self.copy(step).wait_send()


def starts_of(row, lengths):
    start = jnp.zeros_like(row)
    end = 0
    for j in range(DOCS):
        end = end + lengths[j]
        start = start + jnp.where(row >= end, lengths[j], 0)
    return start


def kernel(
    act, wq, wk, wv, wo, lens, out,
    xown, xpar, wbuf, obuf, acc, tmp, psend, precv, ctx, cosb, sinb, bias, rkb, rvb, sbuf, rbuf, fbuf, gbuf,
    w_send, w_recv, o_send, o_recv, x_send, x_recv, p_send, p_recv, e_send, e_recv, c_send, c_recv,
    z_send, z_recv, f_send, f_recv, w_sem,
):
    place = Place()
    mine = pl.ds(pl.multiple_of((place.y * 2 + place.core) * DEPTH, DEPTH), DEPTH)

    own = [
        pltpu.make_async_copy(wq, wbuf.at[mine, pl.ds(0, QCOLS)], w_sem.at[0]),
        pltpu.make_async_copy(wk, wbuf.at[mine, pl.ds(QCOLS, HEAD)], w_sem.at[1]),
        pltpu.make_async_copy(wv, wbuf.at[mine, pl.ds(QCOLS + HEAD, HEAD)], w_sem.at[2]),
    ]
    for copy in own:
        copy.start()
    chip0 = place.chip(0, 0)
    o_cols = pl.ds(pl.multiple_of(place.core * HEAD, HEAD), HEAD)
    own_o = pltpu.make_async_copy(
        wo.at[:, pl.ds(pl.multiple_of(place.x * HEAD, HEAD), HEAD)],
        obuf.at[chip0, pl.ds(pl.multiple_of(place.x * 1024, 1024), 1024), o_cols],
        w_sem.at[3],
    )

    own_x = pltpu.make_async_copy(act.at[:, pl.ds(pl.multiple_of(place.zl * HALF, HALF), HALF)], xown, w_sem.at[4])

    barrier = pltpu.get_barrier_semaphore()
    partners = [
        place.dev(dy=1), place.dev(dy=-1), place.dev(dz=1), place.dev(dc=1),
        place.dev(dx=1), place.dev(dx=2), place.dev(dx=3), place.dev(dh=1),
        place.dev(dz=1, dh=1),
    ]
    for partner in partners:
        pl.semaphore_signal(barrier, inc=1, device_id=partner, device_id_type=MESH)
    pl.semaphore_wait(barrier, len(partners))

    def w_view(y, core, first, count):
        return wbuf.at[pl.ds(pl.multiple_of((y * 2 + core) * DEPTH + first, count), count)]

    def o_view(chip, core, first, count):
        return obuf.at[chip, pl.ds(first, count), pl.ds(pl.multiple_of(core * HEAD, HEAD), HEAD)]

    wg = Ring(place, w_view, DEPTH, w_send, w_recv)
    og = Gather(place, o_view, OROWS, 1024, o_send, o_recv)

    x_routes = [(0, dict(dz=1, dh=1), 0), (0, dict(dx=1), -1), (0, dict(dx=-1), 1), (-1, dict(dx=1), 2), (1, dict(dx=-1), 2)]

    def x_copy(kind, i, arriving=False):
        owner, target, lands = x_routes[kind]
        slot = ring(place.x, lands if arriving else owner, 4) * 2 + i // 2
        rows = pl.ds((i % 2) * 256, 256)
        ref = xpar.at[rows, pl.ds(pl.multiple_of(slot * DEPTH, DEPTH), DEPTH)]
        source = ref
        if kind == 0:
            first = (1 - place.zl) * HALF + slot * DEPTH
            source = act.at[rows, pl.ds(pl.multiple_of(first, DEPTH), DEPTH)]
        return pltpu.make_async_remote_copy(
            src_ref=source,
            dst_ref=ref,
            send_sem=x_send.at[kind, i],
            recv_sem=x_recv.at[kind, i],
            device_id=place.dev(**target),
            device_id_type=MESH,
        )

    for i in range(4):
        x_copy(0, i).start()

    def exchange(d, arriving=False):
        to = ring(place.x, d, 4)
        row = ring(place.x, -d, 4) if arriving else place.x
        return pltpu.make_async_remote_copy(
            src_ref=wo.at[:, pl.ds(pl.multiple_of(to * HEAD, HEAD), HEAD)],
            dst_ref=obuf.at[chip0, pl.ds(pl.multiple_of(row * 1024, 1024), 1024), o_cols],
            send_sem=e_send.at[d - 1],
            recv_sem=e_recv.at[d - 1],
            device_id=place.dev(dx=d),
            device_id_type=MESH,
        )

    for d in (1, 3, 2):
        exchange(d).start()
    for copy in own:
        copy.wait()
    wg.start(0, 1, 2, 3, 6)
    own_x.start()
    own_o.start()

    lengths = [lens[0, j] for j in range(DOCS)]
    row = lax.broadcasted_iota(jnp.int32, (SPAN, HEAD), 0)
    lane = lax.broadcasted_iota(jnp.int32, (SPAN, HEAD), 1)
    low = lane < HEAD // 2
    index = jnp.where(low, lane, lane - HEAD // 2).astype(F32)
    freq = jnp.exp(index * (-2.0 * math.log(500000.0) / HEAD))
    angle = (row - starts_of(row, lengths)).astype(F32) * freq
    cosb[...] = jnp.cos(angle)
    sine = jnp.sin(angle)
    sinb[...] = jnp.where(low, -sine, sine)
    for j, (first, count) in enumerate(TILES):
        q = lax.broadcasted_iota(jnp.int32, (128, count), 0) + j * 128
        k = lax.broadcasted_iota(jnp.int32, (128, count), 1) + first
        keep = (k >= starts_of(q, lengths)) & (k <= q)
        bias[j, :, :count] = jnp.where(keep, 0.0, -1e30)

    def x_pass(i):
        x_copy(0, i, arriving=True).wait_recv()
        x_copy(1, i).start()
        x_copy(2, i).start()

    x_pass(0)
    x_pass(1)
    for d in (1, 3, 2):
        exchange(d, arriving=True).wait_recv()
    own_o.wait()
    og.start(2, 5, 17)
    wg.arrive(0)
    wg.start(4)
    wg.arrive(1)
    wg.start(5)
    x_pass(2)
    x_pass(3)
    og.start(0, 1, 3, 4)
    for i in (0, 1):
        x_copy(1, i, arriving=True).wait_recv()
        x_copy(3, i).start()
    wg.arrive(2)
    wg.start(7)
    wg.arrive(3)
    wg.start(8)
    for i in (2, 3):
        x_copy(2, i, arriving=True).wait_recv()
        x_copy(4, i).start()
    og.arrive(2)
    og.start(10, 11)
    wg.arrive(6, 7, 8, 4, 5)
    wg.start(9)
    own_x.wait()
    for i in range(4):
        x_copy(1 if i >= 2 else 2, i, arriving=True).wait_recv()
    for i in (0, 1):
        x_copy(3, i, arriving=True).wait_recv()
        x_copy(4, i + 2, arriving=True).wait_recv()
    wg.arrive(9)

    def p_copy(n):
        return pltpu.make_async_remote_copy(
            src_ref=psend.at[n],
            dst_ref=precv.at[n],
            send_sem=p_send.at[n],
            recv_sem=p_recv.at[n],
            device_id=place.dev(dz=1),
            device_id_type=MESH,
        )

    def their_tile(i, carry):
        n = lax.rem(i + 4, 5)
        cols = pl.ds(pl.multiple_of(n * 256, 256), 256)
        psend[n] = jnp.dot(xpar[...], wbuf[:, cols], preferred_element_type=F32).astype(BF16)
        p_copy(n).start()
        return carry

    lax.fori_loop(0, 5, their_tile, 0)

    def rotate(u):
        return u * cosb[...] + pltpu.roll(u, HEAD // 2, 1) * sinb[...]

    scale = 1.0 / math.sqrt(HEAD)

    def ctx_copy(kind, n, arriving=False):
        dx = 1 if kind in (0, 2) else -1
        if kind < 2:
            owner, rows = 0, pl.ds(0, SPAN)
        else:
            owner, rows = -dx, pl.ds(0 if kind == 2 else 256, 256)
        if arriving:
            owner = owner - dx
        first = ring(place.x, owner % 4, 4) * QCOLS + n * 256
        ref = ctx.at[rows, pl.ds(pl.multiple_of(first, 256), 256)]
        return pltpu.make_async_remote_copy(
            src_ref=ref,
            dst_ref=ref,
            send_sem=c_send.at[kind, n],
            recv_sem=c_recv.at[kind, n],
            device_id=place.dev(dx=dx),
            device_id_type=MESH,
        )

    def attend(n):
        rq = [rotate(tmp[:, :HEAD]).astype(BF16), rotate(tmp[:, HEAD:]).astype(BF16)]
        cols = pl.ds(pl.multiple_of(place.x * QCOLS + n * 256, 256), 256)
        for j, (first, count) in enumerate(TILES):
            rows = slice(j * 128, (j + 1) * 128)
            q = jnp.concatenate([rq[0][rows], rq[1][rows]], axis=0)
            keys = rkb[first : first + count, :]
            score = lax.dot_general(q, keys, (((1,), (1,)), ((), ())), preferred_element_type=F32)
            mask = bias[j, :, :count]
            score = score * scale + jnp.concatenate([mask, mask], axis=0)
            top = jnp.max(score, axis=-1, keepdims=True)
            weights = jnp.exp(score - top)
            probs = (weights * (1.0 / jnp.sum(weights, axis=-1, keepdims=True))).astype(BF16)
            context = jnp.dot(probs, rvb[first : first + count, :], preferred_element_type=F32)
            context = context.astype(BF16)
            ctx[rows, cols] = jnp.concatenate([context[:128], context[128:]], axis=1)
        ctx_copy(0, n).start()
        ctx_copy(1, n).start()

    def relay(n):
        ctx_copy(0, n, arriving=True).wait_recv()
        ctx_copy(2, n).start()
        ctx_copy(1, n, arriving=True).wait_recv()
        ctx_copy(3, n).start()

    og.arrive(5)
    og.start(20)
    og.arrive(0)
    og.start(6, 8)
    og.arrive(1)
    og.start(7, 9)

    def own_tile(i, carry):
        n = lax.rem(i + 4, 5)
        cols = pl.ds(pl.multiple_of(n * 256, 256), 256)
        tmp[...] = jnp.dot(xown[...], wbuf[:, cols], preferred_element_type=F32)
        p_copy(n).wait_recv()
        tmp[...] += precv[n].astype(F32)

        @pl.when(i == 0)
        def _():
            rkb[...] = rotate(tmp[:, :HEAD]).astype(BF16)
            rvb[...] = tmp[:, HEAD:].astype(BF16)

        @pl.when(i > 0)
        def _():
            attend(i - 1)

        @pl.when(i > 1)
        def _():
            relay(i - 2)

        @pl.when(i == 3)
        def _():
            og.arrive(3)
            og.start(12, 18)
            og.arrive(4)
            og.start(13, 19)

        return carry

    lax.fori_loop(0, 5, own_tile, 0)
    relay(3)
    og.arrive(10)
    og.start(15)
    og.arrive(11)
    og.start(16)
    og.arrive(8)
    og.start(22)
    og.arrive(9)
    og.start(23)
    og.arrive(6, 7)
    og.start(14)

    def far(n, carry):
        ctx_copy(2, n, arriving=True).wait_recv()
        ctx_copy(3, n, arriving=True).wait_recv()
        return carry

    lax.fori_loop(0, 4, far, 0)

    def z_copy(chip):
        return pltpu.make_async_remote_copy(
            src_ref=sbuf.at[chip],
            dst_ref=rbuf.at[chip],
            send_sem=z_send.at[chip],
            recv_sem=z_recv.at[chip],
            device_id=place.dev(dh=1),
            device_id_type=MESH,
        )

    def multiply(chip):

        tmp[...] = jnp.dot(ctx[...], obuf[chip], preferred_element_type=F32)
        for i in range(4):
            there = pl.ds(pl.multiple_of(i * 128 + (1 - place.zh) * 64, 64), 64)
            here = pl.ds(pl.multiple_of(i * 128 + place.zh * 64, 64), 64)
            sbuf[chip, i] = tmp[there, :].astype(BF16)
            acc[lax.div(chip, 2), pl.ds(pl.multiple_of(lax.rem(chip, 2) * 256 + i * 64, 64), 64), :] = tmp[here, :]
        z_copy(chip).start()

    def f_copy(chip, d, arriving=False):
        to = ring(place.x, d, 4)
        source = ring(place.x, -d, 4) if arriving else place.x
        return pltpu.make_async_remote_copy(
            src_ref=fbuf.at[chip, to],
            dst_ref=gbuf.at[chip, source],
            send_sem=f_send.at[chip, d - 1],
            recv_sem=f_recv.at[chip, d - 1],
            device_id=place.dev(dx=d),
            device_id_type=MESH,
        )

    def settle(chip):
        z_copy(chip).wait_recv()
        kept = lax.div(chip, 2)
        for i in range(4):
            rows = pl.ds(pl.multiple_of(lax.rem(chip, 2) * 256 + i * 64, 64), 64)
            fbuf[chip, i] = (acc[kept, rows, :] + rbuf[chip, i].astype(F32)).astype(BF16)
        for d in (1, 3, 2):
            f_copy(chip, d).start()

    def place_rows(chip):
        for d in (1, 3, 2):
            f_copy(chip, d, arriving=True).wait_recv()
        gbuf[chip, place.x] = fbuf[chip, place.x]
        for core in range(2):
            for s in range(4):
                cols = pl.ds(pl.multiple_of(chip * 1024 + core * 512 + s * HEAD, HEAD), HEAD)
                out[:, cols] = gbuf[chip, s, :, core * HEAD : (core + 1) * HEAD]

    def nth(k):
        last, j = lax.div(k, 6), lax.rem(k, 3)
        dz = (1 - last) * lax.div(k, 3) + last * (k - 6)
        dy = (1 - last) * (3 * j - 5 * lax.div(j, 2)) + last * 2
        return place.chip(dz, dy)

    def column_step(k, carry):
        for at, step in enumerate((17, 18, 19, 20, 22, 23, 21, 24)):

            @pl.when(k == at)
            def _(step=step):
                if step == 21:
                    og.arrive(12, 13)
                    og.start(21)
                if step == 24:
                    og.arrive(14, 15, 16)
                    og.start(24)
                og.arrive(step)

        @pl.when(k < 8)
        def _():
            multiply(nth(k))

        @pl.when((k > 0) & (k < 9))
        def _():
            settle(nth(k - 1))

        @pl.when(k > 2)
        def _():
            place_rows(nth(k - 3))

        return carry

    lax.fori_loop(0, 11, column_step, 0)

    wg.finish()
    og.finish()
    for d in (1, 3, 2):
        exchange(d).wait_send()

    for i in range(4):
        for kind in (0, 1, 2, 3 if i < 2 else 4):
            x_copy(kind, i).wait_send()
    for n in range(5):
        p_copy(n).wait_send()

    def drain(n, carry):
        for kind in range(4):
            ctx_copy(kind, n).wait_send()
        return carry

    lax.fori_loop(0, 4, drain, 0)

    def drain_out(chip, carry):
        z_copy(chip).wait_send()
        for d in (1, 3, 2):
            f_copy(chip, d).wait_send()
        return carry

    lax.fori_loop(0, 8, drain_out, 0)


TILES = ((0, 128), (0, 256), (0, 384), (128, 384))


def local(activations, query_weight, key_matrix, value_matrix, output_weight, prompt_lengths):
    anywhere = pl.BlockSpec(memory_space=pl.ANY)
    dma = pltpu.SemaphoreType.DMA
    return pl.pallas_call(
        kernel,
        out_shape=jax.ShapeDtypeStruct((64, WIDTH), BF16),
        in_specs=[anywhere] * 5 + [pl.BlockSpec(memory_space=pltpu.SMEM)],
        out_specs=pl.BlockSpec(memory_space=pltpu.VMEM),
        scratch_shapes=[
            pltpu.VMEM((SPAN, HALF), BF16),
            pltpu.VMEM((SPAN, HALF), BF16),
            pltpu.VMEM((HALF, COLS), BF16),
            pltpu.VMEM((8, OROWS, 256), BF16),
            pltpu.VMEM((4, SPAN, 256), F32),
            pltpu.VMEM((SPAN, 256), F32),
            pltpu.VMEM((5, SPAN, 256), BF16),
            pltpu.VMEM((5, SPAN, 256), BF16),
            pltpu.VMEM((SPAN, 4 * QCOLS), BF16),
            pltpu.VMEM((SPAN, HEAD), F32),
            pltpu.VMEM((SPAN, HEAD), F32),
            pltpu.VMEM((4, 128, 384), F32),
            pltpu.VMEM((SPAN, HEAD), BF16),
            pltpu.VMEM((SPAN, HEAD), BF16),
            pltpu.VMEM((8, 4, 64, 256), BF16),
            pltpu.VMEM((8, 4, 64, 256), BF16),
            pltpu.VMEM((8, 4, 64, 256), BF16),
            pltpu.VMEM((8, 4, 64, 256), BF16),
            dma((10,)), dma((10,)), dma((25,)), dma((25,)), dma((5, 4)), dma((5, 4)), dma((5,)), dma((5,)), dma((3,)), dma((3,)),
            dma((4, 4)), dma((4, 4)), dma((8,)), dma((8,)), dma((8, 3)), dma((8, 3)), dma((5,)),
        ],
        compiler_params=pltpu.CompilerParams(collective_id=0, has_side_effects=True, vmem_limit_bytes=62 << 20),
        cost_estimate=pl.CostEstimate(flops=20 * 10**9, bytes_accessed=12 << 20, transcendentals=1 << 20),
        name="attention_layer",
    )(activations, query_weight, key_matrix, value_matrix, output_weight, prompt_lengths)


def solution(mesh):
    placed = (
        P("group", None),
        P("group", "tp"),
        P("group", "tp"),
        P("group", "tp"),
        P("tp", "group"),
        P("group", None),
    )
    return jax.shard_map(
        local, mesh=mesh, in_specs=placed, out_specs=P(("group", "tp"), None), check_vma=False
    )
```

```python
import math

import jax
import jax.numpy as jnp
from jax import lax
from jax.experimental import pallas as pl
from jax.experimental.pallas import tpu as pltpu
from jax.sharding import PartitionSpec as P

MESH = pl.DeviceIdType.MESH
SPAN = 512
WIDTH = 8192
HEAD = 128
QCOLS = 1024
COLS = 1280
EARLY = 768
DEPTH = 512
HALF = 4096
PART = 256
OROWS = 4096
DOCS = 8
F32 = jnp.float32
BF16 = jnp.bfloat16


def ring(v, step, size):
    return lax.rem(v + (step + size), size)


class Place:
    def __init__(self):
        g = lax.axis_index("group")
        t = lax.axis_index("tp")
        self.g, self.t = g, t
        self.core = lax.rem(g, 2)
        self.y = lax.rem(lax.div(g, 2), 4)
        self.zl = lax.div(g, 8)
        self.x = lax.div(t, 2)
        self.zh = lax.rem(t, 2)

    def chip(self, dz, dy):
        return ring(self.zl, dz, 2) * 4 + ring(self.y, dy, 4)

    def dev(self, dz=0, dy=0, dc=0, dx=0, dh=0):
        group = self.chip(dz, dy) * 2 + ring(self.core, dc, 2)
        return (group, ring(self.x, dx, 4) * 2 + ring(self.zh, dh, 2))


class Gather:
    def __init__(self, place, view, rows, part, send, recv):
        self.place, self.view, self.send, self.recv = place, view, send, recv
        half = part // 2
        rest = rows - part
        self.a, self.a1, self.a2 = (0, part), (0, half), (half, part - half)
        self.b, self.b1, self.b2 = (part, rest), (part, rest // 2), (part + rest // 2, rest - rest // 2)
        self.all = (0, rows)
        up, down, over, twin = place.dev(dy=1), place.dev(dy=-1), place.dev(dz=1), place.dev(dc=1)
        mine, p_up, p_down, p_far = (0, 0), (0, 1), (0, -1), (0, 2)
        z_mine, z_up, z_down, z_far = (1, 0), (1, 1), (1, -1), (1, 2)
        self.steps = [
            (mine, self.a, up, p_down),
            (mine, self.a, down, p_up),
            (mine, self.b, over, z_mine),
            (mine, self.b, up, p_down),
            (mine, self.b, down, p_up),
            (mine, self.a, over, z_mine),
            (p_down, self.a1, up, p_far),
            (p_up, self.a2, down, p_far),
            (p_down, self.a, over, z_down),
            (p_up, self.a, over, z_up),
            (z_mine, self.b, up, z_down),
            (z_mine, self.b, down, z_up),
            (p_down, self.b1, up, p_far),
            (p_up, self.b2, down, p_far),
            (p_far, self.a, over, z_far),
            (z_down, self.b1, up, z_far),
            (z_up, self.b2, down, z_far),
        ]
        self.blocks = [mine, p_down, p_up, z_mine, p_far, z_down, z_up, z_far]
        for block in self.blocks:
            self.steps.append((block, self.all, twin, block))

    def copy(self, step, arriving=False):
        block, rows, target, lands = self.steps[step]
        core = self.place.core
        if arriving:
            block = lands
            if step >= 17:
                core = 1 - core
        ref = self.view(self.place.chip(*block), core, *rows)
        return pltpu.make_async_remote_copy(
            src_ref=ref,
            dst_ref=ref,
            send_sem=self.send.at[step],
            recv_sem=self.recv.at[step],
            device_id=target,
            device_id_type=MESH,
        )

    def start(self, *steps):
        for step in steps:
            self.copy(step).start()

    def arrive(self, *steps):
        for step in steps:
            self.copy(step, arriving=True).wait_recv()

    def finish(self, *steps):
        for step in steps:
            self.copy(step).wait_send()


class Ring:
    def __init__(self, place, view, rows, send, recv):
        self.place, self.view, self.send, self.recv = place, view, send, recv
        whole, first, second = (0, rows), (0, rows // 2), (rows // 2, rows // 2)
        up, down, twin = place.dev(dy=1), place.dev(dy=-1), place.dev(dc=1)
        self.steps = [
            (0, first, up, -1),
            (0, second, down, 1),
            (0, second, up, -1),
            (0, first, down, 1),
            (-1, first, up, 2),
            (1, second, down, 2),
            (0, whole, twin, 0),
            (-1, whole, twin, -1),
            (1, whole, twin, 1),
            (2, whole, twin, 2),
        ]

    def copy(self, step, arriving=False):
        block, rows, target, lands = self.steps[step]
        core = self.place.core
        if arriving:
            block = lands
            if step >= 6:
                core = 1 - core
        ref = self.view(ring(self.place.y, block, 4), core, *rows)
        return pltpu.make_async_remote_copy(
            src_ref=ref,
            dst_ref=ref,
            send_sem=self.send.at[step],
            recv_sem=self.recv.at[step],
            device_id=target,
            device_id_type=MESH,
        )

    def start(self, *steps):
        for step in steps:
            self.copy(step).start()

    def arrive(self, *steps):
        for step in steps:
            self.copy(step, arriving=True).wait_recv()

    def finish(self):
        for step in range(len(self.steps)):
            self.copy(step).wait_send()


def starts_of(row, lengths):
    start = jnp.zeros_like(row)
    end = 0
    for j in range(DOCS):
        end = end + lengths[j]
        start = start + jnp.where(row >= end, lengths[j], 0)
    return start


def kernel(
    act, wq, wk, wv, wo, lens, out,
    xown, xpar, wbuf, obuf, acc, tmp, psend, precv, ctx, cosb, sinb, bias, rkb, rvb, sbuf, rbuf, fbuf, gbuf,
    w_send, w_recv, o_send, o_recv, x_send, x_recv, p_send, p_recv, e_send, e_recv, c_send, c_recv,
    z_send, z_recv, f_send, f_recv, w_sem,
):
    place = Place()
    mine = pl.ds(pl.multiple_of((place.y * 2 + place.core) * DEPTH, DEPTH), DEPTH)

    own = [
        pltpu.make_async_copy(wq, wbuf.at[mine, pl.ds(256, QCOLS)], w_sem.at[0]),
        pltpu.make_async_copy(wk, wbuf.at[mine, pl.ds(0, HEAD)], w_sem.at[1]),
        pltpu.make_async_copy(wv, wbuf.at[mine, pl.ds(HEAD, HEAD)], w_sem.at[2]),
    ]
    for copy in own:
        copy.start()
    chip0 = place.chip(0, 0)
    o_cols = pl.ds(pl.multiple_of(place.core * HEAD, HEAD), HEAD)
    own_o = pltpu.make_async_copy(
        wo.at[:, pl.ds(pl.multiple_of(place.x * HEAD, HEAD), HEAD)],
        obuf.at[chip0, pl.ds(pl.multiple_of(place.x * 1024, 1024), 1024), o_cols],
        w_sem.at[3],
    )

    own_x = pltpu.make_async_copy(act.at[:, pl.ds(pl.multiple_of(place.zl * HALF, HALF), HALF)], xown, w_sem.at[4])

    barrier = pltpu.get_barrier_semaphore()
    partners = [
        place.dev(dy=1), place.dev(dy=-1), place.dev(dz=1), place.dev(dc=1),
        place.dev(dx=1), place.dev(dx=2), place.dev(dx=3), place.dev(dh=1),
        place.dev(dz=1, dh=1),
    ]
    for partner in partners:
        pl.semaphore_signal(barrier, inc=1, device_id=partner, device_id_type=MESH)
    pl.semaphore_wait(barrier, len(partners))

    def w_view(first_col, cols):
        def view(y, core, first, count):
            rows = pl.ds(pl.multiple_of((y * 2 + core) * DEPTH + first, count), count)
            return wbuf.at[rows, pl.ds(first_col, cols)]

        return view

    def o_view(chip, core, first, count):
        return obuf.at[chip, pl.ds(first, count), pl.ds(pl.multiple_of(core * HEAD, HEAD), HEAD)]

    wg = Ring(place, w_view(0, EARLY), DEPTH, w_send.at[0], w_recv.at[0])
    late = Ring(place, w_view(EARLY, COLS - EARLY), DEPTH, w_send.at[1], w_recv.at[1])
    og = Gather(place, o_view, OROWS, 512, o_send, o_recv)

    x_routes = [(0, dict(dz=1, dh=1), 0), (0, dict(dx=1), -1), (0, dict(dx=-1), 1), (-1, dict(dx=1), 2), (1, dict(dx=-1), 2)]
    x_routes.append((2, dict(dz=1, dh=1), 2))

    def x_copy(kind, i, arriving=False):
        owner, target, lands = x_routes[kind]
        slot = ring(place.x, lands if arriving else owner, 4) * 2 + i // 2
        rows = pl.ds((i % 2) * 256, 256)
        ref = xpar.at[rows, pl.ds(pl.multiple_of(slot * DEPTH, DEPTH), DEPTH)]
        source = ref
        if kind in (0, 5):
            first = (1 - place.zl) * HALF + slot * DEPTH
            source = act.at[rows, pl.ds(pl.multiple_of(first, DEPTH), DEPTH)]
        return pltpu.make_async_remote_copy(
            src_ref=source,
            dst_ref=ref,
            send_sem=x_send.at[kind, i],
            recv_sem=x_recv.at[kind, i],
            device_id=place.dev(**target),
            device_id_type=MESH,
        )

    for i in range(4):
        x_copy(0, i).start()
    for i in (2, 3):
        x_copy(5, i).start()

    def exchange(d, arriving=False):
        to = ring(place.x, d, 4)
        row = ring(place.x, -d, 4) if arriving else place.x
        return pltpu.make_async_remote_copy(
            src_ref=wo.at[:, pl.ds(pl.multiple_of(to * HEAD, HEAD), HEAD)],
            dst_ref=obuf.at[chip0, pl.ds(pl.multiple_of(row * 1024, 1024), 1024), o_cols],
            send_sem=e_send.at[d - 1],
            recv_sem=e_recv.at[d - 1],
            device_id=place.dev(dx=d),
            device_id_type=MESH,
        )

    for d in (1, 3, 2):
        exchange(d).start()
    for copy in own:
        copy.wait()
    wg.start(0, 1, 2, 3, 6)
    own_x.start()
    own_o.start()

    lengths = [lens[0, j] for j in range(DOCS)]
    row = lax.broadcasted_iota(jnp.int32, (SPAN, HEAD), 0)
    lane = lax.broadcasted_iota(jnp.int32, (SPAN, HEAD), 1)
    low = lane < HEAD // 2
    index = jnp.where(low, lane, lane - HEAD // 2).astype(F32)
    freq = jnp.exp(index * (-2.0 * math.log(500000.0) / HEAD))
    angle = (row - starts_of(row, lengths)).astype(F32) * freq
    cosb[...] = jnp.cos(angle)
    sine = jnp.sin(angle)
    sinb[...] = jnp.where(low, -sine, sine)
    for j, (first, count) in enumerate(TILES):
        q = lax.broadcasted_iota(jnp.int32, (128, count), 0) + j * 128
        k = lax.broadcasted_iota(jnp.int32, (128, count), 1) + first
        keep = (k >= starts_of(q, lengths)) & (k <= q)
        bias[j, :, :count] = jnp.where(keep, 0.0, -1e30)

    def x_pass(i):
        x_copy(0, i, arriving=True).wait_recv()
        x_copy(1, i).start()
        x_copy(2, i).start()

    x_pass(0)
    x_pass(1)
    for d in (1, 3, 2):
        exchange(d, arriving=True).wait_recv()
    own_o.wait()
    og.start(2, 5, 17)
    wg.arrive(0)
    wg.start(4)
    wg.arrive(1)
    wg.start(5)
    late.start(0, 1, 2, 3, 6)
    x_pass(2)
    x_pass(3)
    wg.arrive(2)
    wg.start(7)
    wg.arrive(3)
    wg.start(8)
    x_copy(1, 0, arriving=True).wait_recv()
    x_copy(3, 0).start()
    x_copy(2, 1, arriving=True).wait_recv()
    x_copy(4, 1).start()
    late.arrive(0)
    late.start(4)
    late.arrive(1)
    late.start(5)
    og.start(0, 1, 3, 4)
    wg.arrive(4, 5)
    wg.start(9)
    late.arrive(2)
    late.start(7)
    late.arrive(3)
    late.start(8)
    og.arrive(2)
    og.start(10, 11)
    wg.arrive(6, 7, 8, 9)
    own_x.wait()
    for i in range(4):
        if i != 0:
            x_copy(1, i, arriving=True).wait_recv()
        if i != 1:
            x_copy(2, i, arriving=True).wait_recv()
    x_copy(5, 2, arriving=True).wait_recv()
    x_copy(5, 3, arriving=True).wait_recv()
    x_copy(3, 0, arriving=True).wait_recv()
    x_copy(4, 1, arriving=True).wait_recv()

    def p_copy(n, h):
        rows = pl.ds(h * PART, PART)
        return pltpu.make_async_remote_copy(
            src_ref=psend.at[n, rows],
            dst_ref=precv.at[n, rows],
            send_sem=p_send.at[n, h],
            recv_sem=p_recv.at[n, h],
            device_id=place.dev(dz=1),
            device_id_type=MESH,
        )

    def tile_cols(n):
        return pl.ds(pl.multiple_of(n * 256, 256), 256)

    def their_tile(i, carry):
        h, n = lax.div(i, 5), lax.rem(i, 5)
        rows = pl.ds(pl.multiple_of(h * PART, PART), PART)
        psend[n, rows] = jnp.dot(xpar[rows, :], wbuf[:, tile_cols(n)], preferred_element_type=F32).astype(BF16)
        p_copy(n, h).start()
        return carry

    lax.fori_loop(0, 3, their_tile, 0)
    late.arrive(4, 5)
    late.start(9)
    late.arrive(6, 7, 8, 9)
    lax.fori_loop(3, 10, their_tile, 0)

    scale = 1.0 / math.sqrt(HEAD)

    def ctx_copy(kind, n, h, arriving=False):
        dx = 1 if kind in (0, 2) else -1
        if kind < 2:
            owner, rows = 0, pl.ds(h * PART, PART)
        else:
            owner, rows = -dx, pl.ds(h * PART + (0 if kind == 2 else PART // 2), PART // 2)
        if arriving:
            owner = owner - dx
        first = ring(place.x, owner % 4, 4) * QCOLS + n * 256
        ref = ctx.at[rows, pl.ds(pl.multiple_of(first, 256), 256)]
        return pltpu.make_async_remote_copy(
            src_ref=ref,
            dst_ref=ref,
            send_sem=c_send.at[kind, n, h],
            recv_sem=c_recv.at[kind, n, h],
            device_id=place.dev(dx=dx),
            device_id_type=MESH,
        )

    def rotate(u, h):
        rows = slice(h * PART, (h + 1) * PART)
        return (u * cosb[rows, :] + pltpu.roll(u, HEAD // 2, 1) * sinb[rows, :]).astype(BF16)

    def attend(n, h):
        rq = [rotate(tmp[:, :HEAD], h), rotate(tmp[:, HEAD:], h)]
        cols = pl.ds(pl.multiple_of(place.x * QCOLS + n * 256, 256), 256)
        for t in range(2):
            j = 2 * h + t
            first, count = TILES[j]
            rows = slice(t * 128, (t + 1) * 128)
            q = jnp.concatenate([rq[0][rows], rq[1][rows]], axis=0)
            keys = rkb[first : first + count, :]
            score = lax.dot_general(q, keys, (((1,), (1,)), ((), ())), preferred_element_type=F32)
            mask = bias[j, :, :count]
            score = score * scale + jnp.concatenate([mask, mask], axis=0)
            top = jnp.max(score, axis=-1, keepdims=True)
            weights = jnp.exp(score - top)
            probs = (weights * (1.0 / jnp.sum(weights, axis=-1, keepdims=True))).astype(BF16)
            context = jnp.dot(probs, rvb[first : first + count, :], preferred_element_type=F32)
            context = context.astype(BF16)
            ctx[j * 128 : (j + 1) * 128, cols] = jnp.concatenate([context[:128], context[128:]], axis=1)
        ctx_copy(0, n, h).start()
        ctx_copy(1, n, h).start()

    def relay(n, h):
        ctx_copy(0, n, h, arriving=True).wait_recv()
        ctx_copy(2, n, h).start()
        ctx_copy(1, n, h, arriving=True).wait_recv()
        ctx_copy(3, n, h).start()

    def ctx_done(h):
        def far(n, carry):
            ctx_copy(2, n, h, arriving=True).wait_recv()
            ctx_copy(3, n, h, arriving=True).wait_recv()
            return carry

        lax.fori_loop(0, 4, far, 0)

    def z_copy(chip, h):
        two = pl.ds(h * 2, 2)
        return pltpu.make_async_remote_copy(
            src_ref=sbuf.at[chip, two],
            dst_ref=rbuf.at[chip, two],
            send_sem=z_send.at[chip, h],
            recv_sem=z_recv.at[chip, h],
            device_id=place.dev(dh=1),
            device_id_type=MESH,
        )

    def nth(k):
        pair, odd = lax.div(k, 2), lax.rem(k, 2)
        middle = lax.div(pair * (3 - pair), 2)
        dz = middle * (pair - 1) + (1 - middle) * odd
        dy = middle * (3 - 2 * odd) + (1 - middle) * 2 * lax.div(pair, 3)
        return place.chip(dz, dy)

    def kept(chip, i):
        return lax.div(chip, 2), pl.ds(pl.multiple_of(lax.rem(chip, 2) * 256 + i * 64, 64), 64)

    def multiply(k, h):
        chip = nth(k)
        rows = pl.ds(pl.multiple_of(h * PART, PART), PART)
        tmp[...] = jnp.dot(ctx[rows, :], obuf[chip], preferred_element_type=F32)
        for i in range(2):
            there = pl.ds(pl.multiple_of(i * 128 + (1 - place.zh) * 64, 64), 64)
            here = pl.ds(pl.multiple_of(i * 128 + place.zh * 64, 64), 64)
            sbuf[chip, h * 2 + i] = tmp[there, :].astype(BF16)
            pair, spot = kept(chip, h * 2 + i)
            acc[pair, spot, :] = tmp[here, :]
        z_copy(chip, h).start()

    og.arrive(5)
    og.start(20)
    og.arrive(0)
    og.start(6, 8)
    og.arrive(1)
    og.start(7, 9)

    for h in range(2):

        def own_tile(i, carry, h=h):
            n = i
            rows = slice(h * PART, (h + 1) * PART)
            tmp[...] = jnp.dot(xown[rows, :], wbuf[:, tile_cols(n)], preferred_element_type=F32)
            p_copy(n, h).wait_recv()
            tmp[...] += precv[n, rows, :].astype(F32)

            @pl.when(i == 0)
            def _():
                rkb[rows, :] = rotate(tmp[:, :HEAD], h)
                rvb[rows, :] = tmp[:, HEAD:].astype(BF16)

            @pl.when(i > 0)
            def _():
                attend(i - 1, h)

            @pl.when(i > 1)
            def _():
                relay(i - 2, h)

            if h == 1:

                @pl.when(i == 0)
                def _():
                    relay(3, 0)

                @pl.when(i == 3)
                def _():
                    og.arrive(3)
                    og.start(12, 18)
                    og.arrive(4)
                    og.start(13, 19)
                    ctx_done(0)
                    og.arrive(17, 20)

                @pl.when(i > 2)
                def _():
                    multiply(i - 3, 0)

            return carry

        lax.fori_loop(0, 5, own_tile, 0)

    def first_half(k, carry):
        multiply(k, 0)
        return carry

    og.arrive(18, 19)
    lax.fori_loop(2, 4, first_half, 0)
    relay(3, 1)
    ctx_done(1)

    def f_copy(chip, d, arriving=False):
        to = ring(place.x, d, 4)
        source = ring(place.x, -d, 4) if arriving else place.x
        return pltpu.make_async_remote_copy(
            src_ref=fbuf.at[chip, to],
            dst_ref=gbuf.at[chip, source],
            send_sem=f_send.at[chip, d - 1],
            recv_sem=f_recv.at[chip, d - 1],
            device_id=place.dev(dx=d),
            device_id_type=MESH,
        )

    def settle(chip):
        for h in range(2):
            z_copy(chip, h).wait_recv()
            for i in (2 * h, 2 * h + 1):
                pair, spot = kept(chip, i)
                fbuf[chip, i] = (acc[pair, spot, :] + rbuf[chip, i].astype(F32)).astype(BF16)
        for d in (1, 3, 2):
            f_copy(chip, d).start()

    def place_rows(chip):
        for d in (1, 3, 2):
            f_copy(chip, d, arriving=True).wait_recv()
        gbuf[chip, place.x] = fbuf[chip, place.x]
        for core in range(2):
            for s in range(4):
                cols = pl.ds(pl.multiple_of(chip * 1024 + core * 512 + s * HEAD, HEAD), HEAD)
                out[:, cols] = gbuf[chip, s, :, core * HEAD : (core + 1) * HEAD]

    def drain():
        wg.finish()
        late.finish()
        for d in (1, 3, 2):
            exchange(d).wait_send()
        for kind, pieces in enumerate(((0, 1, 2, 3), (0, 1, 2, 3), (0, 1, 2, 3), (0,), (1,), (2, 3))):
            for i in pieces:
                x_copy(kind, i).wait_send()
        for h in range(2):
            for n in range(5):
                p_copy(n, h).wait_send()
            for n in range(4):
                for kind in range(4):
                    ctx_copy(kind, n, h).wait_send()

    def column_step(k, carry):
        @pl.when(k == 4)
        def _():
            og.arrive(10)
            og.start(15)
            og.arrive(11)
            og.start(16)
            og.arrive(8)
            og.start(22)
            og.arrive(9)
            og.start(23)
            og.arrive(22)

        @pl.when(k == 5)
        def _():
            og.arrive(6, 7)
            og.start(14)
            og.arrive(23)

        @pl.when(k == 6)
        def _():
            drain()
            og.arrive(12, 13)
            og.start(21)
            og.arrive(21)

        @pl.when(k == 7)
        def _():
            og.finish(*range(14), 17, 18, 19, 20, 22, 23)
            og.arrive(14, 15, 16)
            og.start(24)
            og.arrive(24)

        @pl.when(k < 8)
        def _():
            def half(h, inner):
                multiply(k, h)
                return inner

            lax.fori_loop(1 - lax.div(k, 4), 2, half, 0)

        @pl.when((k > 1) & (k < 10))
        def _():
            settle(nth(k - 2))

        @pl.when(k > 3)
        def _():
            place_rows(nth(k - 4))

        return carry

    lax.fori_loop(0, 12, column_step, 0)

    og.finish(14, 15, 16, 21, 24)

    def drain_out(chip, carry):
        for h in range(2):
            z_copy(chip, h).wait_send()
        for d in (1, 3, 2):
            f_copy(chip, d).wait_send()
        return carry

    lax.fori_loop(0, 8, drain_out, 0)


TILES = ((0, 128), (0, 256), (0, 384), (128, 384))


def local(activations, query_weight, key_matrix, value_matrix, output_weight, prompt_lengths):
    anywhere = pl.BlockSpec(memory_space=pl.ANY)
    dma = pltpu.SemaphoreType.DMA
    return pl.pallas_call(
        kernel,
        out_shape=jax.ShapeDtypeStruct((64, WIDTH), BF16),
        in_specs=[anywhere] * 5 + [pl.BlockSpec(memory_space=pltpu.SMEM)],
        out_specs=pl.BlockSpec(memory_space=pltpu.VMEM),
        scratch_shapes=[
            pltpu.VMEM((SPAN, HALF), BF16),
            pltpu.VMEM((SPAN, HALF), BF16),
            pltpu.VMEM((HALF, COLS), BF16),
            pltpu.VMEM((8, OROWS, 256), BF16),
            pltpu.VMEM((4, SPAN, 256), F32),
            pltpu.VMEM((PART, 256), F32),
            pltpu.VMEM((5, SPAN, 256), BF16),
            pltpu.VMEM((5, SPAN, 256), BF16),
            pltpu.VMEM((SPAN, 4 * QCOLS), BF16),
            pltpu.VMEM((SPAN, HEAD), F32),
            pltpu.VMEM((SPAN, HEAD), F32),
            pltpu.VMEM((4, 128, 384), F32),
            pltpu.VMEM((SPAN, HEAD), BF16),
            pltpu.VMEM((SPAN, HEAD), BF16),
            pltpu.VMEM((8, 4, 64, 256), BF16),
            pltpu.VMEM((8, 4, 64, 256), BF16),
            pltpu.VMEM((8, 4, 64, 256), BF16),
            pltpu.VMEM((8, 4, 64, 256), BF16),
            dma((2, 10)), dma((2, 10)), dma((25,)), dma((25,)), dma((6, 4)), dma((6, 4)), dma((5, 2)), dma((5, 2)), dma((3,)), dma((3,)),
            dma((4, 4, 2)), dma((4, 4, 2)), dma((8, 2)), dma((8, 2)), dma((8, 3)), dma((8, 3)), dma((5,)),
        ],
        compiler_params=pltpu.CompilerParams(collective_id=0, has_side_effects=True, vmem_limit_bytes=62 << 20),
        cost_estimate=pl.CostEstimate(flops=20 * 10**9, bytes_accessed=12 << 20, transcendentals=1 << 20),
        name="attention_layer",
    )(activations, query_weight, key_matrix, value_matrix, output_weight, prompt_lengths)


def solution(mesh):
    placed = (
        P("group", None),
        P("group", "tp"),
        P("group", "tp"),
        P("group", "tp"),
        P("tp", "group"),
        P("group", None),
    )
    return jax.shard_map(
        local, mesh=mesh, in_specs=placed, out_specs=P(("group", "tp"), None), check_vma=False
    )
```

```python
import math

import jax
import jax.numpy as jnp
from jax import lax
from jax.experimental import pallas as pl
from jax.experimental.pallas import tpu as pltpu
from jax.sharding import PartitionSpec as P

MESH = pl.DeviceIdType.MESH
SPAN = 512
WIDTH = 8192
HEAD = 128
QCOLS = 1024
COLS = 1280
EARLY = 768
DEPTH = 512
HALF = 4096
PART = 256
OROWS = 4096
DOCS = 8
F32 = jnp.float32
BF16 = jnp.bfloat16


def ring(v, step, size):
    return lax.rem(v + (step + size), size)


class Place:
    def __init__(self):
        g = lax.axis_index("group")
        t = lax.axis_index("tp")
        self.g, self.t = g, t
        self.core = lax.rem(g, 2)
        self.y = lax.rem(lax.div(g, 2), 4)
        self.zl = lax.div(g, 8)
        self.x = lax.div(t, 2)
        self.zh = lax.rem(t, 2)

    def chip(self, dz, dy):
        return ring(self.zl, dz, 2) * 4 + ring(self.y, dy, 4)

    def dev(self, dz=0, dy=0, dc=0, dx=0, dh=0):
        group = self.chip(dz, dy) * 2 + ring(self.core, dc, 2)
        return (group, ring(self.x, dx, 4) * 2 + ring(self.zh, dh, 2))


class Gather:
    def __init__(self, place, view, rows, part, send, recv):
        self.place, self.view, self.send, self.recv = place, view, send, recv
        half = part // 2
        rest = rows - part
        self.a, self.a1, self.a2 = (0, part), (0, half), (half, part - half)
        self.b, self.b1, self.b2 = (part, rest), (part, rest // 2), (part + rest // 2, rest - rest // 2)
        self.all = (0, rows)
        b1, b2 = ([(at + i * (count // 2), count // 2) for i in range(2)] for at, count in (self.b1, self.b2))
        up, down, over, twin = place.dev(dy=1), place.dev(dy=-1), place.dev(dz=1), place.dev(dc=1)
        mine, p_up, p_down, p_far = (0, 0), (0, 1), (0, -1), (0, 2)
        z_mine, z_up, z_down, z_far = (1, 0), (1, 1), (1, -1), (1, 2)
        self.steps = [
            (mine, self.a, up, p_down),
            (mine, self.a, down, p_up),
            (mine, self.b, over, z_mine),
            (mine, self.b, up, p_down),
            (mine, self.b, down, p_up),
            (mine, self.a, over, z_mine),
            (p_down, self.a1, up, p_far),
            (p_up, self.a2, down, p_far),
            (p_down, self.a, over, z_down),
            (p_up, self.a, over, z_up),
            (z_mine, self.b, up, z_down),
            (z_mine, self.b, down, z_up),
            (p_down, self.b1, up, p_far),
            (p_up, self.b2, down, p_far),
            (p_far, self.a, over, z_far),
            (z_down, b1[0], up, z_far),
            (z_up, b2[0], down, z_far),
        ]
        self.blocks = [mine, p_down, p_up, z_mine, p_far, z_down, z_up, z_far]
        for block in self.blocks:
            self.steps.append((block, self.a if block == z_far else self.all, twin, block))
        self.steps += [(z_down, b1[1], up, z_far), (z_up, b2[1], down, z_far)]
        self.steps += [(z_far, piece, twin, z_far) for piece in (b1[0], b2[0], b1[1], b2[1])]

    def copy(self, step, arriving=False):
        block, rows, target, lands = self.steps[step]
        core = self.place.core
        if arriving:
            block = lands
            if step in range(17, 25) or step >= 27:
                core = 1 - core
        ref = self.view(self.place.chip(*block), core, *rows)
        return pltpu.make_async_remote_copy(
            src_ref=ref,
            dst_ref=ref,
            send_sem=self.send.at[step],
            recv_sem=self.recv.at[step],
            device_id=target,
            device_id_type=MESH,
        )

    def start(self, *steps):
        for step in steps:
            self.copy(step).start()

    def arrive(self, *steps):
        for step in steps:
            self.copy(step, arriving=True).wait_recv()

    def finish(self, *steps):
        for step in steps:
            self.copy(step).wait_send()


class Ring:
    def __init__(self, place, view, rows, send, recv):
        self.place, self.view, self.send, self.recv = place, view, send, recv
        whole, first, second = (0, rows), (0, rows // 2), (rows // 2, rows // 2)
        up, down, twin = place.dev(dy=1), place.dev(dy=-1), place.dev(dc=1)
        self.steps = [
            (0, first, up, -1),
            (0, second, down, 1),
            (0, second, up, -1),
            (0, first, down, 1),
            (-1, first, up, 2),
            (1, second, down, 2),
            (0, whole, twin, 0),
            (-1, whole, twin, -1),
            (1, whole, twin, 1),
            (2, whole, twin, 2),
        ]

    def copy(self, step, arriving=False):
        block, rows, target, lands = self.steps[step]
        core = self.place.core
        if arriving:
            block = lands
            if step >= 6:
                core = 1 - core
        ref = self.view(ring(self.place.y, block, 4), core, *rows)
        return pltpu.make_async_remote_copy(
            src_ref=ref,
            dst_ref=ref,
            send_sem=self.send.at[step],
            recv_sem=self.recv.at[step],
            device_id=target,
            device_id_type=MESH,
        )

    def start(self, *steps):
        for step in steps:
            self.copy(step).start()

    def arrive(self, *steps):
        for step in steps:
            self.copy(step, arriving=True).wait_recv()

    def finish(self):
        for step in range(len(self.steps)):
            self.copy(step).wait_send()


def starts_of(row, lengths):
    start = jnp.zeros_like(row)
    end = 0
    for j in range(DOCS):
        end = end + lengths[j]
        start = start + jnp.where(row >= end, lengths[j], 0)
    return start


def kernel(
    act, wq, wk, wv, wo, lens, out,
    xown, xpar, wbuf, obuf, acc, tmp, psend, precv, ctx, cosb, sinb, bias, rkb, rvb, sbuf, rbuf, fbuf, gbuf,
    w_send, w_recv, o_send, o_recv, x_send, x_recv, p_send, p_recv, e_send, e_recv, c_send, c_recv,
    z_send, z_recv, f_send, f_recv, w_sem, out_sem,
):
    place = Place()
    mine = pl.ds(pl.multiple_of((place.y * 2 + place.core) * DEPTH, DEPTH), DEPTH)

    own = [
        pltpu.make_async_copy(wq, wbuf.at[mine, pl.ds(256, QCOLS)], w_sem.at[0]),
        pltpu.make_async_copy(wk, wbuf.at[mine, pl.ds(0, HEAD)], w_sem.at[1]),
        pltpu.make_async_copy(wv, wbuf.at[mine, pl.ds(HEAD, HEAD)], w_sem.at[2]),
    ]
    for copy in own:
        copy.start()
    chip0 = place.chip(0, 0)
    o_cols = pl.ds(pl.multiple_of(place.core * HEAD, HEAD), HEAD)
    own_o = pltpu.make_async_copy(
        wo.at[:, pl.ds(pl.multiple_of(place.x * HEAD, HEAD), HEAD)],
        obuf.at[chip0, pl.ds(pl.multiple_of(place.x * 1024, 1024), 1024), o_cols],
        w_sem.at[3],
    )

    own_x = pltpu.make_async_copy(act.at[:, pl.ds(pl.multiple_of(place.zl * HALF, HALF), HALF)], xown, w_sem.at[4])

    barrier = pltpu.get_barrier_semaphore()
    partners = [
        place.dev(dy=1), place.dev(dy=-1), place.dev(dz=1), place.dev(dc=1),
        place.dev(dx=1), place.dev(dx=2), place.dev(dx=3), place.dev(dh=1),
        place.dev(dz=1, dh=1),
    ]
    for partner in partners:
        pl.semaphore_signal(barrier, inc=1, device_id=partner, device_id_type=MESH)
    pl.semaphore_wait(barrier, len(partners))

    def w_view(first_col, cols):
        def view(y, core, first, count):
            rows = pl.ds(pl.multiple_of((y * 2 + core) * DEPTH + first, count), count)
            return wbuf.at[rows, pl.ds(first_col, cols)]

        return view

    def o_view(chip, core, first, count):
        return obuf.at[chip, pl.ds(first, count), pl.ds(pl.multiple_of(core * HEAD, HEAD), HEAD)]

    wg = Ring(place, w_view(0, EARLY), DEPTH, w_send.at[0], w_recv.at[0])
    late = Ring(place, w_view(EARLY, COLS - EARLY), DEPTH, w_send.at[1], w_recv.at[1])
    og = Gather(place, o_view, OROWS, 512, o_send, o_recv)

    for copy in own:
        copy.wait()
    wg.start(0, 1, 2, 3, 6)

    x_routes = [(0, dict(dz=1, dh=1), 0), (0, dict(dx=1), -1), (0, dict(dx=-1), 1), (-1, dict(dx=1), 2), (1, dict(dx=-1), 2)]
    x_routes.append((2, dict(dz=1, dh=1), 2))

    def x_copy(kind, i, arriving=False):
        owner, target, lands = x_routes[kind]
        slot = ring(place.x, lands if arriving else owner, 4) * 2 + i // 2
        rows = pl.ds((i % 2) * 256, 256)
        ref = xpar.at[rows, pl.ds(pl.multiple_of(slot * DEPTH, DEPTH), DEPTH)]
        source = ref
        if kind in (0, 5):
            first = (1 - place.zl) * HALF + slot * DEPTH
            source = act.at[rows, pl.ds(pl.multiple_of(first, DEPTH), DEPTH)]
        return pltpu.make_async_remote_copy(
            src_ref=source,
            dst_ref=ref,
            send_sem=x_send.at[kind, i],
            recv_sem=x_recv.at[kind, i],
            device_id=place.dev(**target),
            device_id_type=MESH,
        )

    for i in range(4):
        x_copy(0, i).start()
    for i in (2, 3):
        x_copy(5, i).start()

    def exchange(d, arriving=False):
        to = ring(place.x, d, 4)
        row = ring(place.x, -d, 4) if arriving else place.x
        return pltpu.make_async_remote_copy(
            src_ref=wo.at[:, pl.ds(pl.multiple_of(to * HEAD, HEAD), HEAD)],
            dst_ref=obuf.at[chip0, pl.ds(pl.multiple_of(row * 1024, 1024), 1024), o_cols],
            send_sem=e_send.at[d - 1],
            recv_sem=e_recv.at[d - 1],
            device_id=place.dev(dx=d),
            device_id_type=MESH,
        )

    for d in (1, 3, 2):
        exchange(d).start()
    own_x.start()
    own_o.start()

    lengths = [lens[0, j] for j in range(DOCS)]
    row = lax.broadcasted_iota(jnp.int32, (SPAN, HEAD), 0)
    lane = lax.broadcasted_iota(jnp.int32, (SPAN, HEAD), 1)
    low = lane < HEAD // 2
    index = jnp.where(low, lane, lane - HEAD // 2).astype(F32)
    freq = jnp.exp(index * (-2.0 * math.log(500000.0) / HEAD))
    angle = (row - starts_of(row, lengths)).astype(F32) * freq
    cosb[...] = jnp.cos(angle)
    sine = jnp.sin(angle)
    sinb[...] = jnp.where(low, -sine, sine)
    for j, (first, count) in enumerate(TILES):
        q = lax.broadcasted_iota(jnp.int32, (128, count), 0) + j * 128
        k = lax.broadcasted_iota(jnp.int32, (128, count), 1) + first
        keep = (k >= starts_of(q, lengths)) & (k <= q)
        bias[j, :, :count] = jnp.where(keep, 0.0, -1e30)

    def x_pass(i):
        x_copy(0, i, arriving=True).wait_recv()
        x_copy(1, i).start()
        x_copy(2, i).start()

    x_pass(0)
    x_pass(1)
    for d in (1, 3, 2):
        exchange(d, arriving=True).wait_recv()
    own_o.wait()
    og.start(2, 5, 17)
    wg.arrive(0)
    wg.start(4)
    wg.arrive(1)
    wg.start(5)
    late.start(0, 1, 2, 3, 6)
    x_pass(2)
    x_pass(3)
    wg.arrive(2)
    wg.start(7)
    wg.arrive(3)
    wg.start(8)
    x_copy(1, 0, arriving=True).wait_recv()
    x_copy(3, 0).start()
    x_copy(2, 1, arriving=True).wait_recv()
    x_copy(4, 1).start()
    late.arrive(0)
    late.start(4)
    late.arrive(1)
    late.start(5)
    og.start(0, 1, 3, 4)
    wg.arrive(4, 5)
    wg.start(9)
    late.arrive(2)
    late.start(7)
    late.arrive(3)
    late.start(8)
    wg.arrive(6, 7, 8, 9)
    own_x.wait()
    for i in range(4):
        if i != 0:
            x_copy(1, i, arriving=True).wait_recv()
        if i != 1:
            x_copy(2, i, arriving=True).wait_recv()
    x_copy(5, 2, arriving=True).wait_recv()
    x_copy(5, 3, arriving=True).wait_recv()
    x_copy(3, 0, arriving=True).wait_recv()
    x_copy(4, 1, arriving=True).wait_recv()

    def p_copy(n, h):
        rows = pl.ds(h * PART, PART)
        return pltpu.make_async_remote_copy(
            src_ref=psend.at[n, rows],
            dst_ref=precv.at[n, rows],
            send_sem=p_send.at[n, h],
            recv_sem=p_recv.at[n, h],
            device_id=place.dev(dz=1),
            device_id_type=MESH,
        )

    def tile_cols(n):
        return pl.ds(pl.multiple_of(n * 256, 256), 256)

    def their_tile(i, carry):
        h, n = lax.div(i, 5), lax.rem(i, 5)
        rows = pl.ds(pl.multiple_of(h * PART, PART), PART)
        psend[n, rows] = jnp.dot(xpar[rows, :], wbuf[:, tile_cols(n)], preferred_element_type=F32).astype(BF16)
        p_copy(n, h).start()
        return carry

    lax.fori_loop(0, 3, their_tile, 0)
    late.arrive(4, 5)
    late.start(9)
    late.arrive(6, 7, 8, 9)
    lax.fori_loop(3, 10, their_tile, 0)

    scale = 1.0 / math.sqrt(HEAD)

    def ctx_copy(kind, n, h, arriving=False):
        dx = 1 if kind in (0, 2) else -1
        if kind < 2:
            owner, rows = 0, pl.ds(h * PART, PART)
        else:
            owner, rows = -dx, pl.ds(h * PART + (0 if kind == 2 else PART // 2), PART // 2)
        if arriving:
            owner = owner - dx
        first = ring(place.x, owner % 4, 4) * QCOLS + n * 256
        ref = ctx.at[rows, pl.ds(pl.multiple_of(first, 256), 256)]
        return pltpu.make_async_remote_copy(
            src_ref=ref,
            dst_ref=ref,
            send_sem=c_send.at[kind, n, h],
            recv_sem=c_recv.at[kind, n, h],
            device_id=place.dev(dx=dx),
            device_id_type=MESH,
        )

    def rotate(u, h):
        rows = slice(h * PART, (h + 1) * PART)
        return (u * cosb[rows, :] + pltpu.roll(u, HEAD // 2, 1) * sinb[rows, :]).astype(BF16)

    def attend(n, h):
        rq = [rotate(tmp[:, :HEAD], h), rotate(tmp[:, HEAD:], h)]
        cols = pl.ds(pl.multiple_of(place.x * QCOLS + n * 256, 256), 256)
        for t in range(2):
            j = 2 * h + t
            first, count = TILES[j]
            rows = slice(t * 128, (t + 1) * 128)
            q = jnp.concatenate([rq[0][rows], rq[1][rows]], axis=0)
            keys = rkb[first : first + count, :]
            score = lax.dot_general(q, keys, (((1,), (1,)), ((), ())), preferred_element_type=F32)
            mask = bias[j, :, :count]
            score = score * scale + jnp.concatenate([mask, mask], axis=0)
            top = jnp.max(score, axis=-1, keepdims=True)
            weights = jnp.exp(score - top)
            probs = (weights * (1.0 / jnp.sum(weights, axis=-1, keepdims=True))).astype(BF16)
            context = jnp.dot(probs, rvb[first : first + count, :], preferred_element_type=F32)
            context = context.astype(BF16)
            ctx[j * 128 : (j + 1) * 128, cols] = jnp.concatenate([context[:128], context[128:]], axis=1)
        ctx_copy(0, n, h).start()
        ctx_copy(1, n, h).start()

    def relay(n, h):
        ctx_copy(0, n, h, arriving=True).wait_recv()
        ctx_copy(2, n, h).start()
        ctx_copy(1, n, h, arriving=True).wait_recv()
        ctx_copy(3, n, h).start()

    def ctx_done(h):
        def far(n, carry):
            ctx_copy(2, n, h, arriving=True).wait_recv()
            ctx_copy(3, n, h, arriving=True).wait_recv()
            return carry

        lax.fori_loop(0, 4, far, 0)

    def z_copy(chip, h):
        two = pl.ds(h * 2, 2)
        return pltpu.make_async_remote_copy(
            src_ref=sbuf.at[chip, two],
            dst_ref=rbuf.at[chip, two],
            send_sem=z_send.at[chip, h],
            recv_sem=z_recv.at[chip, h],
            device_id=place.dev(dh=1),
            device_id_type=MESH,
        )

    def nth(k):
        pair, odd = lax.div(k, 2), lax.rem(k, 2)
        middle = lax.div(pair * (3 - pair), 2)
        dz = middle * (pair - 1) + (1 - middle) * odd
        dy = middle * (3 - 2 * odd) + (1 - middle) * 2 * lax.div(pair, 3)
        return place.chip(dz, dy)

    def kept(chip, i):
        return lax.div(chip, 2), pl.ds(pl.multiple_of(lax.rem(chip, 2) * 256 + i * 64, 64), 64)

    def multiply(k, h):
        chip = nth(k)
        rows = pl.ds(pl.multiple_of(h * PART, PART), PART)
        tmp[...] = jnp.dot(ctx[rows, :], obuf[chip], preferred_element_type=F32)
        for i in range(2):
            there = pl.ds(pl.multiple_of(i * 128 + (1 - place.zh) * 64, 64), 64)
            here = pl.ds(pl.multiple_of(i * 128 + place.zh * 64, 64), 64)
            sbuf[chip, h * 2 + i] = tmp[there, :].astype(BF16)
            pair, spot = kept(chip, h * 2 + i)
            acc[pair, spot, :] = tmp[here, :]
        z_copy(chip, h).start()

    og.arrive(2, 5)
    og.start(20)
    og.arrive(0)
    og.start(6, 8)
    og.arrive(1)
    og.start(7, 9)
    og.start(10, 11)

    for h in range(2):

        def own_tile(i, carry, h=h):
            n = i
            rows = slice(h * PART, (h + 1) * PART)
            tmp[...] = jnp.dot(xown[rows, :], wbuf[:, tile_cols(n)], preferred_element_type=F32)
            p_copy(n, h).wait_recv()
            tmp[...] += precv[n, rows, :].astype(F32)

            @pl.when(i == 0)
            def _():
                rkb[rows, :] = rotate(tmp[:, :HEAD], h)
                rvb[rows, :] = tmp[:, HEAD:].astype(BF16)

            @pl.when(i > 0)
            def _():
                attend(i - 1, h)

            @pl.when(i > 1)
            def _():
                relay(i - 2, h)

            if h == 1:

                @pl.when(i == 0)
                def _():
                    relay(3, 0)

                @pl.when(i == 3)
                def _():
                    og.arrive(3)
                    og.start(12, 18)
                    og.arrive(4)
                    og.start(13, 19)
                    ctx_done(0)
                    og.arrive(17, 20)

                @pl.when(i > 2)
                def _():
                    multiply(i - 3, 0)

            return carry

        lax.fori_loop(0, 5, own_tile, 0)

    og.arrive(6, 7)
    og.start(14)

    def first_half(k, carry):
        multiply(k, 0)
        return carry

    og.arrive(18, 19)
    lax.fori_loop(2, 4, first_half, 0)
    relay(3, 1)
    ctx_done(1)

    def f_copy(chip, d, arriving=False):
        to = ring(place.x, d, 4)
        source = ring(place.x, -d, 4) if arriving else place.x
        return pltpu.make_async_remote_copy(
            src_ref=fbuf.at[chip, to],
            dst_ref=gbuf.at[chip, :, :, pl.ds(pl.multiple_of(source * HEAD, HEAD), HEAD)],
            send_sem=f_send.at[chip, d - 1],
            recv_sem=f_recv.at[chip, d - 1],
            device_id=place.dev(dx=d),
            device_id_type=MESH,
        )

    def settle(chip):
        for h in range(2):
            z_copy(chip, h).wait_recv()
            for i in (2 * h, 2 * h + 1):
                pair, spot = kept(chip, i)
                total = (acc[pair, spot, :] + rbuf[chip, i].astype(F32)).astype(BF16)
                fbuf[chip, i, 0] = total[:, :HEAD]
                fbuf[chip, i, 1] = total[:, HEAD:]
        for d in (1, 3, 2):
            f_copy(chip, d).start()

    def out_copy(chip, core):
        cols = pl.ds(pl.multiple_of(chip * 1024 + core * 512, 512), 512)
        return pltpu.make_async_copy(gbuf.at[chip, core], out.at[:, cols], out_sem.at[chip, core])

    def place_rows(chip):
        for d in (1, 3, 2):
            f_copy(chip, d, arriving=True).wait_recv()
        here = pl.ds(pl.multiple_of(place.x * HEAD, HEAD), HEAD)
        for core in range(2):
            gbuf[chip, core, :, here] = fbuf[chip, place.x, core]
            out_copy(chip, core).start()

    def drain():
        wg.finish()
        late.finish()
        for d in (1, 3, 2):
            exchange(d).wait_send()
        for kind, pieces in enumerate(((0, 1, 2, 3), (0, 1, 2, 3), (0, 1, 2, 3), (0,), (1,), (2, 3))):
            for i in pieces:
                x_copy(kind, i).wait_send()
        for h in range(2):
            for n in range(5):
                p_copy(n, h).wait_send()
            for n in range(4):
                for kind in range(4):
                    ctx_copy(kind, n, h).wait_send()

    def column_step(k, carry):
        @pl.when(k == 4)
        def _():
            og.arrive(10)
            og.start(15, 25)
            og.arrive(11)
            og.start(16, 26)
            og.arrive(8)
            og.start(22)
            og.arrive(9)
            og.start(23)
            og.arrive(22)

        @pl.when(k == 5)
        def _():
            og.arrive(23)

        @pl.when(k == 6)
        def _():
            drain()
            og.arrive(12, 13)
            og.start(21)
            og.arrive(21)

        @pl.when(k == 7)
        def _():
            og.finish(*range(14), 17, 18, 19, 20, 22, 23)
            og.arrive(14)
            og.start(24)
            og.arrive(15, 16)
            og.start(27, 28)
            og.arrive(25, 26)
            og.start(29, 30)
            og.arrive(24, 27, 28, 29, 30)

        @pl.when(k < 8)
        def _():
            def half(h, inner):
                multiply(k, h)
                return inner

            lax.fori_loop(1 - lax.div(k, 4), 2, half, 0)

        @pl.when((k > 2) & (k < 11))
        def _():
            settle(nth(k - 3))

        @pl.when(k > 4)
        def _():
            place_rows(nth(k - 5))

        return carry

    lax.fori_loop(0, 13, column_step, 0)

    og.finish(14, 15, 16, 21, *range(24, 31))

    def drain_out(chip, carry):
        for core in range(2):
            out_copy(chip, core).wait()
        for h in range(2):
            z_copy(chip, h).wait_send()
        for d in (1, 3, 2):
            f_copy(chip, d).wait_send()
        return carry

    lax.fori_loop(0, 8, drain_out, 0)


TILES = ((0, 128), (0, 256), (0, 384), (128, 384))


def local(activations, query_weight, key_matrix, value_matrix, output_weight, prompt_lengths):
    anywhere = pl.BlockSpec(memory_space=pl.ANY)
    dma = pltpu.SemaphoreType.DMA
    return pl.pallas_call(
        kernel,
        out_shape=jax.ShapeDtypeStruct((64, WIDTH), BF16),
        in_specs=[anywhere] * 5 + [pl.BlockSpec(memory_space=pltpu.SMEM)],
        out_specs=anywhere,
        scratch_shapes=[
            pltpu.VMEM((SPAN, HALF), BF16),
            pltpu.VMEM((SPAN, HALF), BF16),
            pltpu.VMEM((HALF, COLS), BF16),
            pltpu.VMEM((8, OROWS, 256), BF16),
            pltpu.VMEM((4, SPAN, 256), F32),
            pltpu.VMEM((PART, 256), F32),
            pltpu.VMEM((5, SPAN, 256), BF16),
            pltpu.VMEM((5, SPAN, 256), BF16),
            pltpu.VMEM((SPAN, 4 * QCOLS), BF16),
            pltpu.VMEM((SPAN, HEAD), F32),
            pltpu.VMEM((SPAN, HEAD), F32),
            pltpu.VMEM((4, 128, 384), F32),
            pltpu.VMEM((SPAN, HEAD), BF16),
            pltpu.VMEM((SPAN, HEAD), BF16),
            pltpu.VMEM((8, 4, 64, 256), BF16),
            pltpu.VMEM((8, 4, 64, 256), BF16),
            pltpu.VMEM((8, 4, 2, 64, HEAD), BF16),
            pltpu.VMEM((8, 2, 64, 512), BF16),
            dma((2, 10)), dma((2, 10)), dma((31,)), dma((31,)), dma((6, 4)), dma((6, 4)), dma((5, 2)), dma((5, 2)), dma((3,)), dma((3,)),
            dma((4, 4, 2)), dma((4, 4, 2)), dma((8, 2)), dma((8, 2)), dma((8, 3)), dma((8, 3)), dma((5,)), dma((8, 2)),
        ],
        compiler_params=pltpu.CompilerParams(collective_id=0, has_side_effects=True, vmem_limit_bytes=62 << 20),
        cost_estimate=pl.CostEstimate(flops=20 * 10**9, bytes_accessed=12 << 20, transcendentals=1 << 20),
        name="attention_layer",
    )(activations, query_weight, key_matrix, value_matrix, output_weight, prompt_lengths)


def solution(mesh):
    placed = (
        P("group", None),
        P("group", "tp"),
        P("group", "tp"),
        P("group", "tp"),
        P("tp", "group"),
        P("group", None),
    )
    return jax.shard_map(
        local, mesh=mesh, in_specs=placed, out_specs=P(("group", "tp"), None), check_vma=False
    )
```

```python
import math

import jax
import jax.numpy as jnp
from jax import lax
from jax.experimental import pallas as pl
from jax.experimental.pallas import tpu as pltpu
from jax.sharding import PartitionSpec as P

MESH = pl.DeviceIdType.MESH
SPAN = 512
WIDTH = 8192
HEAD = 128
QCOLS = 1024
COLS = 1280
EARLY = 768
DEPTH = 512
HALF = 4096
PART = 256
OROWS = 4096
DOCS = 8
F32 = jnp.float32
BF16 = jnp.bfloat16


def ring(v, step, size):
    return lax.rem(v + (step + size), size)


class Place:
    def __init__(self):
        g = lax.axis_index("group")
        t = lax.axis_index("tp")
        self.g, self.t = g, t
        self.core = lax.rem(g, 2)
        self.y = lax.rem(lax.div(g, 2), 4)
        self.zl = lax.div(g, 8)
        self.x = lax.div(t, 2)
        self.zh = lax.rem(t, 2)

    def chip(self, dz, dy):
        return ring(self.zl, dz, 2) * 4 + ring(self.y, dy, 4)

    def dev(self, dz=0, dy=0, dc=0, dx=0, dh=0):
        group = self.chip(dz, dy) * 2 + ring(self.core, dc, 2)
        return (group, ring(self.x, dx, 4) * 2 + ring(self.zh, dh, 2))


class Gather:
    def __init__(self, place, view, rows, part, send, recv):
        self.place, self.view, self.send, self.recv = place, view, send, recv
        half = part // 2
        rest = rows - part
        self.a, self.a1, self.a2 = (0, part), (0, half), (half, part - half)
        self.b, self.b1, self.b2 = (part, rest), (part, rest // 2), (part + rest // 2, rest - rest // 2)
        self.all = (0, rows)
        b1, b2 = ([(at + i * (count // 2), count // 2) for i in range(2)] for at, count in (self.b1, self.b2))
        up, down, over, twin = place.dev(dy=1), place.dev(dy=-1), place.dev(dz=1), place.dev(dc=1)
        mine, p_up, p_down, p_far = (0, 0), (0, 1), (0, -1), (0, 2)
        z_mine, z_up, z_down, z_far = (1, 0), (1, 1), (1, -1), (1, 2)
        self.steps = [
            (mine, self.a, up, p_down),
            (mine, self.a, down, p_up),
            (mine, self.b, over, z_mine),
            (mine, self.b, up, p_down),
            (mine, self.b, down, p_up),
            (mine, self.a, over, z_mine),
            (p_down, self.a1, up, p_far),
            (p_up, self.a2, down, p_far),
            (p_down, self.a, over, z_down),
            (p_up, self.a, over, z_up),
            (z_mine, self.b, up, z_down),
            (z_mine, self.b, down, z_up),
            (p_down, self.b1, up, p_far),
            (p_up, self.b2, down, p_far),
            (p_far, self.a, over, z_far),
            (z_down, b1[0], up, z_far),
            (z_up, b2[0], down, z_far),
        ]
        self.blocks = [mine, p_down, p_up, z_mine, p_far, z_down, z_up, z_far]
        for block in self.blocks:
            self.steps.append((block, self.a if block == z_far else self.all, twin, block))
        self.steps += [(z_down, b1[1], up, z_far), (z_up, b2[1], down, z_far)]
        self.steps += [(z_far, piece, twin, z_far) for piece in (b1[0], b2[0], b1[1], b2[1])]

    def copy(self, step, arriving=False):
        block, rows, target, lands = self.steps[step]
        core = self.place.core
        if arriving:
            block = lands
            if step in range(17, 25) or step >= 27:
                core = 1 - core
        ref = self.view(self.place.chip(*block), core, *rows)
        return pltpu.make_async_remote_copy(
            src_ref=ref,
            dst_ref=ref,
            send_sem=self.send.at[step],
            recv_sem=self.recv.at[step],
            device_id=target,
            device_id_type=MESH,
        )

    def start(self, *steps):
        for step in steps:
            self.copy(step).start()

    def arrive(self, *steps):
        for step in steps:
            self.copy(step, arriving=True).wait_recv()

    def finish(self, *steps):
        for step in steps:
            self.copy(step).wait_send()


class Ring:
    def __init__(self, place, view, rows, send, recv):
        self.place, self.view, self.send, self.recv = place, view, send, recv
        whole, first, second = (0, rows), (0, rows // 2), (rows // 2, rows // 2)
        up, down, twin = place.dev(dy=1), place.dev(dy=-1), place.dev(dc=1)
        self.steps = [
            (0, first, up, -1),
            (0, second, down, 1),
            (0, second, up, -1),
            (0, first, down, 1),
            (-1, first, up, 2),
            (1, second, down, 2),
            (0, whole, twin, 0),
            (-1, whole, twin, -1),
            (1, whole, twin, 1),
            (2, whole, twin, 2),
        ]

    def copy(self, step, arriving=False):
        block, rows, target, lands = self.steps[step]
        core = self.place.core
        if arriving:
            block = lands
            if step >= 6:
                core = 1 - core
        ref = self.view(ring(self.place.y, block, 4), core, *rows)
        return pltpu.make_async_remote_copy(
            src_ref=ref,
            dst_ref=ref,
            send_sem=self.send.at[step],
            recv_sem=self.recv.at[step],
            device_id=target,
            device_id_type=MESH,
        )

    def start(self, *steps):
        for step in steps:
            self.copy(step).start()

    def arrive(self, *steps):
        for step in steps:
            self.copy(step, arriving=True).wait_recv()

    def finish(self):
        for step in range(len(self.steps)):
            self.copy(step).wait_send()


def starts_of(row, lengths):
    start = jnp.zeros_like(row)
    end = 0
    for j in range(DOCS):
        end = end + lengths[j]
        start = start + jnp.where(row >= end, lengths[j], 0)
    return start


def kernel(
    act, wq, wk, wv, wo, lens, out,
    xown, xpar, wbuf, obuf, acc, tmp, psend, precv, ctx, cosb, sinb, bias, rkb, rvb, sbuf, rbuf, fbuf, gbuf,
    w_send, w_recv, o_send, o_recv, x_send, x_recv, p_send, p_recv, e_send, e_recv, c_send, c_recv,
    z_send, z_recv, f_send, f_recv, w_sem, out_sem,
):
    place = Place()
    mine = pl.ds(pl.multiple_of((place.y * 2 + place.core) * DEPTH, DEPTH), DEPTH)

    own = [
        pltpu.make_async_copy(wq, wbuf.at[mine, pl.ds(256, QCOLS)], w_sem.at[0]),
        pltpu.make_async_copy(wk, wbuf.at[mine, pl.ds(0, HEAD)], w_sem.at[1]),
        pltpu.make_async_copy(wv, wbuf.at[mine, pl.ds(HEAD, HEAD)], w_sem.at[2]),
    ]
    for copy in own:
        copy.start()
    chip0 = place.chip(0, 0)
    o_cols = pl.ds(pl.multiple_of(place.core * HEAD, HEAD), HEAD)
    own_o = pltpu.make_async_copy(
        wo.at[:, pl.ds(pl.multiple_of(place.x * HEAD, HEAD), HEAD)],
        obuf.at[chip0, pl.ds(pl.multiple_of(place.x * 1024, 1024), 1024), o_cols],
        w_sem.at[3],
    )

    own_x = pltpu.make_async_copy(act.at[:, pl.ds(pl.multiple_of(place.zl * HALF, HALF), HALF)], xown, w_sem.at[4])

    barrier = pltpu.get_barrier_semaphore()
    partners = [
        place.dev(dy=1), place.dev(dy=-1), place.dev(dz=1), place.dev(dc=1),
        place.dev(dx=1), place.dev(dx=2), place.dev(dx=3), place.dev(dh=1),
        place.dev(dz=1, dh=1),
    ]
    for partner in partners:
        pl.semaphore_signal(barrier, inc=1, device_id=partner, device_id_type=MESH)
    pl.semaphore_wait(barrier, len(partners))

    def w_view(first_col, cols):
        def view(y, core, first, count):
            rows = pl.ds(pl.multiple_of((y * 2 + core) * DEPTH + first, count), count)
            return wbuf.at[rows, pl.ds(first_col, cols)]

        return view

    def o_view(chip, core, first, count):
        return obuf.at[chip, pl.ds(first, count), pl.ds(pl.multiple_of(core * HEAD, HEAD), HEAD)]

    wg = Ring(place, w_view(0, EARLY), DEPTH, w_send.at[0], w_recv.at[0])
    late = Ring(place, w_view(EARLY, COLS - EARLY), DEPTH, w_send.at[1], w_recv.at[1])
    og = Gather(place, o_view, OROWS, 512, o_send, o_recv)

    for copy in own:
        copy.wait()
    wg.start(0, 1, 2, 3, 6)

    x_routes = [(0, dict(dz=1, dh=1), 0), (0, dict(dx=1), -1), (0, dict(dx=-1), 1), (-1, dict(dx=1), 2), (1, dict(dx=-1), 2)]
    x_routes.append((2, dict(dz=1, dh=1), 2))

    def x_copy(kind, i, arriving=False):
        owner, target, lands = x_routes[kind]
        slot = ring(place.x, lands if arriving else owner, 4) * 2 + i // 2
        rows = pl.ds((i % 2) * 256, 256)
        ref = xpar.at[rows, pl.ds(pl.multiple_of(slot * DEPTH, DEPTH), DEPTH)]
        source = ref
        if kind in (0, 5):
            first = (1 - place.zl) * HALF + slot * DEPTH
            source = act.at[rows, pl.ds(pl.multiple_of(first, DEPTH), DEPTH)]
        return pltpu.make_async_remote_copy(
            src_ref=source,
            dst_ref=ref,
            send_sem=x_send.at[kind, i],
            recv_sem=x_recv.at[kind, i],
            device_id=place.dev(**target),
            device_id_type=MESH,
        )

    for i in range(4):
        x_copy(0, i).start()
    for i in (2, 3):
        x_copy(5, i).start()

    def exchange(d, arriving=False):
        to = ring(place.x, d, 4)
        row = ring(place.x, -d, 4) if arriving else place.x
        return pltpu.make_async_remote_copy(
            src_ref=wo.at[:, pl.ds(pl.multiple_of(to * HEAD, HEAD), HEAD)],
            dst_ref=obuf.at[chip0, pl.ds(pl.multiple_of(row * 1024, 1024), 1024), o_cols],
            send_sem=e_send.at[d - 1],
            recv_sem=e_recv.at[d - 1],
            device_id=place.dev(dx=d),
            device_id_type=MESH,
        )

    for d in (1, 3, 2):
        exchange(d).start()
    own_x.start()
    own_o.start()

    lengths = [lens[0, j] for j in range(DOCS)]
    row = lax.broadcasted_iota(jnp.int32, (SPAN, HEAD), 0)
    lane = lax.broadcasted_iota(jnp.int32, (SPAN, HEAD), 1)
    low = lane < HEAD // 2
    index = jnp.where(low, lane, lane - HEAD // 2).astype(F32)
    freq = jnp.exp(index * (-2.0 * math.log(500000.0) / HEAD))
    angle = (row - starts_of(row, lengths)).astype(F32) * freq
    cosb[...] = jnp.cos(angle)
    sine = jnp.sin(angle)
    sinb[...] = jnp.where(low, -sine, sine)
    for j, (first, count) in enumerate(TILES):
        q = lax.broadcasted_iota(jnp.int32, (128, count), 0) + j * 128
        k = lax.broadcasted_iota(jnp.int32, (128, count), 1) + first
        keep = (k >= starts_of(q, lengths)) & (k <= q)
        bias[j, :, :count] = jnp.where(keep, 0.0, -1e30)

    def x_pass(i):
        x_copy(0, i, arriving=True).wait_recv()
        x_copy(1, i).start()
        x_copy(2, i).start()

    x_pass(0)
    x_pass(1)
    for d in (1, 3, 2):
        exchange(d, arriving=True).wait_recv()
    own_o.wait()
    og.start(2, 5, 17)
    wg.arrive(0)
    wg.start(4)
    wg.arrive(1)
    wg.start(5)
    late.start(0, 1, 2, 3, 6)
    x_pass(2)
    x_pass(3)
    wg.arrive(2)
    wg.start(7)
    wg.arrive(3)
    wg.start(8)
    x_copy(1, 0, arriving=True).wait_recv()
    x_copy(3, 0).start()
    x_copy(2, 1, arriving=True).wait_recv()
    x_copy(4, 1).start()
    late.arrive(0)
    late.start(4)
    late.arrive(1)
    late.start(5)
    og.start(0, 1, 3, 4)
    wg.arrive(4, 5)
    wg.start(9)
    late.arrive(2)
    late.start(7)
    late.arrive(3)
    late.start(8)
    wg.arrive(6, 7, 8, 9)
    own_x.wait()
    for i in range(4):
        if i != 0:
            x_copy(1, i, arriving=True).wait_recv()
        if i != 1:
            x_copy(2, i, arriving=True).wait_recv()
    x_copy(5, 2, arriving=True).wait_recv()
    x_copy(5, 3, arriving=True).wait_recv()
    x_copy(3, 0, arriving=True).wait_recv()
    x_copy(4, 1, arriving=True).wait_recv()

    def p_copy(n, h):
        rows = pl.ds(h * PART, PART)
        return pltpu.make_async_remote_copy(
            src_ref=psend.at[n, rows],
            dst_ref=precv.at[n, rows],
            send_sem=p_send.at[n, h],
            recv_sem=p_recv.at[n, h],
            device_id=place.dev(dz=1),
            device_id_type=MESH,
        )

    def tile_cols(n):
        return pl.ds(pl.multiple_of(n * 256, 256), 256)

    def their_tile(i, carry):
        h, n = lax.div(i, 5), lax.rem(i, 5)
        rows = pl.ds(pl.multiple_of(h * PART, PART), PART)
        psend[n, rows] = jnp.dot(xpar[rows, :], wbuf[:, tile_cols(n)], preferred_element_type=F32).astype(BF16)
        p_copy(n, h).start()
        return carry

    lax.fori_loop(0, 3, their_tile, 0)
    late.arrive(4, 5)
    late.start(9)
    late.arrive(6, 7, 8, 9)
    lax.fori_loop(3, 10, their_tile, 0)

    scale = 1.0 / math.sqrt(HEAD)

    def ctx_copy(kind, n, h, arriving=False):
        dx = 1 if kind in (0, 2) else -1
        if kind < 2:
            owner, rows = 0, pl.ds(h * PART, PART)
        else:
            owner, rows = -dx, pl.ds(h * PART + (0 if kind == 2 else PART // 2), PART // 2)
        if arriving:
            owner = owner - dx
        first = ring(place.x, owner % 4, 4) * QCOLS + n * 256
        ref = ctx.at[rows, pl.ds(pl.multiple_of(first, 256), 256)]
        return pltpu.make_async_remote_copy(
            src_ref=ref,
            dst_ref=ref,
            send_sem=c_send.at[kind, n, h],
            recv_sem=c_recv.at[kind, n, h],
            device_id=place.dev(dx=dx),
            device_id_type=MESH,
        )

    def rotate(u, h):
        rows = slice(h * PART, (h + 1) * PART)
        return (u * cosb[rows, :] + pltpu.roll(u, HEAD // 2, 1) * sinb[rows, :]).astype(BF16)

    def attend(n, h):
        rq = [rotate(tmp[:, :HEAD], h), rotate(tmp[:, HEAD:], h)]
        cols = pl.ds(pl.multiple_of(place.x * QCOLS + n * 256, 256), 256)
        for t in range(2):
            j = 2 * h + t
            first, count = TILES[j]
            rows = slice(t * 128, (t + 1) * 128)
            q = jnp.concatenate([rq[0][rows], rq[1][rows]], axis=0)
            keys = rkb[first : first + count, :]
            score = lax.dot_general(q, keys, (((1,), (1,)), ((), ())), preferred_element_type=F32)
            mask = bias[j, :, :count]
            score = score * scale + jnp.concatenate([mask, mask], axis=0)
            top = jnp.max(score, axis=-1, keepdims=True)
            weights = jnp.exp(score - top)
            probs = (weights * (1.0 / jnp.sum(weights, axis=-1, keepdims=True))).astype(BF16)
            context = jnp.dot(probs, rvb[first : first + count, :], preferred_element_type=F32)
            context = context.astype(BF16)
            ctx[j * 128 : (j + 1) * 128, cols] = jnp.concatenate([context[:128], context[128:]], axis=1)
        ctx_copy(0, n, h).start()
        ctx_copy(1, n, h).start()

    def relay(n, h):
        ctx_copy(0, n, h, arriving=True).wait_recv()
        ctx_copy(2, n, h).start()
        ctx_copy(1, n, h, arriving=True).wait_recv()
        ctx_copy(3, n, h).start()

    def ctx_done(h):
        def far(n, carry):
            ctx_copy(2, n, h, arriving=True).wait_recv()
            ctx_copy(3, n, h, arriving=True).wait_recv()
            return carry

        lax.fori_loop(0, 4, far, 0)

    def z_copy(chip, h):
        two = pl.ds(h * 2, 2)
        return pltpu.make_async_remote_copy(
            src_ref=sbuf.at[chip, two],
            dst_ref=rbuf.at[chip, two],
            send_sem=z_send.at[chip, h],
            recv_sem=z_recv.at[chip, h],
            device_id=place.dev(dh=1),
            device_id_type=MESH,
        )

    def nth(k):
        pair, odd = lax.div(k, 2), lax.rem(k, 2)
        middle = lax.div(pair * (3 - pair), 2)
        dz = middle * (pair - 1) + (1 - middle) * odd
        dy = middle * (3 - 2 * odd) + (1 - middle) * 2 * lax.div(pair, 3)
        return place.chip(dz, dy)

    def kept(chip, i):
        return lax.div(chip, 2), pl.ds(pl.multiple_of(lax.rem(chip, 2) * 256 + i * 64, 64), 64)

    def multiply(k, h):
        chip = nth(k)
        rows = pl.ds(pl.multiple_of(h * PART, PART), PART)
        tmp[...] = jnp.dot(ctx[rows, :], obuf[chip], preferred_element_type=F32)
        for i in range(2):
            there = pl.ds(pl.multiple_of(i * 128 + (1 - place.zh) * 64, 64), 64)
            here = pl.ds(pl.multiple_of(i * 128 + place.zh * 64, 64), 64)
            sbuf[chip, h * 2 + i] = tmp[there, :].astype(BF16)
            pair, spot = kept(chip, h * 2 + i)
            acc[pair, spot, :] = tmp[here, :]
        z_copy(chip, h).start()

    og.arrive(2, 5)
    og.start(20)
    og.arrive(0)
    og.start(6, 8)
    og.arrive(1)
    og.start(7, 9)
    og.start(10, 11)

    for h in range(2):

        def own_tile(i, carry, h=h):
            n = i
            rows = slice(h * PART, (h + 1) * PART)
            tmp[...] = jnp.dot(xown[rows, :], wbuf[:, tile_cols(n)], preferred_element_type=F32)
            p_copy(n, h).wait_recv()
            tmp[...] += precv[n, rows, :].astype(F32)

            @pl.when(i == 0)
            def _():
                rkb[rows, :] = rotate(tmp[:, :HEAD], h)
                rvb[rows, :] = tmp[:, HEAD:].astype(BF16)

            @pl.when(i > 0)
            def _():
                attend(i - 1, h)

            @pl.when(i > 1)
            def _():
                relay(i - 2, h)

            if h == 1:

                @pl.when(i == 0)
                def _():
                    relay(3, 0)

                @pl.when(i == 3)
                def _():
                    og.arrive(3)
                    og.start(12, 18)
                    og.arrive(4)
                    og.start(13, 19)
                    ctx_done(0)
                    og.arrive(17, 20)

                @pl.when(i > 2)
                def _():
                    multiply(i - 3, 0)

            return carry

        lax.fori_loop(0, 5, own_tile, 0)

    og.arrive(6, 7)
    og.start(14)

    def first_half(k, carry):
        multiply(k, 0)
        return carry

    og.arrive(18, 19)
    lax.fori_loop(2, 4, first_half, 0)
    relay(3, 1)
    ctx_done(1)

    def f_copy(chip, d, arriving=False):
        to = ring(place.x, d, 4)
        source = ring(place.x, -d, 4) if arriving else place.x
        return pltpu.make_async_remote_copy(
            src_ref=fbuf.at[chip, to],
            dst_ref=gbuf.at[chip, :, :, pl.ds(pl.multiple_of(source * HEAD, HEAD), HEAD)],
            send_sem=f_send.at[chip, d - 1],
            recv_sem=f_recv.at[chip, d - 1],
            device_id=place.dev(dx=d),
            device_id_type=MESH,
        )

    def settle(chip):
        for h in range(2):
            z_copy(chip, h).wait_recv()
            for i in (2 * h, 2 * h + 1):
                pair, spot = kept(chip, i)
                total = (acc[pair, spot, :] + rbuf[chip, i].astype(F32)).astype(BF16)
                fbuf[chip, i, 0] = total[:, :HEAD]
                fbuf[chip, i, 1] = total[:, HEAD:]
        for d in (1, 3, 2):
            f_copy(chip, d).start()

    def out_copy(chip, core):
        cols = pl.ds(pl.multiple_of(chip * 1024 + core * 512, 512), 512)
        return pltpu.make_async_copy(gbuf.at[chip, core], out.at[:, cols], out_sem.at[chip, core])

    def place_rows(chip):
        for d in (1, 3, 2):
            f_copy(chip, d, arriving=True).wait_recv()
        here = pl.ds(pl.multiple_of(place.x * HEAD, HEAD), HEAD)
        for core in range(2):
            gbuf[chip, core, :, here] = fbuf[chip, place.x, core]
            out_copy(chip, core).start()

    def drain():
        wg.finish()
        late.finish()
        for d in (1, 3, 2):
            exchange(d).wait_send()
        for kind, pieces in enumerate(((0, 1, 2, 3), (0, 1, 2, 3), (0, 1, 2, 3), (0,), (1,), (2, 3))):
            for i in pieces:
                x_copy(kind, i).wait_send()
        for h in range(2):
            for n in range(5):
                p_copy(n, h).wait_send()
            for n in range(4):
                for kind in range(4):
                    ctx_copy(kind, n, h).wait_send()

    def settle_some(first, last):
        def one(k, carry):
            settle(nth(k))
            return carry

        lax.fori_loop(first, last, one, 0)

    def place_some(first, last):
        def one(k, carry):
            place_rows(nth(k))
            return carry

        lax.fori_loop(first, last, one, 0)

    def column_step(k, carry):
        @pl.when(k == 4)
        def _():
            og.arrive(10)
            og.start(15, 25)
            og.arrive(11)
            og.start(16, 26)
            og.arrive(8)
            og.start(22)
            og.arrive(9)
            og.start(23)
            og.arrive(22)

        @pl.when(k == 5)
        def _():
            og.arrive(23)

        @pl.when(k == 6)
        def _():
            drain()
            og.arrive(12, 13)
            og.start(21)
            og.arrive(21)

        @pl.when(k == 7)
        def _():
            settle_some(3, 5)
            og.finish(*range(14), 17, 18, 19, 20, 22, 23)
            og.arrive(14)
            og.start(24)
            og.arrive(15, 16)
            og.start(27, 28)
            og.arrive(25, 26)
            og.start(29, 30)
            og.arrive(24, 27, 28, 29, 30)

        def half(h, inner):
            multiply(k, h)
            return inner

        lax.fori_loop(1 - lax.div(k, 4), 2, half, 0)

        @pl.when((k > 3) & (k < 7))
        def _():
            settle(nth(k - 4))

        return carry

    lax.fori_loop(0, 8, column_step, 0)
    settle_some(5, 7)
    place_some(0, 4)
    settle_some(7, 8)
    place_some(4, 8)

    og.finish(14, 15, 16, 21, *range(24, 31))

    def drain_out(chip, carry):
        for core in range(2):
            out_copy(chip, core).wait()
        for h in range(2):
            z_copy(chip, h).wait_send()
        for d in (1, 3, 2):
            f_copy(chip, d).wait_send()
        return carry

    lax.fori_loop(0, 8, drain_out, 0)


TILES = ((0, 128), (0, 256), (0, 384), (128, 384))


def local(activations, query_weight, key_matrix, value_matrix, output_weight, prompt_lengths):
    anywhere = pl.BlockSpec(memory_space=pl.ANY)
    dma = pltpu.SemaphoreType.DMA
    return pl.pallas_call(
        kernel,
        out_shape=jax.ShapeDtypeStruct((64, WIDTH), BF16),
        in_specs=[anywhere] * 5 + [pl.BlockSpec(memory_space=pltpu.SMEM)],
        out_specs=anywhere,
        scratch_shapes=[
            pltpu.VMEM((SPAN, HALF), BF16),
            pltpu.VMEM((SPAN, HALF), BF16),
            pltpu.VMEM((HALF, COLS), BF16),
            pltpu.VMEM((8, OROWS, 256), BF16),
            pltpu.VMEM((4, SPAN, 256), F32),
            pltpu.VMEM((PART, 256), F32),
            pltpu.VMEM((5, SPAN, 256), BF16),
            pltpu.VMEM((5, SPAN, 256), BF16),
            pltpu.VMEM((SPAN, 4 * QCOLS), BF16),
            pltpu.VMEM((SPAN, HEAD), F32),
            pltpu.VMEM((SPAN, HEAD), F32),
            pltpu.VMEM((4, 128, 384), F32),
            pltpu.VMEM((SPAN, HEAD), BF16),
            pltpu.VMEM((SPAN, HEAD), BF16),
            pltpu.VMEM((8, 4, 64, 256), BF16),
            pltpu.VMEM((8, 4, 64, 256), BF16),
            pltpu.VMEM((8, 4, 2, 64, HEAD), BF16),
            pltpu.VMEM((8, 2, 64, 512), BF16),
            dma((2, 10)), dma((2, 10)), dma((31,)), dma((31,)), dma((6, 4)), dma((6, 4)), dma((5, 2)), dma((5, 2)), dma((3,)), dma((3,)),
            dma((4, 4, 2)), dma((4, 4, 2)), dma((8, 2)), dma((8, 2)), dma((8, 3)), dma((8, 3)), dma((5,)), dma((8, 2)),
        ],
        compiler_params=pltpu.CompilerParams(collective_id=0, has_side_effects=True, vmem_limit_bytes=62 << 20),
        cost_estimate=pl.CostEstimate(flops=20 * 10**9, bytes_accessed=12 << 20, transcendentals=1 << 20),
        name="attention_layer",
    )(activations, query_weight, key_matrix, value_matrix, output_weight, prompt_lengths)


def solution(mesh):
    placed = (
        P("group", None),
        P("group", "tp"),
        P("group", "tp"),
        P("group", "tp"),
        P("tp", "group"),
        P("group", None),
    )
    return jax.shard_map(
        local, mesh=mesh, in_specs=placed, out_specs=P(("group", "tp"), None), check_vma=False
    )
```

```python
import math

import jax
import jax.numpy as jnp
from jax import lax
from jax.experimental import pallas as pl
from jax.experimental.pallas import tpu as pltpu
from jax.sharding import PartitionSpec as P

MESH = pl.DeviceIdType.MESH
SPAN = 512
WIDTH = 8192
HEAD = 128
QCOLS = 1024
COLS = 1280
EARLY = 768
DEPTH = 512
HALF = 4096
PART = 256
OROWS = 4096
DOCS = 8
F32 = jnp.float32
BF16 = jnp.bfloat16


def ring(v, step, size):
    return lax.rem(v + (step + size), size)


class Place:
    def __init__(self):
        g = lax.axis_index("group")
        t = lax.axis_index("tp")
        self.g, self.t = g, t
        self.core = lax.rem(g, 2)
        self.y = lax.rem(lax.div(g, 2), 4)
        self.zl = lax.div(g, 8)
        self.x = lax.div(t, 2)
        self.zh = lax.rem(t, 2)

    def chip(self, dz, dy):
        return ring(self.zl, dz, 2) * 4 + ring(self.y, dy, 4)

    def dev(self, dz=0, dy=0, dc=0, dx=0, dh=0):
        group = self.chip(dz, dy) * 2 + ring(self.core, dc, 2)
        return (group, ring(self.x, dx, 4) * 2 + ring(self.zh, dh, 2))


class Gather:
    def __init__(self, place, view, rows, part, send, recv):
        self.place, self.view, self.send, self.recv = place, view, send, recv
        half = part // 2
        rest = rows - part
        self.a, self.a1, self.a2 = (0, part), (0, half), (half, part - half)
        self.b, self.b1, self.b2 = (part, rest), (part, rest // 2), (part + rest // 2, rest - rest // 2)
        self.all = (0, rows)
        b1, b2 = ([(at + i * (count // 2), count // 2) for i in range(2)] for at, count in (self.b1, self.b2))
        up, down, over, twin = place.dev(dy=1), place.dev(dy=-1), place.dev(dz=1), place.dev(dc=1)
        mine, p_up, p_down, p_far = (0, 0), (0, 1), (0, -1), (0, 2)
        z_mine, z_up, z_down, z_far = (1, 0), (1, 1), (1, -1), (1, 2)
        self.steps = [
            (mine, self.a, up, p_down),
            (mine, self.a, down, p_up),
            (mine, self.b, over, z_mine),
            (mine, self.b, up, p_down),
            (mine, self.b, down, p_up),
            (mine, self.a, over, z_mine),
            (p_down, self.a1, up, p_far),
            (p_up, self.a2, down, p_far),
            (p_down, self.a, over, z_down),
            (p_up, self.a, over, z_up),
            (z_mine, self.b, up, z_down),
            (z_mine, self.b, down, z_up),
            (p_down, self.b1, up, p_far),
            (p_up, self.b2, down, p_far),
            (p_far, self.a, over, z_far),
            (z_down, b1[0], up, z_far),
            (z_up, b2[0], down, z_far),
        ]
        self.blocks = [mine, p_down, p_up, z_mine, p_far, z_down, z_up, z_far]
        for block in self.blocks:
            self.steps.append((block, self.a if block == z_far else self.all, twin, block))
        self.steps += [(z_down, b1[1], up, z_far), (z_up, b2[1], down, z_far)]
        self.steps += [(z_far, piece, twin, z_far) for piece in (b1[0], b2[0], b1[1], b2[1])]

    def copy(self, step, arriving=False):
        block, rows, target, lands = self.steps[step]
        core = self.place.core
        if arriving:
            block = lands
            if step in range(17, 25) or step >= 27:
                core = 1 - core
        ref = self.view(self.place.chip(*block), core, *rows)
        return pltpu.make_async_remote_copy(
            src_ref=ref,
            dst_ref=ref,
            send_sem=self.send.at[step],
            recv_sem=self.recv.at[step],
            device_id=target,
            device_id_type=MESH,
        )

    def start(self, *steps):
        for step in steps:
            self.copy(step).start()

    def arrive(self, *steps):
        for step in steps:
            self.copy(step, arriving=True).wait_recv()

    def finish(self, *steps):
        for step in steps:
            self.copy(step).wait_send()


class Ring:
    def __init__(self, place, view, rows, send, recv):
        self.place, self.view, self.send, self.recv = place, view, send, recv
        whole, first, second = (0, rows), (0, rows // 2), (rows // 2, rows // 2)
        up, down, twin = place.dev(dy=1), place.dev(dy=-1), place.dev(dc=1)
        self.steps = [
            (0, first, up, -1),
            (0, second, down, 1),
            (0, second, up, -1),
            (0, first, down, 1),
            (-1, first, up, 2),
            (1, second, down, 2),
            (0, whole, twin, 0),
            (-1, whole, twin, -1),
            (1, whole, twin, 1),
            (2, whole, twin, 2),
        ]

    def copy(self, step, arriving=False):
        block, rows, target, lands = self.steps[step]
        core = self.place.core
        if arriving:
            block = lands
            if step >= 6:
                core = 1 - core
        ref = self.view(ring(self.place.y, block, 4), core, *rows)
        return pltpu.make_async_remote_copy(
            src_ref=ref,
            dst_ref=ref,
            send_sem=self.send.at[step],
            recv_sem=self.recv.at[step],
            device_id=target,
            device_id_type=MESH,
        )

    def start(self, *steps):
        for step in steps:
            self.copy(step).start()

    def arrive(self, *steps):
        for step in steps:
            self.copy(step, arriving=True).wait_recv()

    def finish(self):
        for step in range(len(self.steps)):
            self.copy(step).wait_send()


def starts_of(row, lengths):
    start = jnp.zeros_like(row)
    end = 0
    for j in range(DOCS):
        end = end + lengths[j]
        start = start + jnp.where(row >= end, lengths[j], 0)
    return start


def kernel(
    act, wq, wk, wv, wo, lens, out,
    xown, xpar, wbuf, obuf, acc, tmp, psend, precv, ctx, cosb, sinb, bias, rkb, rvb, sbuf, rbuf, fbuf, gbuf,
    w_send, w_recv, o_send, o_recv, x_send, x_recv, p_send, p_recv, e_send, e_recv, c_send, c_recv,
    z_send, z_recv, f_send, f_recv, w_sem, out_sem,
):
    place = Place()
    mine = pl.ds(pl.multiple_of((place.y * 2 + place.core) * DEPTH, DEPTH), DEPTH)

    own = [
        pltpu.make_async_copy(wq, wbuf.at[mine, pl.ds(256, QCOLS)], w_sem.at[0]),
        pltpu.make_async_copy(wk, wbuf.at[mine, pl.ds(0, HEAD)], w_sem.at[1]),
        pltpu.make_async_copy(wv, wbuf.at[mine, pl.ds(HEAD, HEAD)], w_sem.at[2]),
    ]
    for copy in own:
        copy.start()
    chip0 = place.chip(0, 0)
    o_cols = pl.ds(pl.multiple_of(place.core * HEAD, HEAD), HEAD)
    own_o = pltpu.make_async_copy(
        wo.at[:, pl.ds(pl.multiple_of(place.x * HEAD, HEAD), HEAD)],
        obuf.at[chip0, pl.ds(pl.multiple_of(place.x * 1024, 1024), 1024), o_cols],
        w_sem.at[3],
    )

    own_x = pltpu.make_async_copy(act.at[:, pl.ds(pl.multiple_of(place.zl * HALF, HALF), HALF)], xown, w_sem.at[4])

    barrier = pltpu.get_barrier_semaphore()
    partners = [
        place.dev(dy=1), place.dev(dy=-1), place.dev(dz=1), place.dev(dc=1),
        place.dev(dx=1), place.dev(dx=2), place.dev(dx=3), place.dev(dh=1),
        place.dev(dz=1, dh=1),
    ]
    for partner in partners:
        pl.semaphore_signal(barrier, inc=1, device_id=partner, device_id_type=MESH)
    pl.semaphore_wait(barrier, len(partners))

    def w_view(first_col, cols):
        def view(y, core, first, count):
            rows = pl.ds(pl.multiple_of((y * 2 + core) * DEPTH + first, count), count)
            return wbuf.at[rows, pl.ds(first_col, cols)]

        return view

    def o_view(chip, core, first, count):
        return obuf.at[chip, pl.ds(first, count), pl.ds(pl.multiple_of(core * HEAD, HEAD), HEAD)]

    wg = Ring(place, w_view(0, EARLY), DEPTH, w_send.at[0], w_recv.at[0])
    late = Ring(place, w_view(EARLY, COLS - EARLY), DEPTH, w_send.at[1], w_recv.at[1])
    og = Gather(place, o_view, OROWS, 512, o_send, o_recv)

    for copy in own:
        copy.wait()
    wg.start(0, 1, 2, 3, 6)

    x_routes = [(0, dict(dz=1, dh=1), 0), (0, dict(dx=1), -1), (0, dict(dx=-1), 1), (-1, dict(dx=1), 2), (1, dict(dx=-1), 2)]
    x_routes.append((2, dict(dz=1, dh=1), 2))

    def x_copy(kind, i, arriving=False):
        owner, target, lands = x_routes[kind]
        slot = ring(place.x, lands if arriving else owner, 4) * 2 + i // 2
        rows = pl.ds((i % 2) * 256, 256)
        ref = xpar.at[rows, pl.ds(pl.multiple_of(slot * DEPTH, DEPTH), DEPTH)]
        source = ref
        if kind in (0, 5):
            first = (1 - place.zl) * HALF + slot * DEPTH
            source = act.at[rows, pl.ds(pl.multiple_of(first, DEPTH), DEPTH)]
        return pltpu.make_async_remote_copy(
            src_ref=source,
            dst_ref=ref,
            send_sem=x_send.at[kind, i],
            recv_sem=x_recv.at[kind, i],
            device_id=place.dev(**target),
            device_id_type=MESH,
        )

    for i in range(4):
        x_copy(0, i).start()
    for i in (2, 3):
        x_copy(5, i).start()

    def exchange(d, arriving=False):
        to = ring(place.x, d, 4)
        row = ring(place.x, -d, 4) if arriving else place.x
        return pltpu.make_async_remote_copy(
            src_ref=wo.at[:, pl.ds(pl.multiple_of(to * HEAD, HEAD), HEAD)],
            dst_ref=obuf.at[chip0, pl.ds(pl.multiple_of(row * 1024, 1024), 1024), o_cols],
            send_sem=e_send.at[d - 1],
            recv_sem=e_recv.at[d - 1],
            device_id=place.dev(dx=d),
            device_id_type=MESH,
        )

    for d in (1, 3, 2):
        exchange(d).start()
    own_x.start()
    own_o.start()

    lengths = [lens[0, j] for j in range(DOCS)]
    row = lax.broadcasted_iota(jnp.int32, (SPAN, HEAD), 0)
    lane = lax.broadcasted_iota(jnp.int32, (SPAN, HEAD), 1)
    low = lane < HEAD // 2
    index = jnp.where(low, lane, lane - HEAD // 2).astype(F32)
    freq = jnp.exp(index * (-2.0 * math.log(500000.0) / HEAD))
    angle = (row - starts_of(row, lengths)).astype(F32) * freq
    cosb[...] = jnp.cos(angle)
    sine = jnp.sin(angle)
    sinb[...] = jnp.where(low, -sine, sine)
    for j, (first, count) in enumerate(TILES):
        q = lax.broadcasted_iota(jnp.int32, (128, count), 0) + j * 128
        k = lax.broadcasted_iota(jnp.int32, (128, count), 1) + first
        keep = (k >= starts_of(q, lengths)) & (k <= q)
        bias[j, :, :count] = jnp.where(keep, 0.0, -1e30)

    def x_pass(i):
        x_copy(0, i, arriving=True).wait_recv()
        x_copy(1, i).start()
        x_copy(2, i).start()

    x_pass(0)
    x_pass(1)
    for d in (1, 3, 2):
        exchange(d, arriving=True).wait_recv()
    own_o.wait()
    og.start(2, 5, 17)
    wg.arrive(0)
    wg.start(4)
    wg.arrive(1)
    wg.start(5)
    late.start(0, 1, 2, 3, 6)
    x_pass(2)
    x_pass(3)
    wg.arrive(2)
    wg.start(7)
    wg.arrive(3)
    wg.start(8)
    x_copy(1, 0, arriving=True).wait_recv()
    x_copy(3, 0).start()
    x_copy(2, 1, arriving=True).wait_recv()
    x_copy(4, 1).start()
    late.arrive(0)
    late.start(4)
    late.arrive(1)
    late.start(5)
    og.start(0, 1, 3, 4)
    wg.arrive(4, 5)
    wg.start(9)
    late.arrive(2)
    late.start(7)
    late.arrive(3)
    late.start(8)
    wg.arrive(6, 7, 8, 9)
    own_x.wait()
    for i in range(4):
        if i != 0:
            x_copy(1, i, arriving=True).wait_recv()
        if i != 1:
            x_copy(2, i, arriving=True).wait_recv()
    x_copy(5, 2, arriving=True).wait_recv()
    x_copy(5, 3, arriving=True).wait_recv()
    x_copy(3, 0, arriving=True).wait_recv()
    x_copy(4, 1, arriving=True).wait_recv()

    def p_copy(n, h):
        rows = pl.ds(h * PART, PART)
        return pltpu.make_async_remote_copy(
            src_ref=psend.at[n, rows],
            dst_ref=precv.at[n, rows],
            send_sem=p_send.at[n, h],
            recv_sem=p_recv.at[n, h],
            device_id=place.dev(dz=1),
            device_id_type=MESH,
        )

    def tile_cols(n):
        return pl.ds(pl.multiple_of(n * 256, 256), 256)

    def their_tile(i, carry):
        h, n = lax.div(i, 5), lax.rem(i, 5)
        rows = pl.ds(pl.multiple_of(h * PART, PART), PART)
        psend[n, rows] = jnp.dot(xpar[rows, :], wbuf[:, tile_cols(n)], preferred_element_type=F32).astype(BF16)
        p_copy(n, h).start()
        return carry

    lax.fori_loop(0, 3, their_tile, 0)
    late.arrive(4, 5)
    late.start(9)
    late.arrive(6, 7, 8, 9)
    lax.fori_loop(3, 10, their_tile, 0)

    scale = 1.0 / math.sqrt(HEAD)

    def ctx_copy(kind, n, h, arriving=False):
        dx = 1 if kind in (0, 2) else -1
        if kind < 2:
            owner, rows = 0, pl.ds(h * PART, PART)
        else:
            owner, rows = -dx, pl.ds(h * PART + (0 if kind == 2 else PART // 2), PART // 2)
        if arriving:
            owner = owner - dx
        first = ring(place.x, owner % 4, 4) * QCOLS + n * 256
        ref = ctx.at[rows, pl.ds(pl.multiple_of(first, 256), 256)]
        return pltpu.make_async_remote_copy(
            src_ref=ref,
            dst_ref=ref,
            send_sem=c_send.at[kind, n, h],
            recv_sem=c_recv.at[kind, n, h],
            device_id=place.dev(dx=dx),
            device_id_type=MESH,
        )

    def rotate(u, h):
        rows = slice(h * PART, (h + 1) * PART)
        return (u * cosb[rows, :] + pltpu.roll(u, HEAD // 2, 1) * sinb[rows, :]).astype(BF16)

    def attend(n, h):
        rq = [rotate(tmp[:, :HEAD], h), rotate(tmp[:, HEAD:], h)]
        cols = pl.ds(pl.multiple_of(place.x * QCOLS + n * 256, 256), 256)
        for t in range(2):
            j = 2 * h + t
            first, count = TILES[j]
            rows = slice(t * 128, (t + 1) * 128)
            q = jnp.concatenate([rq[0][rows], rq[1][rows]], axis=0)
            keys = rkb[first : first + count, :]
            score = lax.dot_general(q, keys, (((1,), (1,)), ((), ())), preferred_element_type=F32)
            mask = bias[j, :, :count]
            score = score * scale + jnp.concatenate([mask, mask], axis=0)
            top = jnp.max(score, axis=-1, keepdims=True)
            weights = jnp.exp(score - top)
            probs = (weights * (1.0 / jnp.sum(weights, axis=-1, keepdims=True))).astype(BF16)
            context = jnp.dot(probs, rvb[first : first + count, :], preferred_element_type=F32)
            context = context.astype(BF16)
            ctx[j * 128 : (j + 1) * 128, cols] = jnp.concatenate([context[:128], context[128:]], axis=1)
        ctx_copy(0, n, h).start()
        ctx_copy(1, n, h).start()

    def relay(n, h):
        ctx_copy(0, n, h, arriving=True).wait_recv()
        ctx_copy(2, n, h).start()
        ctx_copy(1, n, h, arriving=True).wait_recv()
        ctx_copy(3, n, h).start()

    def ctx_done(h):
        def far(n, carry):
            ctx_copy(2, n, h, arriving=True).wait_recv()
            ctx_copy(3, n, h, arriving=True).wait_recv()
            return carry

        lax.fori_loop(0, 4, far, 0)

    def z_copy(chip, h):
        two = pl.ds(h * 2, 2)
        return pltpu.make_async_remote_copy(
            src_ref=sbuf.at[chip, two],
            dst_ref=rbuf.at[chip, two],
            send_sem=z_send.at[chip, h],
            recv_sem=z_recv.at[chip, h],
            device_id=place.dev(dh=1),
            device_id_type=MESH,
        )

    def nth(k):
        pair, odd = lax.div(k, 2), lax.rem(k, 2)
        middle = lax.div(pair * (3 - pair), 2)
        dz = middle * (pair - 1) + (1 - middle) * odd
        dy = middle * (3 - 2 * odd) + (1 - middle) * 2 * lax.div(pair, 3)
        return place.chip(dz, dy)

    def kept(chip, i):
        return lax.div(chip, 2), pl.ds(pl.multiple_of(lax.rem(chip, 2) * 256 + i * 64, 64), 64)

    def multiply(k, h):
        chip = nth(k)
        rows = pl.ds(pl.multiple_of(h * PART, PART), PART)
        tmp[...] = jnp.dot(ctx[rows, :], obuf[chip], preferred_element_type=F32)
        for i in range(2):
            there = pl.ds(pl.multiple_of(i * 128 + (1 - place.zh) * 64, 64), 64)
            here = pl.ds(pl.multiple_of(i * 128 + place.zh * 64, 64), 64)
            sbuf[chip, h * 2 + i] = tmp[there, :].astype(BF16)
            pair, spot = kept(chip, h * 2 + i)
            acc[pair, spot, :] = tmp[here, :]
        z_copy(chip, h).start()

    og.arrive(2, 5)
    og.start(20)
    og.arrive(0)
    og.start(6, 8)
    og.arrive(1)
    og.start(7, 9)
    og.start(10, 11)

    for h in range(2):

        def own_tile(i, carry, h=h):
            n = i
            rows = slice(h * PART, (h + 1) * PART)
            tmp[...] = jnp.dot(xown[rows, :], wbuf[:, tile_cols(n)], preferred_element_type=F32)
            p_copy(n, h).wait_recv()
            tmp[...] += precv[n, rows, :].astype(F32)

            @pl.when(i == 0)
            def _():
                rkb[rows, :] = rotate(tmp[:, :HEAD], h)
                rvb[rows, :] = tmp[:, HEAD:].astype(BF16)

            @pl.when(i > 0)
            def _():
                attend(i - 1, h)

            @pl.when(i > 1)
            def _():
                relay(i - 2, h)

            if h == 1:

                @pl.when(i == 0)
                def _():
                    relay(3, 0)

                @pl.when(i == 3)
                def _():
                    og.arrive(3)
                    og.start(12, 18)
                    og.arrive(4)
                    og.start(13, 19)
                    ctx_done(0)
                    og.arrive(17, 20)

                @pl.when(i > 2)
                def _():
                    multiply(i - 3, 0)

            return carry

        lax.fori_loop(0, 5, own_tile, 0)

    og.arrive(6, 7)
    og.start(14)

    def first_half(k, carry):
        multiply(k, 0)
        return carry

    og.arrive(18, 19)
    lax.fori_loop(2, 4, first_half, 0)
    relay(3, 1)
    ctx_done(1)

    def f_copy(chip, d, arriving=False):
        to = ring(place.x, d, 4)
        source = ring(place.x, -d, 4) if arriving else place.x
        return pltpu.make_async_remote_copy(
            src_ref=fbuf.at[chip, to],
            dst_ref=gbuf.at[chip, :, :, pl.ds(pl.multiple_of(source * HEAD, HEAD), HEAD)],
            send_sem=f_send.at[chip, d - 1],
            recv_sem=f_recv.at[chip, d - 1],
            device_id=place.dev(dx=d),
            device_id_type=MESH,
        )

    def settle(chip):
        for h in range(2):
            z_copy(chip, h).wait_recv()
            for i in (2 * h, 2 * h + 1):
                pair, spot = kept(chip, i)
                total = (acc[pair, spot, :] + rbuf[chip, i].astype(F32)).astype(BF16)
                fbuf[chip, i, 0] = total[:, :HEAD]
                fbuf[chip, i, 1] = total[:, HEAD:]
        for d in (1, 3, 2):
            f_copy(chip, d).start()

    def out_copy(chip, core):
        cols = pl.ds(pl.multiple_of(chip * 1024 + core * 512, 512), 512)
        return pltpu.make_async_copy(gbuf.at[chip, core], out.at[:, cols], out_sem.at[chip, core])

    def place_rows(chip):
        for d in (1, 3, 2):
            f_copy(chip, d, arriving=True).wait_recv()
        here = pl.ds(pl.multiple_of(place.x * HEAD, HEAD), HEAD)
        for core in range(2):
            gbuf[chip, core, :, here] = fbuf[chip, place.x, core]
            out_copy(chip, core).start()

    def drain():
        wg.finish()
        late.finish()
        for d in (1, 3, 2):
            exchange(d).wait_send()
        for kind, pieces in enumerate(((0, 1, 2, 3), (0, 1, 2, 3), (0, 1, 2, 3), (0,), (1,), (2, 3))):
            for i in pieces:
                x_copy(kind, i).wait_send()
        for h in range(2):
            for n in range(5):
                p_copy(n, h).wait_send()
            for n in range(4):
                for kind in range(4):
                    ctx_copy(kind, n, h).wait_send()

    def settle_some(first, last):
        def one(k, carry):
            settle(nth(k))
            return carry

        lax.fori_loop(first, last, one, 0)

    def place_some(first, last):
        def one(k, carry):
            place_rows(nth(k))
            return carry

        lax.fori_loop(first, last, one, 0)

    def column_step(k, carry):
        @pl.when(k == 4)
        def _():
            og.arrive(10)
            og.start(15, 25)
            og.arrive(11)
            og.start(16, 26)
            og.arrive(8)
            og.start(22)
            og.arrive(9)
            og.start(23)
            og.arrive(22)

        @pl.when(k == 5)
        def _():
            og.arrive(23)

        @pl.when(k == 6)
        def _():
            drain()
            og.arrive(12, 13)
            og.start(21)
            og.arrive(21)

        @pl.when(k == 7)
        def _():
            settle_some(3, 5)
            place_some(0, 2)
            og.finish(*range(14), 17, 18, 19, 20, 22, 23)
            og.arrive(14)
            og.start(24)
            og.arrive(15, 16)
            og.start(27, 28)
            og.arrive(25, 26)
            og.start(29, 30)
            og.arrive(24, 27, 28, 29, 30)

        def half(h, inner):
            multiply(k, h)
            return inner

        lax.fori_loop(1 - lax.div(k, 4), 2, half, 0)

        @pl.when((k > 3) & (k < 7))
        def _():
            settle(nth(k - 4))

        return carry

    lax.fori_loop(0, 8, column_step, 0)
    settle_some(5, 7)
    place_some(2, 4)
    settle_some(7, 8)
    place_some(4, 8)

    og.finish(14, 15, 16, 21, *range(24, 31))

    def drain_out(chip, carry):
        for core in range(2):
            out_copy(chip, core).wait()
        for h in range(2):
            z_copy(chip, h).wait_send()
        for d in (1, 3, 2):
            f_copy(chip, d).wait_send()
        return carry

    lax.fori_loop(0, 8, drain_out, 0)


TILES = ((0, 128), (0, 256), (0, 384), (128, 384))


def local(activations, query_weight, key_matrix, value_matrix, output_weight, prompt_lengths):
    anywhere = pl.BlockSpec(memory_space=pl.ANY)
    dma = pltpu.SemaphoreType.DMA
    return pl.pallas_call(
        kernel,
        out_shape=jax.ShapeDtypeStruct((64, WIDTH), BF16),
        in_specs=[anywhere] * 5 + [pl.BlockSpec(memory_space=pltpu.SMEM)],
        out_specs=anywhere,
        scratch_shapes=[
            pltpu.VMEM((SPAN, HALF), BF16),
            pltpu.VMEM((SPAN, HALF), BF16),
            pltpu.VMEM((HALF, COLS), BF16),
            pltpu.VMEM((8, OROWS, 256), BF16),
            pltpu.VMEM((4, SPAN, 256), F32),
            pltpu.VMEM((PART, 256), F32),
            pltpu.VMEM((5, SPAN, 256), BF16),
            pltpu.VMEM((5, SPAN, 256), BF16),
            pltpu.VMEM((SPAN, 4 * QCOLS), BF16),
            pltpu.VMEM((SPAN, HEAD), F32),
            pltpu.VMEM((SPAN, HEAD), F32),
            pltpu.VMEM((4, 128, 384), F32),
            pltpu.VMEM((SPAN, HEAD), BF16),
            pltpu.VMEM((SPAN, HEAD), BF16),
            pltpu.VMEM((8, 4, 64, 256), BF16),
            pltpu.VMEM((8, 4, 64, 256), BF16),
            pltpu.VMEM((8, 4, 2, 64, HEAD), BF16),
            pltpu.VMEM((8, 2, 64, 512), BF16),
            dma((2, 10)), dma((2, 10)), dma((31,)), dma((31,)), dma((6, 4)), dma((6, 4)), dma((5, 2)), dma((5, 2)), dma((3,)), dma((3,)),
            dma((4, 4, 2)), dma((4, 4, 2)), dma((8, 2)), dma((8, 2)), dma((8, 3)), dma((8, 3)), dma((5,)), dma((8, 2)),
        ],
        compiler_params=pltpu.CompilerParams(collective_id=0, has_side_effects=True, vmem_limit_bytes=62 << 20),
        cost_estimate=pl.CostEstimate(flops=20 * 10**9, bytes_accessed=12 << 20, transcendentals=1 << 20),
        name="attention_layer",
    )(activations, query_weight, key_matrix, value_matrix, output_weight, prompt_lengths)


def solution(mesh):
    placed = (
        P("group", None),
        P("group", "tp"),
        P("group", "tp"),
        P("group", "tp"),
        P("tp", "group"),
        P("group", None),
    )
    return jax.shard_map(
        local, mesh=mesh, in_specs=placed, out_specs=P(("group", "tp"), None), check_vma=False
    )
```
